128 devices in a mesh: ctx: 64 (over x, y, z), tp: 2 (over core).
Axes of the slice: x: 4, y: 4, z: 4, core: 2. Of those that a mesh axis runs over, the one named last changes fastest.
Arguments:
- hidden: bfloat16 [8192, 2048], P('ctx', 'tp'), may hold values from -60 to 60
- grad_out: bfloat16 [8192, 2048], P('ctx', 'tp'), may hold values from -6 to 6
- expert_ids: int32 [8192, 4], P('ctx'), may hold values from 0 to 63, all different within a row; in each aligned block of 128 rows (0 to 127, 128 to 255, ...) at most 10 rows name the same one
- gate_weights: float32 [8192, 4], P('ctx'), may hold values from 0.1 to 1
- norm_gain: float32 [2048], P('tp'), may hold values from 0.25 to 1.75
- w_gate: bfloat16 [64, 2048, 1536], P('ctx', None, 'tp'), may hold values from -0.125 to 0.125
- w_up: bfloat16 [64, 2048, 1536], P('ctx', None, 'tp'), may hold values from -0.125 to 0.125
- w_down: bfloat16 [64, 1536, 2048], P('ctx', 'tp'), may hold values from -0.15625 to 0.15625
- queries: bfloat16 [8192, 2048], P('ctx', 'tp'), may hold values from -6 to 6
- forget_logits: bfloat16 [8192, 2048], P('ctx', 'tp'), may hold values from -1 to 16
- values: bfloat16 [8192, 2048], P('ctx', 'tp'), may hold values from -6 to 6
Outputs:
- grad_hidden: bfloat16 [8192, 2048], P('ctx', 'tp')
- grad_queries: bfloat16 [8192, 2048], P('ctx', 'tp')
- grad_logits: bfloat16 [8192, 2048], P('ctx', 'tp')
- grad_values: bfloat16 [8192, 2048], P('ctx', 'tp')
The draws below stay inside these ranges and needn't reach their ends.
Inputs may be any that keep to these rules, and one draw needn't show every extreme that they name: `expert_ids`: in the 128 rows of one block no expert is named more than 10 times; in some block one expert is named exactly 10 times.
All inputs are finite; a program needn't handle non-finite values.
Results may differ from the reference program's by a relative error of at most 0.0069.
Values may be sent and summed in bfloat16 or wider, within the bound.
No kernel may reach another device: no remote copies, remote signals or barrier semaphores. Data moves between devices by JAX's collectives and lax.ppermute only.
A program may use at most 192 MiB of HBM per device.

```python
import math
import jax
import jax.numpy as jnp
import numpy as np
from jax import lax

MODEL_DIMENSION = 2048
FF = 1536
HEADS = 32
HEAD_DIM = 64
TOP = 4
TOK_DEV = 128
TOKEN_COUNT = 8192
EXPERTS = 64
CAP = 10
N_CTX = 64


def draw_hidden(key, part):
    key = jax.random.fold_in(key, 5)
    key_base, key_rows, key_cols = jax.random.split(key, 3)
    position = jnp.arange(MODEL_DIMENSION, dtype=jnp.float32) / MODEL_DIMENSION
    column_scale = 0.3 * jnp.exp(math.log(10.0) * (0.6 * position + 0.4 * jax.random.uniform(key_cols, (MODEL_DIMENSION,))))
    base = jnp.clip(jax.random.normal(key_base, (TOKEN_COUNT, MODEL_DIMENSION)), -6.0, 6.0)
    row_scale = 0.3 * jnp.exp(math.log(10.0) * jax.random.uniform(key_rows, (TOKEN_COUNT, 1)))
    return (base * row_scale * column_scale[None, :]).astype(jnp.bfloat16)


def draw_forget_logits(key, part):
    key = jax.random.fold_in(key, 9)
    key_sequence = jax.random.split(key, 7)
    slow_share = 0.5
    head_slow = (jax.random.uniform(key_sequence[0], (HEADS,)) < slow_share).astype(jnp.float32)
    column_lag_factor = jnp.repeat(head_slow, HEAD_DIM)
    fast_rate = jnp.exp(jax.random.uniform(key_sequence[1], (MODEL_DIMENSION,), minval=math.log(1.0 / 50.0), maxval=math.log(1.0 / 30.0)))
    slow_rate = jnp.exp(jax.random.uniform(key_sequence[2], (MODEL_DIMENSION,), minval=math.log(0.15), maxval=math.log(0.8))) / TOKEN_COUNT
    baseline_rate = column_lag_factor * slow_rate + (1.0 - column_lag_factor) * fast_rate
    split_factor = jnp.repeat(jnp.exp(jax.random.uniform(key_sequence[3], (TOKEN_COUNT // TOK_DEV, MODEL_DIMENSION), minval=-0.35, maxval=0.35)), TOK_DEV, axis=0)
    random_noise = jnp.exp(jax.random.uniform(key_sequence[4], (TOKEN_COUNT, MODEL_DIMENSION), minval=-0.7, maxval=0.7))
    spike_rows = jax.random.randint(key_sequence[5], (3,), 0, TOKEN_COUNT)
    spike_flag = jnp.any(jnp.arange(TOKEN_COUNT)[:, None] == spike_rows[None, :], axis=1).astype(jnp.float32)
    spike_event = jax.random.uniform(key_sequence[6], (TOKEN_COUNT, MODEL_DIMENSION), minval=0.22, maxval=0.7) * spike_flag[:, None] * column_lag_factor[None, :]
    decay_rate = baseline_rate[None, :] * split_factor * random_noise + spike_event
    return (-jnp.log(jnp.expm1(decay_rate))).astype(jnp.bfloat16)


def block_scale(key, shape, pieces, smallest, largest):
    level, own = 1.0, jax.random.fold_in(key, 6)
    for dim, parts in pieces:
        heights = jnp.exp(jax.random.uniform(jax.random.fold_in(own, dim), (parts,), jnp.float32, smallest / len(pieces), largest / len(pieces)))
        level = level * jnp.repeat(heights, shape[dim] // parts).reshape([-1 if axis == dim else 1 for axis in range(len(shape))])
    return level


def assign_block(own_key, own, number, rows, count, top, bound, lean):
    sequence = jax.random.permutation(own_key, count)
    packed, common = load_shares(count, rows * top, bound, lean, True), load_shares(count, rows * top, bound, lean, False)
    places = jnp.arange(count)

    def named(sizes, offset_by):
        used = int((sizes > 0).sum())
        fixed = max(1, used // 4)
        passed = fixed + (places - fixed + offset_by * (used - fixed)) % max(1, count - fixed)
        return jnp.zeros((count,), jnp.int32).at[sequence[jnp.where(places < fixed, places, passed)]].set(jnp.asarray(sizes, jnp.int32))

    sizes = jnp.where(number % 4 == 0, named(packed, number // 4), named(common, number - number // 4 - 1))
    mixed = jax.random.permutation(jax.random.fold_in(own, 3), count)
    giver, sink = mixed[0:count // 2 * 2:2], mixed[1:count // 2 * 2:2]
    slack = jnp.minimum(sizes[giver] - 1, bound - sizes[sink]) // 2
    slack = jnp.where((giver == sequence[0]) | (sink == sequence[0]) | (sizes[sink] == 0), 0, jnp.maximum(slack, 0))
    passed = jax.random.randint(jax.random.fold_in(own, 4), (count // 2,), 0, 1 << 20) % (slack + 1)
    sizes = sizes.at[giver].add(-passed).at[sink].add(passed)
    items = jnp.searchsorted(jnp.cumsum(sizes), jnp.arange(rows * top), side="right").astype(jnp.int32)
    grid = items.reshape(top, rows).T
    grid = grid[jax.random.permutation(jax.random.fold_in(own, 1), rows)]
    offset_by = jax.random.randint(jax.random.fold_in(own, 2), (rows, 1), 0, top)
    return jnp.take_along_axis(grid, (jnp.arange(top)[None, :] + offset_by) % top, axis=1)


def load_shares(amount, total, reach, skew, full):
    portions = [(1 << 20) // math.isqrt(rank ** skew) + 1 for rank in range(1, amount + 1)]
    largest = reach if full else min(reach, max(-(-total // amount), total * portions[0] // sum(portions)))
    least = 1 if total - largest >= amount - 1 else 0
    holding, surplus = [largest] + [least] * (amount - 1), total - largest - least * (amount - 1)
    while surplus > 0:
        movable = [i for i in range(1, amount) if holding[i] < largest] or [i for i in range(1, amount) if holding[i] < reach]
        mass, left = sum([portions[i] for i in movable]), surplus
        for i in movable:
            addition = min(reach - holding[i], max(1, left * portions[i] // mass), surplus)
            holding[i] = holding[i] + addition
            surplus = surplus - addition
    return np.array(holding)


def centred(own_key, extent, deviation, reach, cuts=(), kind=jnp.bfloat16):
    gain = block_scale(own_key, extent, cuts, -0.22, 0.18) if cuts else 1.0
    drawn = jax.random.normal(own_key, extent, jnp.float32) * deviation * gain
    return jnp.minimum(jnp.maximum(drawn, -reach), reach).astype(kind)


def setup_inputs(seed: int = 0) -> dict:
    arg_keys = jax.random.split(jax.random.key(seed), 12)
    hidden = draw_hidden(jax.random.fold_in(arg_keys[11], 71), 0)
    grad_out = centred(arg_keys[1], (TOKEN_COUNT, MODEL_DIMENSION), 1.0, 6.0, ((0, 64), (1, 2)))
    expert_ids_keys = jax.random.split(jax.random.fold_in(arg_keys[2], 1), TOKEN_COUNT // TOK_DEV)
    expert_ids_turns = jax.random.permutation(jax.random.fold_in(arg_keys[2], 3), TOKEN_COUNT // TOK_DEV)
    expert_ids = jax.vmap(lambda own, number: assign_block(jax.random.fold_in(arg_keys[2], 2), own, number, TOK_DEV, EXPERTS, TOP, CAP, 2))(expert_ids_keys, expert_ids_turns).reshape((TOKEN_COUNT, TOP))
    gate_weights = jnp.clip(jnp.exp(math.log(1.0) - 2.3025851 * jax.random.uniform(arg_keys[3], (TOKEN_COUNT, TOP), jnp.float32) ** block_scale(arg_keys[3], (TOKEN_COUNT, TOP), ((0, 64),), -0.2, 0.2)), 0.1, 1.0)
    norm_gain = jnp.clip(1.0 + 0.15 * jax.random.normal(arg_keys[4], (MODEL_DIMENSION,), jnp.float32), 0.25, 1.75)
    w_gate = centred(arg_keys[5], (EXPERTS, MODEL_DIMENSION, FF), MODEL_DIMENSION ** -0.5, 0.125, ((0, 64), (2, 2)))
    w_up = centred(arg_keys[6], (EXPERTS, MODEL_DIMENSION, FF), MODEL_DIMENSION ** -0.5, 0.125, ((0, 64), (2, 2)))
    w_down = centred(arg_keys[7], (EXPERTS, FF, MODEL_DIMENSION), FF ** -0.5, 0.15625, ((0, 64), (1, 2)))
    queries = centred(arg_keys[8], (TOKEN_COUNT, MODEL_DIMENSION), 1.0, 6.0, ((0, 64), (1, 2)))
    forget_logits = draw_forget_logits(jax.random.fold_in(arg_keys[11], 71), 0)
    values = centred(arg_keys[10], (TOKEN_COUNT, MODEL_DIMENSION), 1.0, 6.0, ((0, 64), (1, 2)))
    return dict(hidden=hidden, grad_out=grad_out, expert_ids=expert_ids, gate_weights=gate_weights, norm_gain=norm_gain, w_gate=w_gate, w_up=w_up, w_down=w_down, queries=queries, forget_logits=forget_logits, values=values)


NORM_EPS = 1e-06
EXACT_PRECISION = lax.Precision.HIGHEST

def slot_tables(routed, weighting, capacity, expert_count):
    entries = routed.reshape(-1).astype(jnp.int32)
    entry_count = entries.shape[0]
    one_hot = (entries[:, None] == jnp.arange(expert_count, dtype=jnp.int32)[None, :]).astype(jnp.int32)
    ranking = lax.optimization_barrier(jnp.sum((jnp.cumsum(one_hot, axis=0) - 1) * one_hot, axis=1)).astype(jnp.int32)
    slot_index = (entries * capacity + ranking).astype(jnp.int32)
    entry_of_slot = jnp.zeros((expert_count * capacity,), jnp.int32).at[slot_index].set(jnp.arange(entry_count, dtype=jnp.int32))
    filled = jnp.zeros((expert_count * capacity,), jnp.float32).at[slot_index].set(1.0)
    slot_weight = filled * weighting.reshape(-1)[entry_of_slot].astype(jnp.float32)
    slot_token = (entry_of_slot // routed.shape[1]).astype(jnp.int32)
    return (slot_index, slot_token, slot_weight)

def expert_grads(rows_in, rows_cot, gate_mat, up_mat, down_mat):
    pre_gate = jnp.dot(rows_in, gate_mat, preferred_element_type=jnp.float32)
    pre_up = jnp.dot(rows_in, up_mat, preferred_element_type=jnp.float32)
    gate_sig = jax.nn.sigmoid(pre_gate)
    d_act = lax.dot_general(rows_cot, down_mat, (((1,), (1,)), ((), ())), preferred_element_type=jnp.float32)
    d_gate = (d_act * pre_up * gate_sig * (1.0 + pre_gate * (1.0 - gate_sig))).astype(jnp.bfloat16)
    d_up = (d_act * pre_gate * gate_sig).astype(jnp.bfloat16)
    back_gate = lax.dot_general(d_gate, gate_mat, (((1,), (1,)), ((), ())), preferred_element_type=jnp.float32)
    back_up = lax.dot_general(d_up, up_mat, (((1,), (1,)), ((), ())), preferred_element_type=jnp.float32)
    return back_gate + back_up

def decay_terms(logit_in):
    raw_logits = logit_in.astype(jnp.float32)
    return (jax.nn.sigmoid(-raw_logits), jax.nn.log_sigmoid(raw_logits))

def block_grads(query_input, key_input, running_total, value_input, upstream_gradient, initial_state, incoming_gradient, decay_end, local_state, lower_tri):
    upper_tri = lower_tri.T
    growth_factor = jnp.exp(running_total)
    shrink_factor = jnp.exp(-running_total)
    query_scaled = query_input * growth_factor
    key_scaled = key_input * shrink_factor
    carried_state = decay_end[:, :, None] * incoming_gradient
    pair_output_value = jnp.einsum('thv,shv->hts', upstream_gradient, value_input, precision=EXACT_PRECISION) * lower_tri[None]
    query_gradient = growth_factor * (jnp.einsum('sdl,dol->sdo', upstream_gradient, initial_state, precision=EXACT_PRECISION) + jnp.einsum('xgq,qxu->gxu', pair_output_value, key_scaled, precision=EXACT_PRECISION))
    pair_value_output = jnp.einsum('thv,shv->hts', value_input, upstream_gradient, precision=EXACT_PRECISION) * upper_tri[None]
    key_gradient = shrink_factor * (jnp.einsum('xgq,qxu->gxu', pair_value_output, query_scaled, precision=EXACT_PRECISION) + jnp.einsum('sdl,dol->sdo', value_input, carried_state, precision=EXACT_PRECISION))
    pair_key_query = jnp.einsum('thk,shk->hts', key_scaled, query_scaled, precision=EXACT_PRECISION) * upper_tri[None]
    value_gradient = jnp.einsum('xuk,kxf->uxf', pair_key_query, upstream_gradient, precision=EXACT_PRECISION) + jnp.einsum('ale,lej->alj', key_scaled, carried_state, precision=EXACT_PRECISION)
    final_state = decay_end[:, :, None] * initial_state + local_state
    past_limit = jnp.einsum('rfp,rfp->rf', final_state, incoming_gradient, precision=EXACT_PRECISION)
    cumul_grad = query_input * query_gradient - key_input * key_gradient
    suffix = jnp.einsum('st,shk->thk', lower_tri, cumul_grad, precision=EXACT_PRECISION) + past_limit[None]
    logit_grad = suffix * key_input - key_gradient * key_input * (1.0 - key_input)
    return (query_gradient, logit_grad, value_gradient)

def to_blocks(array):
    return array.astype(jnp.float32).reshape(N_CTX, TOK_DEV, HEADS, HEAD_DIM)

def reference(hidden, grad_out, expert_ids, gate_weights, norm_gain, w_gate, w_up, w_down, queries, forget_logits, values):
    hidden_f = hidden.astype(jnp.float32)
    row_scale = lax.rsqrt(lax.optimization_barrier(jnp.mean(hidden_f * hidden_f, axis=1)) + NORM_EPS)
    normed = (hidden_f * row_scale[:, None] * norm_gain[None, :]).astype(jnp.bfloat16)

    def tables(routed, weighting):
        return slot_tables(routed, weighting, CAP, EXPERTS)
    slot_index, slot_token, slot_weight = jax.vmap(tables)(expert_ids.reshape(N_CTX, TOK_DEV, TOP), gate_weights.reshape(N_CTX, TOK_DEV, TOP))
    global_token = (slot_token + (jnp.arange(N_CTX, dtype=jnp.int32) * TOK_DEV)[:, None]).astype(jnp.int32)
    slot_rows = normed[global_token.reshape(-1)].reshape(N_CTX, EXPERTS, CAP, MODEL_DIMENSION)
    slot_cot = (slot_weight.reshape(-1)[:, None] * grad_out[global_token.reshape(-1)].astype(jnp.float32)).astype(jnp.bfloat16)
    slot_cot = slot_cot.reshape(N_CTX, EXPERTS, CAP, MODEL_DIMENSION)
    rows_by_expert = jnp.moveaxis(slot_rows, 1, 0).reshape(EXPERTS, N_CTX * CAP, MODEL_DIMENSION)
    cot_by_expert = jnp.moveaxis(slot_cot, 1, 0).reshape(EXPERTS, N_CTX * CAP, MODEL_DIMENSION)

    def one_expert(pack):
        rows_in, rows_cot, gate_mat, up_mat, down_mat = pack
        return expert_grads(rows_in, rows_cot, gate_mat, up_mat, down_mat).astype(jnp.bfloat16)
    slot_grad = lax.map(one_expert, (rows_by_expert, cot_by_expert, w_gate, w_up, w_down))
    flat_slot = (slot_index // CAP * (N_CTX * CAP) + (jnp.arange(N_CTX, dtype=jnp.int32) * CAP)[:, None] + slot_index % CAP).astype(jnp.int32)
    per_entry = slot_grad.reshape(EXPERTS * N_CTX * CAP, MODEL_DIMENSION)[flat_slot.reshape(-1)].astype(jnp.float32)
    normed_grad = lax.optimization_barrier(jnp.sum(per_entry.reshape(TOKEN_COUNT, TOP, MODEL_DIMENSION), axis=1))
    gained = normed_grad * norm_gain[None, :]
    dotted = lax.optimization_barrier(jnp.sum(gained * hidden_f, axis=1))
    norm_back = row_scale[:, None] * gained - hidden_f * (row_scale ** 3 * dotted / MODEL_DIMENSION)[:, None]
    grad_hidden = (grad_out.astype(jnp.float32) + norm_back).astype(jnp.bfloat16)
    query_b = to_blocks(queries)
    value_b = to_blocks(values)
    upstream_b = to_blocks(grad_hidden)
    key_b, log_b = decay_terms(to_blocks(forget_logits))
    cumul_b = jnp.cumsum(log_b, axis=1)
    decay_b = jnp.exp(cumul_b[:, -1])
    local_b = jnp.einsum('blhk,blhv->bhkv', key_b * jnp.exp(cumul_b[:, -1:] - cumul_b), value_b, precision=EXACT_PRECISION)
    grad_elem_b = jnp.einsum('blhk,blhv->bhkv', query_b * jnp.exp(cumul_b), upstream_b, precision=EXACT_PRECISION)

    def chain_step(carry_state, element):
        decay_end, local_term = element
        return (decay_end[:, :, None] * carry_state + local_term, carry_state)
    empty_state = jnp.zeros((HEADS, HEAD_DIM, HEAD_DIM), jnp.float32)
    _, starts = lax.scan(chain_step, empty_state, (decay_b, local_b))
    _, incomings = lax.scan(chain_step, empty_state, (decay_b, grad_elem_b), reverse=True)
    positions = jnp.arange(TOK_DEV)
    lower_tri = (positions[:, None] >= positions[None, :]).astype(jnp.float32)

    def run_block(pack):
        query_input, key_input, running_total, value_input, upstream_gradient, initial_state, incoming_gradient, decay_end, local_state = pack
        return block_grads(query_input, key_input, running_total, value_input, upstream_gradient, initial_state, incoming_gradient, decay_end, local_state, lower_tri)
    query_gradient, logit_grad, value_gradient = lax.map(run_block, (query_b, key_b, cumul_b, value_b, upstream_b, starts, incomings, decay_b, local_b))
    return (grad_hidden, query_gradient.reshape(TOKEN_COUNT, MODEL_DIMENSION).astype(jnp.bfloat16), logit_grad.reshape(TOKEN_COUNT, MODEL_DIMENSION).astype(jnp.bfloat16), value_gradient.reshape(TOKEN_COUNT, MODEL_DIMENSION).astype(jnp.bfloat16))
```

```python
import functools

import jax
import jax.numpy as jnp
from jax import lax
from jax.experimental import pallas as pl
from jax.experimental.pallas import tpu as pltpu
from jax.sharding import PartitionSpec as P

HEAD_DIM = 64
NORM_EPS = 1e-06
LANES = 128
BF16 = jnp.bfloat16
F32 = jnp.float32
EXACT = lax.Precision.HIGHEST
NT = (((1,), (1,)), ((), ()))
TN = (((0,), (0,)), ((), ()))
NN = (((1,), (0,)), ((), ()))


def iota(shape, dim):
    return lax.broadcasted_iota(jnp.int32, shape, dim)


def exact_dot(a, b, dims=NN):
    return lax.dot_general(a, b, dims, precision=EXACT, preferred_element_type=F32)


def fast_dot(a, b, dims=NN):
    return lax.dot_general(a, b, dims, preferred_element_type=F32)


def call(kernel, out_shape, *args, scratch=(), in_specs=None, mib=48, flops=0, nbytes=0):
    return pl.pallas_call(
        kernel,
        out_shape=out_shape,
        in_specs=in_specs or [pl.BlockSpec(memory_space=pltpu.VMEM)] * len(args),
        out_specs=jax.tree.map(lambda _: pl.BlockSpec(memory_space=pltpu.VMEM), out_shape),
        scratch_shapes=list(scratch),
        compiler_params=pltpu.CompilerParams(vmem_limit_bytes=mib << 20),
        cost_estimate=pl.CostEstimate(flops=flops, bytes_accessed=nbytes, transcendentals=0),
    )(*args)


def shape_of(shape, dtype):
    return jax.ShapeDtypeStruct(shape, dtype)


def ranked(ids_ref):
    rows = ids_ref.shape[0]
    lane = iota((rows, LANES), 1)
    named = jnp.zeros((rows, LANES), F32)
    for choice in range(ids_ref.shape[1]):
        named = named + (ids_ref[:, choice : choice + 1] == lane).astype(F32)
    before = (iota((rows, rows), 1) < iota((rows, rows), 0)).astype(BF16)
    rank = fast_dot(before, named.astype(BF16))
    return jnp.where(named > 0.0, rank, -1.0)


def dispatch_kernel(hidden_ref, cot_ref, squares_ref, gain_ref, ids_ref, weight_ref, width, out_ref, rhs, rhs_rem):
    rows = hidden_ref.shape[0]
    row_scale = lax.rsqrt(squares_ref[...] / width + NORM_EPS)
    normed = (hidden_ref[...].astype(F32) * row_scale * gain_ref[...]).astype(BF16)
    rhs[0:rows, :] = normed
    rhs[rows : 2 * rows, :] = cot_ref[...]
    for j in range(8):
        lo, col = 2 * rows * (j % 4), LANES * (j // 4)
        rhs_rem[lo : lo + rows, col : col + LANES] = normed[:, j * LANES : (j + 1) * LANES]
        rhs_rem[lo + rows : lo + 2 * rows, col : col + LANES] = cot_ref[:, j * LANES : (j + 1) * LANES]
    rank = ranked(ids_ref).T
    lane = iota((rows, LANES), 1)
    weight = jnp.zeros((rows, LANES), F32)
    for choice in range(ids_ref.shape[1]):
        weight = weight + jnp.where(
            ids_ref[:, choice : choice + 1] == lane, weight_ref[:, choice : choice + 1], 0.0
        )
    weight = weight.T
    rank_b = rank.astype(BF16)
    for group in range(8):
        expand = (iota((128, LANES), 0) // 16 + group * 8 == iota((128, LANES), 1)).astype(BF16)
        ranks = fast_dot(expand, rank_b)
        weights = exact_dot(expand.astype(F32), weight)
        inner = iota((128, LANES), 0) % 16
        hit = ranks == (inner % 8).astype(F32)
        is_cot = inner >= 8
        left = jnp.concatenate([hit & ~is_cot, hit & is_cot], axis=1).astype(BF16)
        scale = jnp.sum(jnp.where(hit & is_cot, weights, 0.0), axis=1, keepdims=True)
        scale = jnp.where(is_cot[:, :1], scale, 1.0)
        main = (fast_dot(left, rhs[...]) * scale).astype(BF16)
        for j in range(8):
            out_ref[group * 8 : group * 8 + 8, j * 16 : (j + 1) * 16, :] = main[
                :, j * LANES : (j + 1) * LANES
            ].reshape(8, 16, LANES)
        hit = ranks == (8 + inner % 2).astype(F32)
        is_cot = (inner // 2) % 2 == 1
        parts = []
        for j in range(4):
            here = hit & (inner // 4 == j)
            parts += [here & ~is_cot, here & is_cot]
        left = jnp.concatenate(parts, axis=1).astype(BF16)
        scale = jnp.sum(jnp.where(hit & is_cot, weights, 0.0), axis=1, keepdims=True)
        scale = jnp.where(is_cot[:, :1], scale, 1.0)
        rest = (fast_dot(left, rhs_rem[...]) * scale).astype(BF16)
        for half in range(2):
            out_ref[group * 8 : group * 8 + 8, 128 + 16 * half : 144 + 16 * half, :] = rest[
                :, half * LANES : (half + 1) * LANES
            ].reshape(8, 16, LANES)


def table_kernel(ids_ref, main_ref, rest_ref):
    rank = ranked(ids_ref).astype(BF16)
    count = main_ref.shape[1]
    expand = (iota((LANES, count), 1) // 16 == iota((LANES, count), 0)).astype(BF16)
    ranks = fast_dot(rank, expand)
    inner = iota(ranks.shape, 1) % 16
    hit = ranks == (inner % 8).astype(F32)
    rows = ranks.shape[0]
    main_ref[0:rows, :] = (hit & (inner < 8)).astype(BF16)
    main_ref[rows : 2 * rows, :] = (hit & (inner >= 8)).astype(BF16)
    hit = ranks == (8 + inner % 2).astype(F32)
    for j in range(8):
        rest_ref[j * rows : (j + 1) * rows, :] = (hit & (inner // 2 == j)).astype(BF16)


def unpack(raw_ref, x_ref, c_ref, offset):
    count = raw_ref.shape[0]
    for j in range(8):
        tile = raw_ref[:, j * 16 : (j + 1) * 16, :].astype(F32).reshape(count, 2, 8, LANES)
        cols = pl.ds(pl.multiple_of(offset + j * LANES, LANES), LANES)
        x_ref[0 : count * 8, cols] = tile[:, 0].reshape(count * 8, LANES).astype(BF16)
        c_ref[0 : count * 8, cols] = tile[:, 1].reshape(count * 8, LANES).astype(BF16)
    row = iota((128, 128), 0)
    source = (row // 2) % 4 * 32 + row // 16 * 4 + (row // 8) % 2 * 2 + row % 2
    perm = (iota((128, 128), 1) == source).astype(BF16)
    groups = count // 4
    rest = jnp.concatenate(
        [raw_ref[g * 4 : (g + 1) * 4, 128:160, :].reshape(128, LANES) for g in range(groups)], axis=1
    )
    rest = fast_dot(perm, rest)
    for j in range(8):
        cols = pl.ds(pl.multiple_of(offset + j * LANES, LANES), LANES)
        for kind, ref in enumerate((x_ref, c_ref)):
            lo = j * 16 + kind * 8
            ref[count * 8 : count * 10, cols] = jnp.concatenate(
                [rest[lo : lo + 8, g * LANES : (g + 1) * LANES] for g in range(groups)], axis=0
            ).astype(BF16)


def expert_kernel(
    core_ref, own_ref, peer_ref, gate_hbm, up_hbm, down_hbm, keep_ref, send_ref, x, c, gate, up, down, dg, du, sems
):
    copies = [
        pltpu.make_async_copy(source, target, sems.at[number])
        for number, (source, target) in enumerate(((gate_hbm, gate), (up_hbm, up), (down_hbm, down)))
    ]
    for copy in copies:
        copy.start()
    core = core_ref[0]
    half = keep_ref.shape[1]
    unpack(own_ref, x, c, core * half)
    unpack(peer_ref, x, c, (1 - core) * half)
    for copy in copies:
        copy.wait()

    @pl.loop(0, gate.shape[1] // 256)
    def _(step):
        cols = pl.ds(pl.multiple_of(step * 256, 256), 256)
        pre_gate = fast_dot(x[...], gate[:, cols])
        pre_up = fast_dot(x[...], up[:, cols])
        d_act = fast_dot(c[...], down[cols, :], NT)
        sig = jax.nn.sigmoid(pre_gate)
        dg[:, cols] = (d_act * pre_up * sig * (1.0 + pre_gate * (1.0 - sig))).astype(BF16)
        du[:, cols] = (d_act * pre_gate * sig).astype(BF16)

    @pl.loop(0, half // 256)
    def _(step):
        cols = pl.ds(pl.multiple_of(step * 256, 256), 256)
        for ref, first in ((send_ref, (1 - core) * half), (keep_ref, core * half)):
            feats = pl.ds(pl.multiple_of(first + step * 256, 256), 256)
            value = fast_dot(dg[...], gate[feats, :], NT) + fast_dot(du[...], up[feats, :], NT)
            ref[:, cols] = value.astype(ref.dtype)


def pack_kernel(keep_ref, got_ref, out_ref):
    count = out_ref.shape[0]
    for pair in range(4):
        tiles = []
        for j in (2 * pair, 2 * pair + 1):
            cols = slice(j * LANES, (j + 1) * LANES)
            value = keep_ref[0 : count * 8, cols] + got_ref[0 : count * 8, cols].astype(F32)
            tiles.append(value.reshape(count, 8, LANES))
        out_ref[:, pair * 16 : (pair + 1) * 16, :] = jnp.concatenate(tiles, axis=1).astype(BF16)
    rest = (keep_ref[count * 8 :, :] + got_ref[count * 8 :, :].astype(F32)).astype(BF16)
    row = iota((128, 128), 0)
    source = (row // 2) % 8 * 16 + row // 16 * 2 + row % 2
    perm = (iota((128, 128), 1) == source).astype(BF16)
    groups = count // 8
    stacked = jnp.concatenate(
        [
            jnp.concatenate(
                [rest[g * 16 : (g + 1) * 16, j * LANES : (j + 1) * LANES] for j in range(8)], axis=0
            )
            for g in range(groups)
        ],
        axis=1,
    )
    moved = fast_dot(perm, stacked).astype(BF16)
    for g in range(groups):
        out_ref[g * 8 : (g + 1) * 8, 64:80, :] = moved[:, g * LANES : (g + 1) * LANES].reshape(8, 16, LANES)


def combine_kernel(back_ref, main_ref, rest_ref, hidden_ref, gain_ref, gained_ref, dot_ref):
    count = back_ref.shape[0]
    rows = hidden_ref.shape[0]
    main = jnp.concatenate(
        [back_ref[:, m * 16 : (m + 1) * 16, :].reshape(count * 16, LANES) for m in range(4)], axis=1
    )
    main = fast_dot(main_ref[...], main)
    rest = fast_dot(rest_ref[...], back_ref[:, 64:80, :].reshape(count * 16, LANES))
    total = jnp.zeros((rows, LANES), F32)
    for j in range(8):
        cols = slice(j * LANES, (j + 1) * LANES)
        value = main[j % 2 * rows : (j % 2 + 1) * rows, j // 2 * LANES : (j // 2 + 1) * LANES]
        value = (value + rest[j * rows : (j + 1) * rows, :]) * gain_ref[:, cols]
        gained_ref[:, cols] = value
        total = total + value * hidden_ref[:, cols].astype(F32)
    dot_ref[...] = jnp.sum(total, axis=1, keepdims=True)


def log_sigmoid(x):
    return -(jnp.maximum(-x, 0.0) + jnp.log1p(jnp.exp(-jnp.abs(x))))


def decay_kernel(logit_ref, value_ref, total_ref, state_ref):
    rows, feats = logit_ref.shape
    logits = logit_ref[...].astype(F32)
    key = jax.nn.sigmoid(-logits)
    lower = (iota((rows, rows), 0) >= iota((rows, rows), 1)).astype(F32)
    running = exact_dot(lower, log_sigmoid(logits))
    total_ref[...] = running
    end = running[rows - 1 : rows, :]
    key_end = key * jnp.exp(end - running)
    decay = jnp.exp(end)
    same = iota((LANES, LANES), 0) // HEAD_DIM == iota((LANES, LANES), 1) // HEAD_DIM
    pick = iota((HEAD_DIM, LANES), 0) == iota((HEAD_DIM, LANES), 1) % HEAD_DIM
    for pair in range(feats // LANES):
        cols = slice(pair * LANES, (pair + 1) * LANES)
        local = exact_dot(key_end[:, cols], value_ref[:, cols].astype(F32), TN)
        local = jnp.where(same, local, 0.0)
        local = local[:HEAD_DIM] + local[HEAD_DIM:]
        spread = exact_dot(jnp.where(pick, decay[:, cols], 0.0), same.astype(F32))
        for part in range(8):
            state_ref[pair * 8 + part, 0:8, :] = local[part * 8 : (part + 1) * 8, :]
            state_ref[pair * 8 + part, 8:16, :] = spread[part * 8 : (part + 1) * 8, :]


def forward_kernel(piece_ref, out_ref):
    count = piece_ref.shape[0]
    state = jnp.zeros((8, LANES), F32)
    for block in range(count):
        out_ref[block] = state
        state = piece_ref[block, 8:16, :] * state + piece_ref[block, 0:8, :]


def backward_kernel(piece_ref, decay_ref, out_ref):
    count = piece_ref.shape[0]
    state = jnp.zeros((8, LANES), F32)
    for block in range(count - 1, -1, -1):
        out_ref[block] = state
        state = decay_ref[block, 8:16, :] * state + piece_ref[block]


def hidden_kernel(
    hidden_ref, cot_ref, squares_ref, gained_ref, dot_ref, query_ref, total_ref, width, out_ref, piece_ref
):
    row_scale = lax.rsqrt(squares_ref[...] / width + NORM_EPS)
    back = row_scale * gained_ref[...] - hidden_ref[...].astype(F32) * (
        row_scale * row_scale * row_scale * dot_ref[...] / width
    )
    upstream = (cot_ref[...].astype(F32) + back).astype(BF16)
    out_ref[...] = upstream
    query = query_ref[...].astype(F32) * jnp.exp(total_ref[...])
    same = iota((LANES, LANES), 0) // HEAD_DIM == iota((LANES, LANES), 1) // HEAD_DIM
    for pair in range(hidden_ref.shape[1] // LANES):
        cols = slice(pair * LANES, (pair + 1) * LANES)
        elem = exact_dot(query[:, cols], upstream[:, cols].astype(F32), TN)
        elem = jnp.where(same, elem, 0.0)
        elem = elem[:HEAD_DIM] + elem[HEAD_DIM:]
        piece_ref[pair * 8 : (pair + 1) * 8] = elem.reshape(8, 8, LANES)


def final_kernel(
    query_ref,
    logit_ref,
    value_ref,
    total_ref,
    upstream_ref,
    start_ref,
    incoming_ref,
    state_ref,
    query_out,
    logit_out,
    value_out,
):
    rows, feats = query_ref.shape
    lower = iota((rows, rows), 0) >= iota((rows, rows), 1)
    upper = iota((rows, rows), 0) <= iota((rows, rows), 1)
    same = iota((LANES, LANES), 0) // HEAD_DIM == iota((LANES, LANES), 1) // HEAD_DIM
    first = iota((rows, LANES), 1) < HEAD_DIM

    def split(array):
        zero = jnp.zeros_like(array)
        return jnp.where(first, array, zero), jnp.where(first, zero, array)

    def spread(array):
        return jnp.where(same, jnp.concatenate([array, array], axis=0), 0.0)

    for pair in range(feats // LANES):
        cols = slice(pair * LANES, (pair + 1) * LANES)
        eight = slice(pair * 8, (pair + 1) * 8)
        query = query_ref[:, cols].astype(F32)
        logits = logit_ref[:, cols].astype(F32)
        key = jax.nn.sigmoid(-logits)
        running = total_ref[:, cols]
        end = running[rows - 1 : rows, :]
        centre = 0.5 * end
        grow = jnp.exp(running - centre)
        shrink = jnp.exp(centre - running)
        value = value_ref[:, cols]
        upstream = upstream_ref[:, cols]
        value_f, upstream_f = value.astype(F32), upstream.astype(F32)
        start = start_ref[eight].reshape(HEAD_DIM, LANES)
        incoming = incoming_ref[eight].reshape(HEAD_DIM, LANES)
        local = state_ref[eight, 0:8, :].reshape(HEAD_DIM, LANES)
        decay = state_ref[eight, 8:16, :].reshape(HEAD_DIM, LANES)
        start_2, incoming_2 = spread(start), spread(incoming)
        query_s, key_s = query * grow, key * shrink
        up_split, value_split = split(upstream), split(value)
        query_split, key_split = split(query_s), split(key_s)
        raw = [fast_dot(u, v, NT) for u, v in zip(up_split, value_split)]
        pairs = jnp.concatenate([jnp.where(lower, r, 0.0) for r in raw], axis=1)
        query_grad = jnp.exp(running) * exact_dot(upstream_f, start_2, NT) + grow * exact_dot(
            pairs, jnp.concatenate(key_split, axis=0)
        )
        raw = [fast_dot(v, u, NT) for u, v in zip(up_split, value_split)]
        pairs = jnp.concatenate([jnp.where(upper, r, 0.0) for r in raw], axis=1)
        tail = jnp.exp(end - running)
        key_grad = tail * exact_dot(value_f, incoming_2, NT) + shrink * exact_dot(
            pairs, jnp.concatenate(query_split, axis=0)
        )
        raw = [exact_dot(k, q, NT) for k, q in zip(key_split, query_split)]
        pairs = jnp.concatenate([jnp.where(upper, r, 0.0) for r in raw], axis=1)
        value_grad = exact_dot(
            pairs, jnp.concatenate([u.astype(F32) for u in up_split], axis=0)
        ) + exact_dot(key * tail, incoming_2)
        past = spread((decay * start + local) * incoming)
        past = exact_dot(jnp.ones((8, LANES), F32), past, NT)[0:1, :]
        suffix = exact_dot(upper.astype(F32), query * query_grad - key * key_grad) + past
        logit_grad = suffix * key - key_grad * key * (1.0 - key)
        query_out[:, cols] = query_grad.astype(BF16)
        logit_out[:, cols] = logit_grad.astype(BF16)
        value_out[:, cols] = value_grad.astype(BF16)


def on_device(
    hidden, grad_out, expert_ids, gate_weights, norm_gain, w_gate, w_up, w_down, queries, forget_logits, values
):
    rows, feats = hidden.shape
    ctx = lax.axis_size("ctx")
    width = w_gate.shape[1]
    units = w_gate.shape[2]
    slots = ctx * 10
    core = lax.axis_index("tp")
    swap = [(0, 1), (1, 0)]
    gain = norm_gain.reshape(1, feats)

    def exchange(array):
        return lax.all_to_all(array, "ctx", split_axis=0, concat_axis=0, tiled=True)

    hidden_f = hidden.astype(F32)
    squares = lax.psum(jnp.sum(hidden_f * hidden_f, axis=1), "tp").reshape(rows, 1)

    sent = call(
        lambda h, g, s, n, i, w, o, a, b: dispatch_kernel(h, g, s, n, i, w, width, o, a, b),
        shape_of((ctx, 160, LANES), BF16),
        hidden,
        grad_out,
        squares,
        gain,
        expert_ids,
        gate_weights,
        scratch=(pltpu.VMEM((2 * rows, feats), BF16), pltpu.VMEM((8 * rows, 2 * LANES), BF16)),
        flops=1 << 30,
        nbytes=4 << 20,
    )
    own = exchange(sent)
    main_table, rest_table = call(
        table_kernel,
        (shape_of((2 * rows, ctx * 16), BF16), shape_of((8 * rows, ctx * 16), BF16)),
        expert_ids,
        flops=1 << 26,
        nbytes=3 << 20,
    )
    total, state = call(
        decay_kernel,
        (shape_of((rows, feats), F32), shape_of((ctx, 16, LANES), F32)),
        forget_logits,
        values,
        flops=1 << 30,
        nbytes=2 << 20,
    )
    pieces = exchange(state)
    starts = exchange(call(forward_kernel, shape_of((ctx, 8, LANES), F32), pieces, nbytes=1 << 20))

    peer = lax.ppermute(own, "tp", swap)
    vmem, hbm = pl.BlockSpec(memory_space=pltpu.VMEM), pl.BlockSpec(memory_space=pl.ANY)
    keep, send = call(
        expert_kernel,
        (shape_of((slots, feats), F32), shape_of((slots, feats), BF16)),
        core.reshape(1).astype(jnp.int32),
        own,
        peer,
        w_gate[0],
        w_up[0],
        w_down[0],
        in_specs=[pl.BlockSpec(memory_space=pltpu.SMEM), vmem, vmem, hbm, hbm, hbm],
        scratch=(
            pltpu.VMEM((slots, width), BF16),
            pltpu.VMEM((slots, width), BF16),
            pltpu.VMEM((width, units), BF16),
            pltpu.VMEM((width, units), BF16),
            pltpu.VMEM((units, width), BF16),
            pltpu.VMEM((slots, units), BF16),
            pltpu.VMEM((slots, units), BF16),
            pltpu.SemaphoreType.DMA((3,)),
        ),
        flops=10 * slots * width * units,
        nbytes=20 << 20,
    )
    got = lax.ppermute(send, "tp", swap)
    packed = call(pack_kernel, shape_of((ctx, 80, LANES), BF16), keep, got, flops=1 << 26, nbytes=6 << 20)
    back = exchange(packed)
    gained, dots = call(
        combine_kernel,
        (shape_of((rows, feats), F32), shape_of((rows, 1), F32)),
        back,
        main_table,
        rest_table,
        hidden,
        gain,
        flops=1 << 29,
        nbytes=6 << 20,
    )
    dots = lax.psum(dots, "tp")
    grad_hidden, piece = call(
        lambda h, g, s, a, d, q, t, o, p: hidden_kernel(h, g, s, a, d, q, t, width, o, p),
        (shape_of((rows, feats), BF16), shape_of((ctx, 8, LANES), F32)),
        hidden,
        grad_out,
        squares,
        gained,
        dots,
        queries,
        total,
        flops=1 << 28,
        nbytes=3 << 20,
    )
    incoming = exchange(
        call(backward_kernel, shape_of((ctx, 8, LANES), F32), exchange(piece), pieces, nbytes=1 << 20)
    )
    grad_queries, grad_logits, grad_values = call(
        final_kernel,
        (shape_of((rows, feats), BF16),) * 3,
        queries,
        forget_logits,
        values,
        total,
        grad_hidden,
        starts,
        incoming,
        state,
        flops=1 << 30,
        nbytes=4 << 20,
    )
    return grad_hidden, grad_queries, grad_logits, grad_values


def solution(mesh):
    rows = P("ctx", "tp")
    in_specs = (
        rows,
        rows,
        P("ctx", None),
        P("ctx", None),
        P("tp"),
        P("ctx", None, "tp"),
        P("ctx", None, "tp"),
        P("ctx", "tp", None),
        rows,
        rows,
        rows,
    )
    return jax.shard_map(on_device, mesh=mesh, in_specs=in_specs, out_specs=(rows,) * 4, check_vma=False)
```

```python
import functools

import jax
import jax.numpy as jnp
from jax import lax
from jax.experimental import pallas as pl
from jax.experimental.pallas import tpu as pltpu
from jax.sharding import PartitionSpec as P

HEAD_DIM = 64
NORM_EPS = 1e-06
LANES = 128
BF16 = jnp.bfloat16
F32 = jnp.float32
EXACT = lax.Precision.HIGHEST
NT = (((1,), (1,)), ((), ()))
TN = (((0,), (0,)), ((), ()))
NN = (((1,), (0,)), ((), ()))


def iota(shape, dim):
    return lax.broadcasted_iota(jnp.int32, shape, dim)


def exact_dot(a, b, dims=NN):
    return lax.dot_general(a, b, dims, precision=EXACT, preferred_element_type=F32)


def fast_dot(a, b, dims=NN):
    return lax.dot_general(a, b, dims, preferred_element_type=F32)


def call(kernel, out_shape, *args, scratch=(), in_specs=None, mib=48, flops=0, nbytes=0):
    return pl.pallas_call(
        kernel,
        out_shape=out_shape,
        in_specs=in_specs or [pl.BlockSpec(memory_space=pltpu.VMEM)] * len(args),
        out_specs=jax.tree.map(lambda _: pl.BlockSpec(memory_space=pltpu.VMEM), out_shape),
        scratch_shapes=list(scratch),
        compiler_params=pltpu.CompilerParams(vmem_limit_bytes=mib << 20),
        cost_estimate=pl.CostEstimate(flops=flops, bytes_accessed=nbytes, transcendentals=0),
    )(*args)


def shape_of(shape, dtype):
    return jax.ShapeDtypeStruct(shape, dtype)


def ranked(ids_ref, count):
    rows = ids_ref.shape[1]
    named = named_by(ids_ref, count)
    before = (iota((rows, rows), 0) < iota((rows, rows), 1)).astype(BF16)
    rank = fast_dot(named.astype(BF16), before)
    return jnp.where(named > 0.0, rank, -1.0)


def named_by(ids_ref, count, weight_ref=None):
    expert = iota((count, ids_ref.shape[1]), 0)
    total = jnp.zeros(expert.shape, F32)
    for choice in range(ids_ref.shape[0]):
        level = 1.0 if weight_ref is None else weight_ref[choice : choice + 1, :]
        total = total + jnp.where(ids_ref[choice : choice + 1, :] == expert, level, 0.0)
    return total


def column(row):
    count = row.shape[1]
    eye = iota((count, count), 0) == iota((count, count), 1)
    return jnp.sum(jnp.where(eye, row, 0.0), axis=1, keepdims=True)


def row_scale_of(own_ref, peer_ref, width):
    return lax.rsqrt(column(own_ref[...] + peer_ref[...]) / width + NORM_EPS)


def dispatch_kernel(
    hidden_ref, cot_ref, own_sq_ref, peer_sq_ref, gain_ref, ids_ref, weight_ref, width, out_ref, rhs, rhs_rem
):
    rows = hidden_ref.shape[0]
    count = out_ref.shape[0]
    row_scale = row_scale_of(own_sq_ref, peer_sq_ref, width)
    normed = (hidden_ref[...].astype(F32) * row_scale * gain_ref[...]).astype(BF16)
    rhs[0:rows, :] = normed
    rhs[rows : 2 * rows, :] = cot_ref[...]
    for j in range(8):
        lo, col = 2 * rows * (j % 4), LANES * (j // 4)
        rhs_rem[lo : lo + rows, col : col + LANES] = normed[:, j * LANES : (j + 1) * LANES]
        rhs_rem[lo + rows : lo + 2 * rows, col : col + LANES] = cot_ref[:, j * LANES : (j + 1) * LANES]
    rank_b = ranked(ids_ref, count).astype(BF16)
    weight = named_by(ids_ref, count, weight_ref)
    for group in range(count // 8):
        expand = (iota((128, count), 0) // 16 + group * 8 == iota((128, count), 1)).astype(BF16)
        ranks = fast_dot(expand, rank_b)
        weights = exact_dot(expand.astype(F32), weight)
        inner = iota((128, LANES), 0) % 16
        hit = ranks == (inner % 8).astype(F32)
        is_cot = inner >= 8
        left = jnp.concatenate([hit & ~is_cot, hit & is_cot], axis=1).astype(BF16)
        scale = jnp.sum(jnp.where(hit & is_cot, weights, 0.0), axis=1, keepdims=True)
        scale = jnp.where(is_cot[:, :1], scale, 1.0)
        main = (fast_dot(left, rhs[...]) * scale).astype(BF16)
        for j in range(8):
            out_ref[group * 8 : group * 8 + 8, j * 16 : (j + 1) * 16, :] = main[
                :, j * LANES : (j + 1) * LANES
            ].reshape(8, 16, LANES)
        hit = ranks == (8 + inner % 2).astype(F32)
        is_cot = (inner // 2) % 2 == 1
        parts = []
        for j in range(4):
            here = hit & (inner // 4 == j)
            parts += [here & ~is_cot, here & is_cot]
        left = jnp.concatenate(parts, axis=1).astype(BF16)
        scale = jnp.sum(jnp.where(hit & is_cot, weights, 0.0), axis=1, keepdims=True)
        scale = jnp.where(is_cot[:, :1], scale, 1.0)
        rest = (fast_dot(left, rhs_rem[...]) * scale).astype(BF16)
        for half in range(2):
            out_ref[group * 8 : group * 8 + 8, 128 + 16 * half : 144 + 16 * half, :] = rest[
                :, half * LANES : (half + 1) * LANES
            ].reshape(8, 16, LANES)


def table_kernel(ids_ref, main_ref, rest_ref):
    slots = main_ref.shape[1]
    count = slots // 16
    rank = ranked(ids_ref, count).astype(BF16)
    expand = (iota((count, slots), 1) // 16 == iota((count, slots), 0)).astype(BF16)
    ranks = fast_dot(rank, expand, TN)
    inner = iota(ranks.shape, 1) % 16
    hit = ranks == (inner % 8).astype(F32)
    rows = ranks.shape[0]
    main_ref[0:rows, :] = (hit & (inner < 8)).astype(BF16)
    main_ref[rows : 2 * rows, :] = (hit & (inner >= 8)).astype(BF16)
    hit = ranks == (8 + inner % 2).astype(F32)
    for j in range(8):
        rest_ref[j * rows : (j + 1) * rows, :] = (hit & (inner // 2 == j)).astype(BF16)


def unpack(raw_ref, x_ref, c_ref, offset):
    count = raw_ref.shape[0]
    for j in range(8):
        tile = raw_ref[:, j * 16 : (j + 1) * 16, :].astype(F32).reshape(count, 2, 8, LANES)
        cols = pl.ds(pl.multiple_of(offset + j * LANES, LANES), LANES)
        x_ref[0 : count * 8, cols] = tile[:, 0].reshape(count * 8, LANES).astype(BF16)
        c_ref[0 : count * 8, cols] = tile[:, 1].reshape(count * 8, LANES).astype(BF16)
    row = iota((128, 128), 0)
    source = (row // 2) % 4 * 32 + row // 16 * 4 + (row // 8) % 2 * 2 + row % 2
    perm = (iota((128, 128), 1) == source).astype(BF16)
    groups = count // 4
    rest = jnp.concatenate(
        [raw_ref[g * 4 : (g + 1) * 4, 128:160, :].reshape(128, LANES) for g in range(groups)], axis=1
    )
    rest = fast_dot(perm, rest)
    for j in range(8):
        cols = pl.ds(pl.multiple_of(offset + j * LANES, LANES), LANES)
        for kind, ref in enumerate((x_ref, c_ref)):
            lo = j * 16 + kind * 8
            ref[count * 8 : count * 10, cols] = jnp.concatenate(
                [rest[lo : lo + 8, g * LANES : (g + 1) * LANES] for g in range(groups)], axis=0
            ).astype(BF16)


def expert_kernel(
    core_ref, own_ref, peer_ref, gate_hbm, up_hbm, down_hbm, keep_ref, send_ref, x, c, gate, up, down, dg, du, sems
):
    copies = [
        pltpu.make_async_copy(source, target, sems.at[number])
        for number, (source, target) in enumerate(((gate_hbm, gate), (up_hbm, up), (down_hbm, down)))
    ]
    for copy in copies:
        copy.start()
    core = core_ref[0]
    half = keep_ref.shape[1]
    unpack(own_ref, x, c, core * half)
    unpack(peer_ref, x, c, (1 - core) * half)
    for copy in copies:
        copy.wait()

    @pl.loop(0, gate.shape[1] // 256)
    def _(step):
        cols = pl.ds(pl.multiple_of(step * 256, 256), 256)
        pre_gate = fast_dot(x[...], gate[:, cols])
        pre_up = fast_dot(x[...], up[:, cols])
        d_act = fast_dot(c[...], down[cols, :], NT)
        sig = jax.nn.sigmoid(pre_gate)
        dg[:, cols] = (d_act * pre_up * sig * (1.0 + pre_gate * (1.0 - sig))).astype(BF16)
        du[:, cols] = (d_act * pre_gate * sig).astype(BF16)

    @pl.loop(0, half // 256)
    def _(step):
        cols = pl.ds(pl.multiple_of(step * 256, 256), 256)
        for ref, first in ((send_ref, (1 - core) * half), (keep_ref, core * half)):
            feats = pl.ds(pl.multiple_of(first + step * 256, 256), 256)
            value = fast_dot(dg[...], gate[feats, :], NT) + fast_dot(du[...], up[feats, :], NT)
            ref[:, cols] = value.astype(ref.dtype)


def pack_kernel(keep_ref, got_ref, out_ref):
    count = out_ref.shape[0]
    for pair in range(4):
        tiles = []
        for j in (2 * pair, 2 * pair + 1):
            cols = slice(j * LANES, (j + 1) * LANES)
            value = keep_ref[0 : count * 8, cols] + got_ref[0 : count * 8, cols].astype(F32)
            tiles.append(value.reshape(count, 8, LANES))
        out_ref[:, pair * 16 : (pair + 1) * 16, :] = jnp.concatenate(tiles, axis=1).astype(BF16)
    rest = (keep_ref[count * 8 :, :] + got_ref[count * 8 :, :].astype(F32)).astype(BF16)
    row = iota((128, 128), 0)
    source = (row // 2) % 8 * 16 + row // 16 * 2 + row % 2
    perm = (iota((128, 128), 1) == source).astype(BF16)
    groups = count // 8
    stacked = jnp.concatenate(
        [
            jnp.concatenate(
                [rest[g * 16 : (g + 1) * 16, j * LANES : (j + 1) * LANES] for j in range(8)], axis=0
            )
            for g in range(groups)
        ],
        axis=1,
    )
    moved = fast_dot(perm, stacked).astype(BF16)
    for g in range(groups):
        out_ref[g * 8 : (g + 1) * 8, 64:80, :] = moved[:, g * LANES : (g + 1) * LANES].reshape(8, 16, LANES)


def combine_kernel(back_ref, main_ref, rest_ref, hidden_ref, gain_ref, gained_ref, dot_ref):
    count = back_ref.shape[0]
    rows = hidden_ref.shape[0]
    main = jnp.concatenate(
        [back_ref[:, m * 16 : (m + 1) * 16, :].reshape(count * 16, LANES) for m in range(4)], axis=1
    )
    main = fast_dot(main_ref[...], main)
    rest = fast_dot(rest_ref[...], back_ref[:, 64:80, :].reshape(count * 16, LANES))
    total = jnp.zeros((rows, LANES), F32)
    for j in range(8):
        cols = slice(j * LANES, (j + 1) * LANES)
        value = main[j % 2 * rows : (j % 2 + 1) * rows, j // 2 * LANES : (j // 2 + 1) * LANES]
        value = (value + rest[j * rows : (j + 1) * rows, :]) * gain_ref[:, cols]
        gained_ref[:, cols] = value
        total = total + value * hidden_ref[:, cols].astype(F32)
    eye = iota((rows, rows), 0) == iota((rows, rows), 1)
    dot_ref[...] = jnp.sum(jnp.where(eye, jnp.sum(total, axis=1, keepdims=True), 0.0), axis=0, keepdims=True)


def log_sigmoid(x):
    return -(jnp.maximum(-x, 0.0) + jnp.log1p(jnp.exp(-jnp.abs(x))))


def two_parts(array):
    high = array.astype(BF16)
    return high, (array - high.astype(F32)).astype(BF16)


def head_mask():
    return iota((LANES, LANES), 0) // HEAD_DIM == iota((LANES, LANES), 1) // HEAD_DIM


def decay_kernel(logit_ref, value_ref, total_ref, state_ref, parts_ref):
    rows, feats = logit_ref.shape
    logits = logit_ref[...].astype(F32)
    key = jax.nn.sigmoid(-logits)
    lower = (iota((rows, rows), 0) >= iota((rows, rows), 1)).astype(F32)
    running = exact_dot(lower, log_sigmoid(logits))
    total_ref[...] = running
    end = running[rows - 1 : rows, :]
    key_end = key * jnp.exp(end - running)
    decay = jnp.exp(end)
    same = head_mask()
    pick = iota((HEAD_DIM, LANES), 0) == iota((HEAD_DIM, LANES), 1) % HEAD_DIM
    for pair in range(feats // LANES):
        cols = slice(pair * LANES, (pair + 1) * LANES)
        eight = slice(pair * 8, (pair + 1) * 8)
        local = exact_dot(key_end[:, cols], value_ref[:, cols].astype(F32), TN)
        local = jnp.where(same, local, 0.0)
        local = (local[:HEAD_DIM] + local[HEAD_DIM:]).reshape(8, 8, LANES)
        spread = exact_dot(jnp.where(pick, decay[:, cols], 0.0), same.astype(F32)).reshape(8, 8, LANES)
        state_ref[eight, 0:8, :] = local
        state_ref[eight, 8:16, :] = spread
        rest = spread - spread.astype(BF16).astype(F32)
        parts_ref[eight] = jnp.concatenate([spread, rest], axis=1).astype(BF16)


def chain_kernel(piece_ref, out_ref, decay, both):
    count = piece_ref.shape[0]
    decay[...] = piece_ref[:, 16:32, :].astype(F32)
    both[...] = piece_ref[:, 0:16, :].astype(F32)
    later = jnp.zeros((8, LANES), F32)
    earlier = jnp.zeros((8, LANES), F32)
    for block in range(count):
        piece = both[block, 8:16, :]
        both[block, 8:16, :] = earlier
        earlier = (decay[block, 0:8, :] + decay[block, 8:16, :]) * earlier + piece
        other = count - 1 - block
        piece = both[other, 0:8, :]
        both[other, 0:8, :] = later
        later = (decay[other, 0:8, :] + decay[other, 8:16, :]) * later + piece
    out_ref[...] = both[...].astype(BF16)


def hidden_kernel(
    hidden_ref,
    cot_ref,
    own_sq_ref,
    peer_sq_ref,
    gained_ref,
    own_dot_ref,
    peer_dot_ref,
    query_ref,
    total_ref,
    state_ref,
    parts_ref,
    width,
    out_ref,
    piece_ref,
):
    row_scale = row_scale_of(own_sq_ref, peer_sq_ref, width)
    dot = column(own_dot_ref[...] + peer_dot_ref[...])
    back = row_scale * gained_ref[...] - hidden_ref[...].astype(F32) * (
        row_scale * row_scale * row_scale * dot / width
    )
    upstream = (cot_ref[...].astype(F32) + back).astype(BF16)
    out_ref[...] = upstream
    query = query_ref[...].astype(F32) * jnp.exp(total_ref[...])
    same = head_mask()
    piece_ref[:, 16:32, :] = parts_ref[...]
    for pair in range(hidden_ref.shape[1] // LANES):
        cols = slice(pair * LANES, (pair + 1) * LANES)
        eight = slice(pair * 8, (pair + 1) * 8)
        elem = exact_dot(query[:, cols], upstream[:, cols].astype(F32), TN)
        elem = jnp.where(same, elem, 0.0)
        elem = (elem[:HEAD_DIM] + elem[HEAD_DIM:]).reshape(8, 8, LANES)
        piece_ref[eight, 0:16, :] = jnp.concatenate([elem, state_ref[eight, 0:8, :]], axis=1).astype(BF16)


def block_kernel(query_ref, logit_ref, value_ref, total_ref, upstream_ref, query_out, key_out, value_out):
    rows, feats = query_ref.shape
    lower = iota((rows, rows), 0) >= iota((rows, rows), 1)
    upper = iota((rows, rows), 0) <= iota((rows, rows), 1)
    first = iota((rows, LANES), 1) < HEAD_DIM

    def split(array):
        zero = jnp.zeros_like(array)
        return jnp.where(first, array, zero), jnp.where(first, zero, array)

    for pair in range(feats // LANES):
        cols = slice(pair * LANES, (pair + 1) * LANES)
        query = query_ref[:, cols].astype(F32)
        key = jax.nn.sigmoid(-logit_ref[:, cols].astype(F32))
        running = total_ref[:, cols]
        centre = 0.5 * running[rows - 1 : rows, :]
        grow = jnp.exp(running - centre)
        shrink = jnp.exp(centre - running)
        up_split, value_split = split(upstream_ref[:, cols]), split(value_ref[:, cols])
        query_split, key_split = split(query * grow), split(key * shrink)
        raw = [fast_dot(u, v, NT) for u, v in zip(up_split, value_split)]
        pairs = jnp.concatenate([jnp.where(lower, r, 0.0) for r in raw], axis=1)
        query_out[:, cols] = grow * exact_dot(pairs, jnp.concatenate(key_split, axis=0))
        raw = [fast_dot(v, u, NT) for u, v in zip(up_split, value_split)]
        pairs = jnp.concatenate([jnp.where(upper, r, 0.0) for r in raw], axis=1)
        key_out[:, cols] = shrink * exact_dot(pairs, jnp.concatenate(query_split, axis=0))
        raw = [exact_dot(k, q, NT) for k, q in zip(key_split, query_split)]
        pairs = jnp.concatenate([jnp.where(upper, r, 0.0) for r in raw], axis=1)
        value_out[:, cols] = exact_dot(pairs, jnp.concatenate([u.astype(F32) for u in up_split], axis=0))


def final_kernel(
    query_ref,
    logit_ref,
    value_ref,
    total_ref,
    upstream_ref,
    query_in,
    key_in,
    value_in,
    carried_ref,
    state_ref,
    query_out,
    logit_out,
    value_out,
):
    rows, feats = query_ref.shape
    upper = (iota((rows, rows), 0) <= iota((rows, rows), 1)).astype(BF16)
    same = head_mask()

    def spread(array):
        return jnp.where(same, jnp.concatenate([array, array], axis=0), 0.0)

    for pair in range(feats // LANES):
        cols = slice(pair * LANES, (pair + 1) * LANES)
        eight = slice(pair * 8, (pair + 1) * 8)
        key = jax.nn.sigmoid(-logit_ref[:, cols].astype(F32))
        running = total_ref[:, cols]
        tail = jnp.exp(running[rows - 1 : rows, :] - running)
        carried = carried_ref[eight].astype(F32)
        incoming = carried[:, 0:8].reshape(HEAD_DIM, LANES)
        start = carried[:, 8:16].reshape(HEAD_DIM, LANES)
        local = state_ref[eight, 0:8, :].reshape(HEAD_DIM, LANES)
        decay = state_ref[eight, 8:16, :].reshape(HEAD_DIM, LANES)
        start_b, incoming_b = spread(start).astype(BF16), spread(incoming).astype(BF16)
        query_grad = query_in[:, cols] + jnp.exp(running) * fast_dot(upstream_ref[:, cols], start_b, NT)
        key_grad = key_in[:, cols] + tail * fast_dot(value_ref[:, cols], incoming_b, NT)
        high, low = two_parts(key * tail)
        value_grad = value_in[:, cols] + fast_dot(high, incoming_b) + fast_dot(low, incoming_b)
        past = spread((decay * start + local) * incoming)
        past = exact_dot(jnp.ones((8, LANES), F32), past, NT)[0:1, :]
        cumul = query_ref[:, cols].astype(F32) * query_grad - key * key_grad
        high, rest = two_parts(cumul)
        middle, low = two_parts(cumul - high.astype(F32))
        suffix = fast_dot(upper, high) + fast_dot(upper, middle) + fast_dot(upper, low) + past
        logit_grad = suffix * key - key_grad * key * (1.0 - key)
        query_out[:, cols] = query_grad.astype(BF16)
        logit_out[:, cols] = logit_grad.astype(BF16)
        value_out[:, cols] = value_grad.astype(BF16)


def on_device(
    hidden, grad_out, expert_ids, gate_weights, norm_gain, w_gate, w_up, w_down, queries, forget_logits, values
):
    rows, feats = hidden.shape
    ctx = lax.axis_size("ctx")
    width = w_gate.shape[1]
    units = w_gate.shape[2]
    slots = ctx * 10
    core = lax.axis_index("tp")
    swap = [(0, 1), (1, 0)]
    gain = norm_gain.reshape(1, feats)

    def exchange(array):
        return lax.all_to_all(array, "ctx", split_axis=0, concat_axis=0, tiled=True)

    ids, weights = expert_ids.T, gate_weights.T

    hidden_f = hidden.astype(F32)
    squares = jnp.sum(hidden_f * hidden_f, axis=1)
    squares = (squares.reshape(1, rows), lax.ppermute(squares, "tp", swap).reshape(1, rows))

    sent = call(
        lambda h, g, s, z, n, i, w, o, a, b: dispatch_kernel(h, g, s, z, n, i, w, width, o, a, b),
        shape_of((ctx, 160, LANES), BF16),
        hidden,
        grad_out,
        *squares,
        gain,
        ids,
        weights,
        scratch=(pltpu.VMEM((2 * rows, feats), BF16), pltpu.VMEM((8 * rows, 2 * LANES), BF16)),
        flops=1 << 30,
        nbytes=4 << 20,
    )
    own = exchange(sent)
    main_table, rest_table = call(
        table_kernel,
        (shape_of((2 * rows, ctx * 16), BF16), shape_of((8 * rows, ctx * 16), BF16)),
        ids,
        flops=1 << 26,
        nbytes=3 << 20,
    )
    total, state, parts = call(
        decay_kernel,
        (shape_of((rows, feats), F32), shape_of((ctx, 16, LANES), F32), shape_of((ctx, 16, LANES), BF16)),
        forget_logits,
        values,
        flops=1 << 30,
        nbytes=2 << 20,
    )

    peer = lax.ppermute(own, "tp", swap)
    vmem, hbm = pl.BlockSpec(memory_space=pltpu.VMEM), pl.BlockSpec(memory_space=pl.ANY)
    keep, send = call(
        expert_kernel,
        (shape_of((slots, feats), F32), shape_of((slots, feats), BF16)),
        core.reshape(1).astype(jnp.int32),
        own,
        peer,
        w_gate[0],
        w_up[0],
        w_down[0],
        in_specs=[pl.BlockSpec(memory_space=pltpu.SMEM), vmem, vmem, hbm, hbm, hbm],
        scratch=(
            pltpu.VMEM((slots, width), BF16),
            pltpu.VMEM((slots, width), BF16),
            pltpu.VMEM((width, units), BF16),
            pltpu.VMEM((width, units), BF16),
            pltpu.VMEM((units, width), BF16),
            pltpu.VMEM((slots, units), BF16),
            pltpu.VMEM((slots, units), BF16),
            pltpu.SemaphoreType.DMA((3,)),
        ),
        flops=10 * slots * width * units,
        nbytes=20 << 20,
    )
    got = lax.ppermute(send, "tp", swap)
    packed = call(pack_kernel, shape_of((ctx, 80, LANES), BF16), keep, got, flops=1 << 26, nbytes=6 << 20)
    back = exchange(packed)
    gained, dots = call(
        combine_kernel,
        (shape_of((rows, feats), F32), shape_of((1, rows), F32)),
        back,
        main_table,
        rest_table,
        hidden,
        gain,
        flops=1 << 29,
        nbytes=6 << 20,
    )
    dots = (dots, lax.ppermute(dots, "tp", swap))
    grad_hidden, piece = call(
        lambda h, g, s, z, a, d, e, q, t, x, y, o, p: hidden_kernel(
            h, g, s, z, a, d, e, q, t, x, y, width, o, p
        ),
        (shape_of((rows, feats), BF16), shape_of((ctx, 32, LANES), BF16)),
        hidden,
        grad_out,
        *squares,
        gained,
        *dots,
        queries,
        total,
        state,
        parts,
        flops=1 << 28,
        nbytes=3 << 20,
    )
    pieces = exchange(piece)
    inner = call(
        block_kernel,
        (shape_of((rows, feats), F32),) * 3,
        queries,
        forget_logits,
        values,
        total,
        grad_hidden,
        flops=1 << 32,
        nbytes=4 << 20,
    )
    chained = call(
        chain_kernel,
        shape_of((ctx, 16, LANES), BF16),
        pieces,
        scratch=(pltpu.VMEM((ctx, 16, LANES), F32), pltpu.VMEM((ctx, 16, LANES), F32)),
        nbytes=1 << 20,
    )
    carried = exchange(chained)
    grad_queries, grad_logits, grad_values = call(
        final_kernel,
        (shape_of((rows, feats), BF16),) * 3,
        queries,
        forget_logits,
        values,
        total,
        grad_hidden,
        *inner,
        carried,
        state,
        flops=1 << 30,
        nbytes=4 << 20,
    )
    return grad_hidden, grad_queries, grad_logits, grad_values


def solution(mesh):
    rows = P("ctx", "tp")
    in_specs = (
        rows,
        rows,
        P("ctx", None),
        P("ctx", None),
        P("tp"),
        P("ctx", None, "tp"),
        P("ctx", None, "tp"),
        P("ctx", "tp", None),
        rows,
        rows,
        rows,
    )
    return jax.shard_map(on_device, mesh=mesh, in_specs=in_specs, out_specs=(rows,) * 4, check_vma=False)
```

```python
import functools

import jax
import jax.numpy as jnp
from jax import lax
from jax.experimental import pallas as pl
from jax.experimental.pallas import tpu as pltpu
from jax.sharding import PartitionSpec as P

HEAD_DIM = 64
NORM_EPS = 1e-06
LANES = 128
BF16 = jnp.bfloat16
F32 = jnp.float32
EXACT = lax.Precision.HIGHEST
NT = (((1,), (1,)), ((), ()))
TN = (((0,), (0,)), ((), ()))
NN = (((1,), (0,)), ((), ()))


def iota(shape, dim):
    return lax.broadcasted_iota(jnp.int32, shape, dim)


def exact_dot(a, b, dims=NN):
    return lax.dot_general(a, b, dims, precision=EXACT, preferred_element_type=F32)


def fast_dot(a, b, dims=NN):
    return lax.dot_general(a, b, dims, preferred_element_type=F32)


def call(kernel, out_shape, *args, scratch=(), in_specs=None, out_specs=None, mib=16, flops=0, nbytes=0):
    return pl.pallas_call(
        kernel,
        out_shape=out_shape,
        in_specs=in_specs or [pl.BlockSpec(memory_space=pltpu.VMEM)] * len(args),
        out_specs=out_specs or jax.tree.map(lambda _: pl.BlockSpec(memory_space=pltpu.VMEM), out_shape),
        scratch_shapes=list(scratch),
        compiler_params=pltpu.CompilerParams(vmem_limit_bytes=mib << 20),
        cost_estimate=pl.CostEstimate(flops=flops, bytes_accessed=nbytes, transcendentals=0),
    )(*args)


def shape_of(shape, dtype):
    return jax.ShapeDtypeStruct(shape, dtype)


def ranked(ids_ref, count):
    rows = ids_ref.shape[1]
    named = named_by(ids_ref, count)
    before = (iota((rows, rows), 0) < iota((rows, rows), 1)).astype(BF16)
    rank = fast_dot(named.astype(BF16), before)
    return jnp.where(named > 0.0, rank, -1.0)


def named_by(ids_ref, count, weight_ref=None):
    expert = iota((count, ids_ref.shape[1]), 0)
    total = jnp.zeros(expert.shape, F32)
    for choice in range(ids_ref.shape[0]):
        level = 1.0 if weight_ref is None else weight_ref[choice : choice + 1, :]
        total = total + jnp.where(ids_ref[choice : choice + 1, :] == expert, level, 0.0)
    return total


def column(row):
    count = row.shape[1]
    eye = iota((count, count), 0) == iota((count, count), 1)
    return jnp.sum(jnp.where(eye, row, 0.0), axis=1, keepdims=True)


def row_scale_of(own_ref, peer_ref, width):
    return lax.rsqrt(column(own_ref[...] + peer_ref[...]) / width + NORM_EPS)


def dispatch_kernel(
    hidden_ref, cot_ref, own_sq_ref, peer_sq_ref, gain_ref, ids_ref, weight_ref, width, out_ref, rhs, rhs_rem
):
    rows = hidden_ref.shape[0]
    count = out_ref.shape[0]
    row_scale = row_scale_of(own_sq_ref, peer_sq_ref, width)
    normed = (hidden_ref[...].astype(F32) * row_scale * gain_ref[...]).astype(BF16)
    rhs[0:rows, :] = normed
    rhs[rows : 2 * rows, :] = cot_ref[...]
    for j in range(8):
        lo, col = 2 * rows * (j % 4), LANES * (j // 4)
        rhs_rem[lo : lo + rows, col : col + LANES] = normed[:, j * LANES : (j + 1) * LANES]
        rhs_rem[lo + rows : lo + 2 * rows, col : col + LANES] = cot_ref[:, j * LANES : (j + 1) * LANES]
    rank_b = ranked(ids_ref, count).astype(BF16)
    weight = named_by(ids_ref, count, weight_ref)
    for group in range(count // 8):
        expand = (iota((128, count), 0) // 16 + group * 8 == iota((128, count), 1)).astype(BF16)
        ranks = fast_dot(expand, rank_b)
        weights = exact_dot(expand.astype(F32), weight)
        inner = iota((128, LANES), 0) % 16
        hit = ranks == (inner % 8).astype(F32)
        is_cot = inner >= 8
        left = jnp.concatenate([hit & ~is_cot, hit & is_cot], axis=1).astype(BF16)
        scale = jnp.sum(jnp.where(hit & is_cot, weights, 0.0), axis=1, keepdims=True)
        scale = jnp.where(is_cot[:, :1], scale, 1.0)
        main = (fast_dot(left, rhs[...]) * scale).astype(BF16)
        for j in range(8):
            out_ref[group * 8 : group * 8 + 8, j * 16 : (j + 1) * 16, :] = main[
                :, j * LANES : (j + 1) * LANES
            ].reshape(8, 16, LANES)
        hit = ranks == (8 + inner % 2).astype(F32)
        is_cot = (inner // 2) % 2 == 1
        parts = []
        for j in range(4):
            here = hit & (inner // 4 == j)
            parts += [here & ~is_cot, here & is_cot]
        left = jnp.concatenate(parts, axis=1).astype(BF16)
        scale = jnp.sum(jnp.where(hit & is_cot, weights, 0.0), axis=1, keepdims=True)
        scale = jnp.where(is_cot[:, :1], scale, 1.0)
        rest = (fast_dot(left, rhs_rem[...]) * scale).astype(BF16)
        for half in range(2):
            out_ref[group * 8 : group * 8 + 8, 128 + 16 * half : 144 + 16 * half, :] = rest[
                :, half * LANES : (half + 1) * LANES
            ].reshape(8, 16, LANES)


def table_kernel(ids_ref, main_ref, rest_ref):
    slots = main_ref.shape[1]
    count = slots // 16
    rank = ranked(ids_ref, count).astype(BF16)
    expand = (iota((count, slots), 1) // 16 == iota((count, slots), 0)).astype(BF16)
    ranks = fast_dot(rank, expand, TN)
    inner = iota(ranks.shape, 1) % 16
    hit = ranks == (inner % 8).astype(F32)
    rows = ranks.shape[0]
    main_ref[0:rows, :] = (hit & (inner < 8)).astype(BF16)
    main_ref[rows : 2 * rows, :] = (hit & (inner >= 8)).astype(BF16)
    hit = ranks == (8 + inner % 2).astype(F32)
    rest_ref[...] = hit.astype(BF16)


def unpack(raw_ref, x_ref, c_ref):
    count = raw_ref.shape[0]
    for j in range(8):
        tile = raw_ref[:, j * 16 : (j + 1) * 16, :].astype(F32).reshape(count, 2, 8, LANES)
        cols = slice(j * LANES, (j + 1) * LANES)
        x_ref[0 : count * 8, cols] = tile[:, 0].reshape(count * 8, LANES).astype(BF16)
        c_ref[0 : count * 8, cols] = tile[:, 1].reshape(count * 8, LANES).astype(BF16)
    row = iota((128, 128), 0)
    source = (row // 2) % 4 * 32 + row // 16 * 4 + (row // 8) % 2 * 2 + row % 2
    perm = (iota((128, 128), 1) == source).astype(BF16)
    groups = count // 4
    rest = jnp.concatenate(
        [raw_ref[g * 4 : (g + 1) * 4, 128:160, :].reshape(128, LANES) for g in range(groups)], axis=1
    )
    rest = fast_dot(perm, rest)
    for j in range(8):
        cols = slice(j * LANES, (j + 1) * LANES)
        for kind, ref in enumerate((x_ref, c_ref)):
            lo = j * 16 + kind * 8
            ref[count * 8 : count * 10, cols] = jnp.concatenate(
                [rest[lo : lo + 8, g * LANES : (g + 1) * LANES] for g in range(groups)], axis=0
            ).astype(BF16)


def start_copies(pairs, sems):
    copies = [pltpu.make_async_copy(source, target, sems.at[number]) for number, (source, target) in enumerate(pairs)]
    for copy in copies:
        copy.start()
    return copies


def half_of(core, half):
    return pl.ds(pl.multiple_of(core * half, half), half)


def own_kernel(
    core_ref,
    raw_ref,
    gate_hbm,
    up_hbm,
    down_hbm,
    part_0,
    part_1,
    part_2,
    gate,
    up,
    peer_gate,
    peer_up,
    peer_down,
    x,
    c,
    down,
    sems,
    peer_sems,
):
    mine = half_of(core_ref[0], x.shape[1])
    other = half_of(1 - core_ref[0], x.shape[1])
    copies = start_copies(
        ((gate_hbm.at[mine, :], gate), (up_hbm.at[mine, :], up), (down_hbm.at[:, mine], down)), sems
    )
    later = [
        pltpu.make_async_copy(source, target, peer_sems.at[number])
        for number, (source, target) in enumerate(
            ((gate_hbm.at[other, :], peer_gate), (up_hbm.at[other, :], peer_up), (down_hbm.at[:, other], peer_down))
        )
    ]
    unpack(raw_ref, x, c)
    copies[0].wait()
    later[0].start()
    part_0[...] = fast_dot(x[...], gate[...])
    copies[1].wait()
    later[1].start()
    part_1[...] = fast_dot(x[...], up[...])
    copies[2].wait()
    later[2].start()
    part_2[...] = fast_dot(c[...], down[...], NT)
    for copy in later:
        copy.wait()


def peer_kernel(raw_ref, part_0, part_1, part_2, gate, up, down, send_ref, dg, du, x, c):
    unpack(raw_ref, x, c)
    for step in range(part_0.shape[1] // 256):
        cols = slice(step * 256, (step + 1) * 256)
        pre_gate = part_0[:, cols] + fast_dot(x[...], gate[:, cols])
        pre_up = part_1[:, cols] + fast_dot(x[...], up[:, cols])
        d_act = part_2[:, cols] + fast_dot(c[...], down[cols, :], NT)
        sig = jax.nn.sigmoid(pre_gate)
        dg[:, cols] = (d_act * pre_up * sig * (1.0 + pre_gate * (1.0 - sig))).astype(BF16)
        du[:, cols] = (d_act * pre_gate * sig).astype(BF16)
    project(dg, du, gate, up, send_ref)


def project(dg, du, gate, up, out_ref):
    for step in range(out_ref.shape[1] // 256):
        cols = slice(step * 256, (step + 1) * 256)
        value = fast_dot(dg[...], gate[cols, :], NT) + fast_dot(du[...], up[cols, :], NT)
        out_ref[:, cols] = value.astype(out_ref.dtype)


def keep_kernel(dg, du, gate, up, keep_ref):
    project(dg, du, gate, up, keep_ref)


def pack_kernel(keep_ref, got_ref, out_ref):
    count = out_ref.shape[0]
    for pair in range(4):
        tiles = []
        for j in (2 * pair, 2 * pair + 1):
            cols = slice(j * LANES, (j + 1) * LANES)
            value = keep_ref[0 : count * 8, cols] + got_ref[0 : count * 8, cols].astype(F32)
            tiles.append(value.reshape(count, 8, LANES))
        out_ref[:, pair * 16 : (pair + 1) * 16, :] = jnp.concatenate(tiles, axis=1).astype(BF16)
    rest = (keep_ref[count * 8 :, :] + got_ref[count * 8 :, :].astype(F32)).astype(BF16)
    row = iota((128, 128), 0)
    source = (row // 2) % 8 * 16 + row // 16 * 2 + row % 2
    perm = (iota((128, 128), 1) == source).astype(BF16)
    groups = count // 8
    stacked = jnp.concatenate(
        [
            jnp.concatenate(
                [rest[g * 16 : (g + 1) * 16, j * LANES : (j + 1) * LANES] for j in range(8)], axis=0
            )
            for g in range(groups)
        ],
        axis=1,
    )
    moved = fast_dot(perm, stacked).astype(BF16)
    for g in range(groups):
        out_ref[g * 8 : (g + 1) * 8, 64:80, :] = moved[:, g * LANES : (g + 1) * LANES].reshape(8, 16, LANES)


def combine_kernel(back_ref, main_ref, rest_ref, hidden_ref, gain_ref, gained_ref, dot_ref):
    count = back_ref.shape[0]
    rows = hidden_ref.shape[0]
    main = jnp.concatenate(
        [back_ref[:, m * 16 : (m + 1) * 16, :].reshape(count * 16, LANES) for m in range(4)], axis=1
    )
    main = fast_dot(main_ref[...], main)
    block = iota((1, count * 16), 1) % 16 // 2
    left = jnp.concatenate([jnp.where(block == j, rest_ref[...], 0.0) for j in range(8)], axis=0)
    rest = fast_dot(left.astype(BF16), back_ref[:, 64:80, :].reshape(count * 16, LANES))
    total = jnp.zeros((rows, LANES), F32)
    for j in range(8):
        cols = slice(j * LANES, (j + 1) * LANES)
        value = main[j % 2 * rows : (j % 2 + 1) * rows, j // 2 * LANES : (j // 2 + 1) * LANES]
        value = (value + rest[j * rows : (j + 1) * rows, :]) * gain_ref[:, cols]
        gained_ref[:, cols] = value
        total = total + value * hidden_ref[:, cols].astype(F32)
    eye = iota((rows, rows), 0) == iota((rows, rows), 1)
    dot_ref[...] = jnp.sum(jnp.where(eye, jnp.sum(total, axis=1, keepdims=True), 0.0), axis=0, keepdims=True)


def log_sigmoid(x):
    return -(jnp.maximum(-x, 0.0) + jnp.log1p(jnp.exp(-jnp.abs(x))))


def two_parts(array):
    high = array.astype(BF16)
    return high, (array - high.astype(F32)).astype(BF16)


def head_mask():
    return iota((LANES, LANES), 0) // HEAD_DIM == iota((LANES, LANES), 1) // HEAD_DIM


def decay_kernel(logit_ref, value_ref, total_ref, state_ref, parts_ref):
    rows, feats = logit_ref.shape
    logits = logit_ref[...].astype(F32)
    key = jax.nn.sigmoid(-logits)
    lower = (iota((rows, rows), 0) >= iota((rows, rows), 1)).astype(F32)
    running = exact_dot(lower, log_sigmoid(logits))
    total_ref[...] = running
    end = running[rows - 1 : rows, :]
    key_end = key * jnp.exp(end - running)
    decay = jnp.exp(end)
    same = head_mask()
    pick = iota((HEAD_DIM, LANES), 0) == iota((HEAD_DIM, LANES), 1) % HEAD_DIM
    for pair in range(feats // LANES):
        cols = slice(pair * LANES, (pair + 1) * LANES)
        eight = slice(pair * 8, (pair + 1) * 8)
        local = exact_dot(key_end[:, cols], value_ref[:, cols].astype(F32), TN)
        local = jnp.where(same, local, 0.0)
        local = (local[:HEAD_DIM] + local[HEAD_DIM:]).reshape(8, 8, LANES)
        spread = exact_dot(jnp.where(pick, decay[:, cols], 0.0), same.astype(F32)).reshape(8, 8, LANES)
        state_ref[eight, 0:8, :] = local
        state_ref[eight, 8:16, :] = spread
        rest = spread - spread.astype(BF16).astype(F32)
        parts_ref[eight] = jnp.concatenate([spread, rest], axis=1).astype(BF16)


def chain_kernel(piece_ref, out_ref, decay, both):
    count = piece_ref.shape[0]
    decay[...] = piece_ref[:, 16:32, :].astype(F32)
    both[...] = piece_ref[:, 0:16, :].astype(F32)
    later = jnp.zeros((8, LANES), F32)
    earlier = jnp.zeros((8, LANES), F32)
    for block in range(count):
        piece = both[block, 8:16, :]
        both[block, 8:16, :] = earlier
        earlier = (decay[block, 0:8, :] + decay[block, 8:16, :]) * earlier + piece
        other = count - 1 - block
        piece = both[other, 0:8, :]
        both[other, 0:8, :] = later
        later = (decay[other, 0:8, :] + decay[other, 8:16, :]) * later + piece
    out_ref[...] = both[...].astype(BF16)


def hidden_kernel(
    hidden_ref,
    cot_ref,
    own_sq_ref,
    peer_sq_ref,
    gained_ref,
    own_dot_ref,
    peer_dot_ref,
    query_ref,
    total_ref,
    state_ref,
    parts_ref,
    width,
    out_ref,
    piece_ref,
):
    row_scale = row_scale_of(own_sq_ref, peer_sq_ref, width)
    dot = column(own_dot_ref[...] + peer_dot_ref[...])
    back = row_scale * gained_ref[...] - hidden_ref[...].astype(F32) * (
        row_scale * row_scale * row_scale * dot / width
    )
    upstream = (cot_ref[...].astype(F32) + back).astype(BF16)
    out_ref[...] = upstream
    query = query_ref[...].astype(F32) * jnp.exp(total_ref[...])
    same = head_mask()
    piece_ref[:, 16:32, :] = parts_ref[...]
    for pair in range(hidden_ref.shape[1] // LANES):
        cols = slice(pair * LANES, (pair + 1) * LANES)
        eight = slice(pair * 8, (pair + 1) * 8)
        elem = exact_dot(query[:, cols], upstream[:, cols].astype(F32), TN)
        elem = jnp.where(same, elem, 0.0)
        elem = (elem[:HEAD_DIM] + elem[HEAD_DIM:]).reshape(8, 8, LANES)
        piece_ref[eight, 0:16, :] = jnp.concatenate([elem, state_ref[eight, 0:8, :]], axis=1).astype(BF16)


def block_kernel(query_ref, logit_ref, value_ref, total_ref, upstream_ref, query_out, key_out, value_out):
    rows, feats = query_ref.shape
    lower = iota((rows, rows), 0) >= iota((rows, rows), 1)
    upper = iota((rows, rows), 0) <= iota((rows, rows), 1)
    first = iota((rows, LANES), 1) < HEAD_DIM

    def split(array):
        zero = jnp.zeros_like(array)
        return jnp.where(first, array, zero), jnp.where(first, zero, array)

    for pair in range(feats // LANES):
        cols = slice(pair * LANES, (pair + 1) * LANES)
        query = query_ref[:, cols].astype(F32)
        key = jax.nn.sigmoid(-logit_ref[:, cols].astype(F32))
        running = total_ref[:, cols]
        centre = 0.5 * running[rows - 1 : rows, :]
        grow = jnp.exp(running - centre)
        shrink = jnp.exp(centre - running)
        up_split, value_split = split(upstream_ref[:, cols]), split(value_ref[:, cols])
        query_split, key_split = split(query * grow), split(key * shrink)
        raw = [fast_dot(u, v, NT) for u, v in zip(up_split, value_split)]
        pairs = jnp.concatenate([jnp.where(lower, r, 0.0) for r in raw], axis=1)
        query_out[:, cols] = grow * exact_dot(pairs, jnp.concatenate(key_split, axis=0))
        raw = [fast_dot(v, u, NT) for u, v in zip(up_split, value_split)]
        pairs = jnp.concatenate([jnp.where(upper, r, 0.0) for r in raw], axis=1)
        key_out[:, cols] = shrink * exact_dot(pairs, jnp.concatenate(query_split, axis=0))
        raw = [exact_dot(k, q, NT) for k, q in zip(key_split, query_split)]
        pairs = jnp.concatenate([jnp.where(upper, r, 0.0) for r in raw], axis=1)
        value_out[:, cols] = exact_dot(pairs, jnp.concatenate([u.astype(F32) for u in up_split], axis=0))


def final_kernel(
    query_ref,
    logit_ref,
    value_ref,
    total_ref,
    upstream_ref,
    query_in,
    key_in,
    value_in,
    carried_ref,
    state_ref,
    query_out,
    logit_out,
    value_out,
):
    rows, feats = query_ref.shape
    upper = (iota((rows, rows), 0) <= iota((rows, rows), 1)).astype(BF16)
    same = head_mask()

    def spread(array):
        return jnp.where(same, jnp.concatenate([array, array], axis=0), 0.0)

    for pair in range(feats // LANES):
        cols = slice(pair * LANES, (pair + 1) * LANES)
        eight = slice(pair * 8, (pair + 1) * 8)
        key = jax.nn.sigmoid(-logit_ref[:, cols].astype(F32))
        running = total_ref[:, cols]
        tail = jnp.exp(running[rows - 1 : rows, :] - running)
        carried = carried_ref[eight].astype(F32)
        incoming = carried[:, 0:8].reshape(HEAD_DIM, LANES)
        start = carried[:, 8:16].reshape(HEAD_DIM, LANES)
        local = state_ref[eight, 0:8, :].reshape(HEAD_DIM, LANES)
        decay = state_ref[eight, 8:16, :].reshape(HEAD_DIM, LANES)
        start_b, incoming_b = spread(start).astype(BF16), spread(incoming).astype(BF16)
        query_grad = query_in[:, cols] + jnp.exp(running) * fast_dot(upstream_ref[:, cols], start_b, NT)
        key_grad = key_in[:, cols] + tail * fast_dot(value_ref[:, cols], incoming_b, NT)
        high, low = two_parts(key * tail)
        value_grad = value_in[:, cols] + fast_dot(high, incoming_b) + fast_dot(low, incoming_b)
        past = spread((decay * start + local) * incoming)
        past = exact_dot(jnp.ones((8, LANES), F32), past, NT)[0:1, :]
        cumul = query_ref[:, cols].astype(F32) * query_grad - key * key_grad
        high, rest = two_parts(cumul)
        middle, low = two_parts(cumul - high.astype(F32))
        suffix = fast_dot(upper, high) + fast_dot(upper, middle) + fast_dot(upper, low) + past
        logit_grad = suffix * key - key_grad * key * (1.0 - key)
        query_out[:, cols] = query_grad.astype(BF16)
        logit_out[:, cols] = logit_grad.astype(BF16)
        value_out[:, cols] = value_grad.astype(BF16)


def on_device(
    hidden, grad_out, expert_ids, gate_weights, norm_gain, w_gate, w_up, w_down, queries, forget_logits, values
):
    rows, feats = hidden.shape
    ctx = lax.axis_size("ctx")
    width = w_gate.shape[1]
    units = w_gate.shape[2]
    slots = ctx * 10
    core = lax.axis_index("tp")
    swap = [(0, 1), (1, 0)]
    gain = norm_gain.reshape(1, feats)

    def exchange(array):
        return lax.all_to_all(array, "ctx", split_axis=0, concat_axis=0, tiled=True)

    ids, weights = expert_ids.T, gate_weights.T

    hidden_f = hidden.astype(F32)
    squares = jnp.sum(hidden_f * hidden_f, axis=1)
    squares = (squares.reshape(1, rows), lax.ppermute(squares, "tp", swap).reshape(1, rows))

    sent = call(
        lambda h, g, s, z, n, i, w, o, a, b: dispatch_kernel(h, g, s, z, n, i, w, width, o, a, b),
        shape_of((ctx, 160, LANES), BF16),
        hidden,
        grad_out,
        *squares,
        gain,
        ids,
        weights,
        scratch=(pltpu.VMEM((2 * rows, feats), BF16), pltpu.VMEM((8 * rows, 2 * LANES), BF16)),
        mib=60,
        flops=1 << 24,
        nbytes=1 << 12,
    )
    own = exchange(sent)
    main_table, rest_table = call(
        table_kernel,
        (shape_of((2 * rows, ctx * 16), BF16), shape_of((rows, ctx * 16), BF16)),
        ids,
        flops=1 << 26,
        nbytes=3 << 20,
    )
    total, state, decays = call(
        decay_kernel,
        (shape_of((rows, feats), F32), shape_of((ctx, 16, LANES), F32), shape_of((ctx, 16, LANES), BF16)),
        forget_logits,
        values,
        flops=1 << 30,
        nbytes=2 << 20,
    )

    peer = lax.ppermute(own, "tp", swap)
    vmem = pl.BlockSpec(memory_space=pltpu.VMEM)
    smem, hbm = pl.BlockSpec(memory_space=pltpu.SMEM), pl.BlockSpec(memory_space=pl.ANY)
    which = core.reshape(1).astype(jnp.int32)
    half_in, half_out = shape_of((feats, units), BF16), shape_of((units, feats), BF16)
    *parts, gate, up, peer_gate, peer_up, peer_down = call(
        own_kernel,
        (*(shape_of((slots, units), F32),) * 3, half_in, half_in, half_in, half_in, half_out),
        which,
        own,
        w_gate[0],
        w_up[0],
        w_down[0],
        in_specs=[smem, vmem, hbm, hbm, hbm],
        scratch=(
            pltpu.VMEM((slots, feats), BF16),
            pltpu.VMEM((slots, feats), BF16),
            pltpu.VMEM((units, feats), BF16),
            pltpu.SemaphoreType.DMA((3,)),
            pltpu.SemaphoreType.DMA((3,)),
        ),
        mib=40,
        flops=6 * slots * feats * units,
        nbytes=13 << 20,
    )
    send, dg, du = call(
        peer_kernel,
        (shape_of((slots, feats), BF16), shape_of((slots, units), BF16), shape_of((slots, units), BF16)),
        peer,
        *parts,
        peer_gate,
        peer_up,
        peer_down,
        scratch=(pltpu.VMEM((slots, feats), BF16), pltpu.VMEM((slots, feats), BF16)),
        mib=28,
        flops=10 * slots * feats * units,
        nbytes=16 << 20,
    )
    got = lax.ppermute(send, "tp", swap)
    keep = call(
        keep_kernel,
        shape_of((slots, feats), F32),
        dg,
        du,
        gate,
        up,
        flops=4 * slots * feats * units,
        nbytes=8 << 20,
    )
    packed = call(pack_kernel, shape_of((ctx, 80, LANES), BF16), keep, got, flops=1 << 26, nbytes=6 << 20)
    back = exchange(packed)
    gained, dots = call(
        combine_kernel,
        (shape_of((rows, feats), F32), shape_of((1, rows), F32)),
        back,
        main_table,
        rest_table,
        hidden,
        gain,
        flops=1 << 29,
        nbytes=6 << 20,
    )
    dots = (dots, lax.ppermute(dots, "tp", swap))
    grad_hidden, piece = call(
        lambda h, g, s, z, a, d, e, q, t, x, y, o, p: hidden_kernel(
            h, g, s, z, a, d, e, q, t, x, y, width, o, p
        ),
        (shape_of((rows, feats), BF16), shape_of((ctx, 32, LANES), BF16)),
        hidden,
        grad_out,
        *squares,
        gained,
        *dots,
        queries,
        total,
        state,
        decays,
        flops=1 << 28,
        nbytes=3 << 20,
    )
    pieces = exchange(piece)
    inner = call(
        block_kernel,
        (shape_of((rows, feats), F32),) * 3,
        queries,
        forget_logits,
        values,
        total,
        grad_hidden,
        mib=60,
        flops=1 << 32,
        nbytes=4 << 20,
    )
    chained = call(
        chain_kernel,
        shape_of((ctx, 16, LANES), BF16),
        pieces,
        scratch=(pltpu.VMEM((ctx, 16, LANES), F32), pltpu.VMEM((ctx, 16, LANES), F32)),
        nbytes=1 << 20,
    )
    carried = exchange(chained)
    grad_queries, grad_logits, grad_values = call(
        final_kernel,
        (shape_of((rows, feats), BF16),) * 3,
        queries,
        forget_logits,
        values,
        total,
        grad_hidden,
        *inner,
        carried,
        state,
        mib=60,
        flops=1 << 30,
        nbytes=4 << 20,
    )
    return grad_hidden, grad_queries, grad_logits, grad_values


def solution(mesh):
    rows = P("ctx", "tp")
    in_specs = (
        rows,
        rows,
        P("ctx", None),
        P("ctx", None),
        P("tp"),
        P("ctx", None, "tp"),
        P("ctx", None, "tp"),
        P("ctx", "tp", None),
        rows,
        rows,
        rows,
    )
    return jax.shard_map(on_device, mesh=mesh, in_specs=in_specs, out_specs=(rows,) * 4, check_vma=False)
```

```python
import functools

import jax
import jax.numpy as jnp
from jax import lax
from jax.experimental import pallas as pl
from jax.experimental.pallas import tpu as pltpu
from jax.sharding import PartitionSpec as P

HEAD_DIM = 64
NORM_EPS = 1e-06
LANES = 128
BF16 = jnp.bfloat16
F32 = jnp.float32
EXACT = lax.Precision.HIGHEST
NT = (((1,), (1,)), ((), ()))
TN = (((0,), (0,)), ((), ()))
NN = (((1,), (0,)), ((), ()))


def iota(shape, dim):
    return lax.broadcasted_iota(jnp.int32, shape, dim)


def exact_dot(a, b, dims=NN):
    return lax.dot_general(a, b, dims, precision=EXACT, preferred_element_type=F32)


def fast_dot(a, b, dims=NN):
    return lax.dot_general(a, b, dims, preferred_element_type=F32)


def call(kernel, out_shape, *args, scratch=(), in_specs=None, out_specs=None, mib=16, flops=0, nbytes=0):
    return pl.pallas_call(
        kernel,
        out_shape=out_shape,
        in_specs=in_specs or [pl.BlockSpec(memory_space=pltpu.VMEM)] * len(args),
        out_specs=out_specs or jax.tree.map(lambda _: pl.BlockSpec(memory_space=pltpu.VMEM), out_shape),
        scratch_shapes=list(scratch),
        compiler_params=pltpu.CompilerParams(vmem_limit_bytes=mib << 20),
        cost_estimate=pl.CostEstimate(flops=flops, bytes_accessed=nbytes, transcendentals=0),
    )(*args)


def shape_of(shape, dtype):
    return jax.ShapeDtypeStruct(shape, dtype)


def ranked(ids_ref, count):
    rows = ids_ref.shape[1]
    named = named_by(ids_ref, count)
    before = (iota((rows, rows), 0) < iota((rows, rows), 1)).astype(BF16)
    rank = fast_dot(named.astype(BF16), before)
    return jnp.where(named > 0.0, rank, -1.0)


def named_by(ids_ref, count, weight_ref=None):
    expert = iota((count, ids_ref.shape[1]), 0)
    total = jnp.zeros(expert.shape, F32)
    for choice in range(ids_ref.shape[0]):
        level = 1.0 if weight_ref is None else weight_ref[choice : choice + 1, :]
        total = total + jnp.where(ids_ref[choice : choice + 1, :] == expert, level, 0.0)
    return total


def column(row):
    count = row.shape[1]
    eye = iota((count, count), 0) == iota((count, count), 1)
    return jnp.sum(jnp.where(eye, row, 0.0), axis=1, keepdims=True)


def row_scale_of(own_ref, peer_ref, width):
    return lax.rsqrt(column(own_ref[...] + peer_ref[...]) / width + NORM_EPS)


def dispatch_kernel(
    hidden_ref, cot_ref, own_sq_ref, peer_sq_ref, gain_ref, ids_ref, weight_ref, width, out_hbm, out_ref, rhs, rhs_rem, sems
):
    rows = hidden_ref.shape[0]
    count = out_ref.shape[0]
    row_scale = row_scale_of(own_sq_ref, peer_sq_ref, width)
    normed = (hidden_ref[...].astype(F32) * row_scale * gain_ref[...]).astype(BF16)
    rhs[0:rows, :] = normed
    rhs[rows : 2 * rows, :] = cot_ref[...]
    for j in range(8):
        lo, col = 2 * rows * (j % 4), LANES * (j // 4)
        rhs_rem[lo : lo + rows, col : col + LANES] = normed[:, j * LANES : (j + 1) * LANES]
        rhs_rem[lo + rows : lo + 2 * rows, col : col + LANES] = cot_ref[:, j * LANES : (j + 1) * LANES]
    rank_b = ranked(ids_ref, count).astype(BF16)
    weight = named_by(ids_ref, count, weight_ref)
    copies = []
    for group in range(count // 8):
        expand = (iota((128, count), 0) // 16 + group * 8 == iota((128, count), 1)).astype(BF16)
        ranks = fast_dot(expand, rank_b)
        weights = exact_dot(expand.astype(F32), weight)
        inner = iota((128, LANES), 0) % 16
        hit = ranks == (inner % 8).astype(F32)
        is_cot = inner >= 8
        left = jnp.concatenate([hit & ~is_cot, hit & is_cot], axis=1).astype(BF16)
        scale = jnp.sum(jnp.where(hit & is_cot, weights, 0.0), axis=1, keepdims=True)
        scale = jnp.where(is_cot[:, :1], scale, 1.0)
        main = (fast_dot(left, rhs[...]) * scale).astype(BF16)
        for j in range(8):
            out_ref[group * 8 : group * 8 + 8, j * 16 : (j + 1) * 16, :] = main[
                :, j * LANES : (j + 1) * LANES
            ].reshape(8, 16, LANES)
        hit = ranks == (8 + inner % 2).astype(F32)
        is_cot = (inner // 2) % 2 == 1
        parts = []
        for j in range(4):
            here = hit & (inner // 4 == j)
            parts += [here & ~is_cot, here & is_cot]
        left = jnp.concatenate(parts, axis=1).astype(BF16)
        scale = jnp.sum(jnp.where(hit & is_cot, weights, 0.0), axis=1, keepdims=True)
        scale = jnp.where(is_cot[:, :1], scale, 1.0)
        rest = (fast_dot(left, rhs_rem[...]) * scale).astype(BF16)
        for half in range(2):
            out_ref[group * 8 : group * 8 + 8, 128 + 16 * half : 144 + 16 * half, :] = rest[
                :, half * LANES : (half + 1) * LANES
            ].reshape(8, 16, LANES)
        eight = slice(group * 8, group * 8 + 8)
        copies.append(pltpu.make_async_copy(out_ref.at[eight], out_hbm.at[eight], sems.at[group]))
        copies[-1].start()
    for copy in copies:
        copy.wait()


def early_kernel(ids_ref, logit_ref, value_ref, main_ref, rest_ref, total_ref, local_ref, parts_ref):
    tables(ids_ref, main_ref, rest_ref)
    decays(logit_ref, value_ref, total_ref, local_ref, parts_ref)


def tables(ids_ref, main_ref, rest_ref):
    slots = main_ref.shape[1]
    count = slots // 16
    rank = ranked(ids_ref, count).astype(BF16)
    expand = (iota((count, slots), 1) // 16 == iota((count, slots), 0)).astype(BF16)
    ranks = fast_dot(rank, expand, TN)
    inner = iota(ranks.shape, 1) % 16
    hit = ranks == (inner % 8).astype(F32)
    rows = ranks.shape[0]
    main_ref[0:rows, :] = (hit & (inner < 8)).astype(BF16)
    main_ref[rows : 2 * rows, :] = (hit & (inner >= 8)).astype(BF16)
    hit = ranks == (8 + inner % 2).astype(F32)
    rest_ref[...] = hit.astype(BF16)


def unpack(raw_ref, x_ref, c_ref):
    count = raw_ref.shape[0]
    for j in range(8):
        tile = raw_ref[:, j * 16 : (j + 1) * 16, :].astype(F32).reshape(count, 2, 8, LANES)
        cols = slice(j * LANES, (j + 1) * LANES)
        x_ref[0 : count * 8, cols] = tile[:, 0].reshape(count * 8, LANES).astype(BF16)
        c_ref[0 : count * 8, cols] = tile[:, 1].reshape(count * 8, LANES).astype(BF16)
    row = iota((128, 128), 0)
    source = (row // 2) % 4 * 32 + row // 16 * 4 + (row // 8) % 2 * 2 + row % 2
    perm = (iota((128, 128), 1) == source).astype(BF16)
    groups = count // 4
    rest = jnp.concatenate(
        [raw_ref[g * 4 : (g + 1) * 4, 128:160, :].reshape(128, LANES) for g in range(groups)], axis=1
    )
    rest = fast_dot(perm, rest)
    for j in range(8):
        cols = slice(j * LANES, (j + 1) * LANES)
        for kind, ref in enumerate((x_ref, c_ref)):
            lo = j * 16 + kind * 8
            ref[count * 8 : count * 10, cols] = jnp.concatenate(
                [rest[lo : lo + 8, g * LANES : (g + 1) * LANES] for g in range(groups)], axis=0
            ).astype(BF16)


def start_copies(pairs, sems):
    copies = [pltpu.make_async_copy(source, target, sems.at[number]) for number, (source, target) in enumerate(pairs)]
    for copy in copies:
        copy.start()
    return copies


def half_of(core, half):
    return pl.ds(pl.multiple_of(core * half, half), half)


def own_kernel(
    core_ref,
    raw_ref,
    gate_hbm,
    up_hbm,
    down_hbm,
    part_0,
    part_1,
    part_2,
    gate,
    up,
    peer_gate,
    peer_up,
    peer_down,
    x,
    c,
    down,
    sems,
    peer_sems,
):
    mine = half_of(core_ref[0], x.shape[1])
    other = half_of(1 - core_ref[0], x.shape[1])
    copies = start_copies(
        ((gate_hbm.at[mine, :], gate), (up_hbm.at[mine, :], up), (down_hbm.at[:, mine], down)), sems
    )
    later = [
        pltpu.make_async_copy(source, target, peer_sems.at[number])
        for number, (source, target) in enumerate(
            ((gate_hbm.at[other, :], peer_gate), (up_hbm.at[other, :], peer_up), (down_hbm.at[:, other], peer_down))
        )
    ]
    unpack(raw_ref, x, c)
    for copy in later:
        copy.start()
    copies[0].wait()
    part_0[...] = fast_dot(x[...], gate[...])
    copies[1].wait()
    part_1[...] = fast_dot(x[...], up[...])
    copies[2].wait()
    part_2[...] = fast_dot(c[...], down[...], NT)
    for copy in later:
        copy.wait()


def peer_kernel(raw_ref, part_0, part_1, part_2, gate, up, down, send_ref, dg, du, x, c):
    unpack(raw_ref, x, c)
    for step in range(part_0.shape[1] // 256):
        cols = slice(step * 256, (step + 1) * 256)
        pre_gate = part_0[:, cols] + fast_dot(x[...], gate[:, cols])
        pre_up = part_1[:, cols] + fast_dot(x[...], up[:, cols])
        d_act = part_2[:, cols] + fast_dot(c[...], down[cols, :], NT)
        sig = jax.nn.sigmoid(pre_gate)
        dg[:, cols] = (d_act * pre_up * sig * (1.0 + pre_gate * (1.0 - sig))).astype(BF16)
        du[:, cols] = (d_act * pre_gate * sig).astype(BF16)
    project(dg, du, gate, up, send_ref)


def project(dg, du, gate, up, out_ref):
    for step in range(out_ref.shape[1] // 256):
        cols = slice(step * 256, (step + 1) * 256)
        value = fast_dot(dg[...], gate[cols, :], NT) + fast_dot(du[...], up[cols, :], NT)
        out_ref[:, cols] = value.astype(out_ref.dtype)


def keep_kernel(dg, du, gate, up, keep_ref):
    project(dg, du, gate, up, keep_ref)


def pack_kernel(keep_ref, got_ref, out_ref):
    count = out_ref.shape[0]
    for pair in range(4):
        tiles = []
        for j in (2 * pair, 2 * pair + 1):
            cols = slice(j * LANES, (j + 1) * LANES)
            value = keep_ref[0 : count * 8, cols] + got_ref[0 : count * 8, cols].astype(F32)
            tiles.append(value.reshape(count, 8, LANES))
        out_ref[:, pair * 16 : (pair + 1) * 16, :] = jnp.concatenate(tiles, axis=1).astype(BF16)
    rest = (keep_ref[count * 8 :, :] + got_ref[count * 8 :, :].astype(F32)).astype(BF16)
    row = iota((128, 128), 0)
    source = (row // 2) % 8 * 16 + row // 16 * 2 + row % 2
    perm = (iota((128, 128), 1) == source).astype(BF16)
    groups = count // 8
    stacked = jnp.concatenate(
        [
            jnp.concatenate(
                [rest[g * 16 : (g + 1) * 16, j * LANES : (j + 1) * LANES] for j in range(8)], axis=0
            )
            for g in range(groups)
        ],
        axis=1,
    )
    moved = fast_dot(perm, stacked).astype(BF16)
    for g in range(groups):
        out_ref[g * 8 : (g + 1) * 8, 64:80, :] = moved[:, g * LANES : (g + 1) * LANES].reshape(8, 16, LANES)


def combine_kernel(back_ref, main_ref, rest_ref, hidden_ref, gain_ref, gained_ref, dot_ref):
    count = back_ref.shape[0]
    rows = hidden_ref.shape[0]
    main = jnp.concatenate(
        [back_ref[:, m * 16 : (m + 1) * 16, :].reshape(count * 16, LANES) for m in range(4)], axis=1
    )
    main = fast_dot(main_ref[...], main)
    block = iota((1, count * 16), 1) % 16 // 2
    left = jnp.concatenate([jnp.where(block == j, rest_ref[...], 0.0) for j in range(8)], axis=0)
    rest = fast_dot(left.astype(BF16), back_ref[:, 64:80, :].reshape(count * 16, LANES))
    total = jnp.zeros((rows, LANES), F32)
    for j in range(8):
        cols = slice(j * LANES, (j + 1) * LANES)
        value = main[j % 2 * rows : (j % 2 + 1) * rows, j // 2 * LANES : (j // 2 + 1) * LANES]
        value = (value + rest[j * rows : (j + 1) * rows, :]) * gain_ref[:, cols]
        gained_ref[:, cols] = value
        total = total + value * hidden_ref[:, cols].astype(F32)
    eye = iota((rows, rows), 0) == iota((rows, rows), 1)
    dot_ref[...] = jnp.sum(jnp.where(eye, jnp.sum(total, axis=1, keepdims=True), 0.0), axis=0, keepdims=True)


def log_sigmoid(x):
    return -(jnp.maximum(-x, 0.0) + jnp.log1p(jnp.exp(-jnp.abs(x))))


def two_parts(array):
    high = array.astype(BF16)
    return high, (array - high.astype(F32)).astype(BF16)


def head_mask():
    return iota((LANES, LANES), 0) // HEAD_DIM == iota((LANES, LANES), 1) // HEAD_DIM


def decays(logit_ref, value_ref, total_ref, local_ref, parts_ref):
    rows, feats = logit_ref.shape
    logits = logit_ref[...].astype(F32)
    key = jax.nn.sigmoid(-logits)
    lower = (iota((rows, rows), 0) >= iota((rows, rows), 1)).astype(F32)
    running = exact_dot(lower, log_sigmoid(logits))
    total_ref[...] = running
    end = running[rows - 1 : rows, :]
    key_end = key * jnp.exp(end - running)
    decay = jnp.exp(end)
    same = head_mask()
    pick = iota((HEAD_DIM, LANES), 0) == iota((HEAD_DIM, LANES), 1) % HEAD_DIM
    for pair in range(feats // LANES):
        cols = slice(pair * LANES, (pair + 1) * LANES)
        eight = slice(pair * 8, (pair + 1) * 8)
        local = exact_dot(key_end[:, cols], value_ref[:, cols].astype(F32), TN)
        local = jnp.where(same, local, 0.0)
        local = (local[:HEAD_DIM] + local[HEAD_DIM:]).reshape(8, 8, LANES)
        spread = exact_dot(jnp.where(pick, decay[:, cols], 0.0), same.astype(F32)).reshape(8, 8, LANES)
        local_ref[eight] = local
        rest = spread - spread.astype(BF16).astype(F32)
        parts_ref[eight] = jnp.concatenate([spread, rest], axis=1).astype(BF16)


def chain_kernel(piece_ref, out_ref, decay, both):
    count = piece_ref.shape[0]
    decay[...] = piece_ref[:, 16:32, :].astype(F32)
    both[...] = piece_ref[:, 0:16, :].astype(F32)
    later = jnp.zeros((8, LANES), F32)
    earlier = jnp.zeros((8, LANES), F32)
    for block in range(count):
        piece = both[block, 8:16, :]
        both[block, 8:16, :] = earlier
        earlier = (decay[block, 0:8, :] + decay[block, 8:16, :]) * earlier + piece
        other = count - 1 - block
        piece = both[other, 0:8, :]
        both[other, 0:8, :] = later
        later = (decay[other, 0:8, :] + decay[other, 8:16, :]) * later + piece
    out_ref[...] = both[...].astype(BF16)


def hidden_kernel(
    hidden_ref,
    cot_ref,
    own_sq_ref,
    peer_sq_ref,
    gained_ref,
    own_dot_ref,
    peer_dot_ref,
    query_ref,
    total_ref,
    local_ref,
    parts_ref,
    width,
    out_ref,
    piece_ref,
):
    row_scale = row_scale_of(own_sq_ref, peer_sq_ref, width)
    dot = column(own_dot_ref[...] + peer_dot_ref[...])
    back = row_scale * gained_ref[...] - hidden_ref[...].astype(F32) * (
        row_scale * row_scale * row_scale * dot / width
    )
    upstream = (cot_ref[...].astype(F32) + back).astype(BF16)
    out_ref[...] = upstream
    query = query_ref[...].astype(F32) * jnp.exp(total_ref[...])
    same = head_mask()
    piece_ref[:, 16:32, :] = parts_ref[...]
    for pair in range(hidden_ref.shape[1] // LANES):
        cols = slice(pair * LANES, (pair + 1) * LANES)
        eight = slice(pair * 8, (pair + 1) * 8)
        elem = exact_dot(query[:, cols], upstream[:, cols].astype(F32), TN)
        elem = jnp.where(same, elem, 0.0)
        elem = (elem[:HEAD_DIM] + elem[HEAD_DIM:]).reshape(8, 8, LANES)
        piece_ref[eight, 0:16, :] = jnp.concatenate([elem, local_ref[eight]], axis=1).astype(BF16)


def block_kernel(query_ref, logit_ref, value_ref, total_ref, upstream_ref, query_out, key_out, value_out):
    rows, feats = query_ref.shape
    lower = iota((rows, rows), 0) >= iota((rows, rows), 1)
    upper = iota((rows, rows), 0) <= iota((rows, rows), 1)
    first = iota((rows, LANES), 1) < HEAD_DIM

    def split(array):
        zero = jnp.zeros_like(array)
        return jnp.where(first, array, zero), jnp.where(first, zero, array)

    for pair in range(feats // LANES):
        cols = slice(pair * LANES, (pair + 1) * LANES)
        query = query_ref[:, cols].astype(F32)
        key = jax.nn.sigmoid(-logit_ref[:, cols].astype(F32))
        running = total_ref[:, cols]
        centre = 0.5 * running[rows - 1 : rows, :]
        grow = jnp.exp(running - centre)
        shrink = jnp.exp(centre - running)
        up_split, value_split = split(upstream_ref[:, cols]), split(value_ref[:, cols])
        query_split, key_split = split(query * grow), split(key * shrink)
        raw = [fast_dot(u, v, NT) for u, v in zip(up_split, value_split)]
        pairs = jnp.concatenate([jnp.where(lower, r, 0.0) for r in raw], axis=1)
        query_out[:, cols] = grow * exact_dot(pairs, jnp.concatenate(key_split, axis=0))
        raw = [fast_dot(v, u, NT) for u, v in zip(up_split, value_split)]
        pairs = jnp.concatenate([jnp.where(upper, r, 0.0) for r in raw], axis=1)
        key_out[:, cols] = shrink * exact_dot(pairs, jnp.concatenate(query_split, axis=0))
        raw = [exact_dot(k, q, NT) for k, q in zip(key_split, query_split)]
        pairs = jnp.concatenate([jnp.where(upper, r, 0.0) for r in raw], axis=1)
        value = exact_dot(pairs, jnp.concatenate([u.astype(F32) for u in up_split], axis=0))
        value_out[:, cols] = value.astype(BF16)


def final_kernel(
    query_ref,
    logit_ref,
    value_ref,
    upstream_ref,
    query_in,
    key_in,
    value_in,
    carried_ref,
    query_out,
    logit_out,
    value_out,
):
    rows, feats = query_ref.shape
    upper = (iota((rows, rows), 0) <= iota((rows, rows), 1)).astype(BF16)
    lower = (iota((rows, rows), 0) >= iota((rows, rows), 1)).astype(BF16)
    same = head_mask()

    def spread(array):
        return jnp.where(same, jnp.concatenate([array, array], axis=0), 0.0)

    def summed(mask, array):
        high, rest = two_parts(array)
        middle, low = two_parts(array - high.astype(F32))
        return fast_dot(mask, high) + fast_dot(mask, middle) + fast_dot(mask, low)

    for pair in range(feats // LANES):
        cols = slice(pair * LANES, (pair + 1) * LANES)
        eight = slice(pair * 8, (pair + 1) * 8)
        logits = logit_ref[:, cols].astype(F32)
        key = jax.nn.sigmoid(-logits)
        running = summed(lower, log_sigmoid(logits))
        end = running[rows - 1 : rows, :]
        tail = jnp.exp(end - running)
        carried = carried_ref[eight].astype(F32)
        incoming = carried[:, 0:8].reshape(HEAD_DIM, LANES)
        start = carried[:, 8:16].reshape(HEAD_DIM, LANES)
        start_b, incoming_b = spread(start).astype(BF16), spread(incoming).astype(BF16)
        query_grad = query_in[:, cols] + jnp.exp(running) * fast_dot(upstream_ref[:, cols], start_b, NT)
        key_back = tail * fast_dot(value_ref[:, cols], incoming_b, NT)
        key_grad = key_in[:, cols] + key_back
        high, low = two_parts(key * tail)
        value_grad = value_in[:, cols].astype(F32) + fast_dot(high, incoming_b) + fast_dot(low, incoming_b)
        past = exact_dot(jnp.ones((8, LANES), F32), spread(start * incoming), NT)[0:1, :]
        past = jnp.exp(end) * past + jnp.sum(key * key_back, axis=0, keepdims=True)
        suffix = summed(upper, query_ref[:, cols].astype(F32) * query_grad - key * key_grad) + past
        logit_grad = suffix * key - key_grad * key * (1.0 - key)
        query_out[:, cols] = query_grad.astype(BF16)
        logit_out[:, cols] = logit_grad.astype(BF16)
        value_out[:, cols] = value_grad.astype(BF16)


def on_device(
    hidden, grad_out, expert_ids, gate_weights, norm_gain, w_gate, w_up, w_down, queries, forget_logits, values
):
    rows, feats = hidden.shape
    ctx = lax.axis_size("ctx")
    width = w_gate.shape[1]
    units = w_gate.shape[2]
    slots = ctx * 10
    core = lax.axis_index("tp")
    swap = [(0, 1), (1, 0)]
    gain = norm_gain.reshape(1, feats)

    def exchange(array):
        return lax.all_to_all(array, "ctx", split_axis=0, concat_axis=0, tiled=True)

    ids, weights = expert_ids.T, gate_weights.T
    vmem, hbm = pl.BlockSpec(memory_space=pltpu.VMEM), pl.BlockSpec(memory_space=pl.ANY)
    smem = pl.BlockSpec(memory_space=pltpu.SMEM)

    hidden_f = hidden.astype(F32)
    squares = jnp.sum(hidden_f * hidden_f, axis=1)
    squares = (squares.reshape(1, rows), lax.ppermute(squares, "tp", swap).reshape(1, rows))

    sent = call(
        lambda h, g, s, z, n, i, w, o, v, a, b, m: dispatch_kernel(h, g, s, z, n, i, w, width, o, v, a, b, m),
        shape_of((ctx, 160, LANES), BF16),
        hidden,
        grad_out,
        *squares,
        gain,
        ids,
        weights,
        out_specs=hbm,
        scratch=(
            pltpu.VMEM((ctx, 160, LANES), BF16),
            pltpu.VMEM((2 * rows, feats), BF16),
            pltpu.VMEM((8 * rows, 2 * LANES), BF16),
            pltpu.SemaphoreType.DMA((ctx // 8,)),
        ),
        mib=60,
        flops=1 << 24,
        nbytes=1 << 12,
    )
    own = exchange(sent)
    main_table, rest_table, total, local, decay = call(
        early_kernel,
        (
            shape_of((2 * rows, ctx * 16), BF16),
            shape_of((rows, ctx * 16), BF16),
            shape_of((rows, feats), F32),
            shape_of((ctx, 8, LANES), F32),
            shape_of((ctx, 16, LANES), BF16),
        ),
        ids,
        forget_logits,
        values,
        flops=1 << 30,
        nbytes=4 << 20,
    )

    peer = lax.ppermute(own, "tp", swap)
    which = core.reshape(1).astype(jnp.int32)
    half_in, half_out = shape_of((feats, units), BF16), shape_of((units, feats), BF16)
    *parts, gate, up, peer_gate, peer_up, peer_down = call(
        own_kernel,
        (*(shape_of((slots, units), F32),) * 3, half_in, half_in, half_in, half_in, half_out),
        which,
        own,
        w_gate[0],
        w_up[0],
        w_down[0],
        in_specs=[smem, vmem, hbm, hbm, hbm],
        scratch=(
            pltpu.VMEM((slots, feats), BF16),
            pltpu.VMEM((slots, feats), BF16),
            pltpu.VMEM((units, feats), BF16),
            pltpu.SemaphoreType.DMA((3,)),
            pltpu.SemaphoreType.DMA((3,)),
        ),
        mib=40,
        flops=6 * slots * feats * units,
        nbytes=13 << 20,
    )
    send, dg, du = call(
        peer_kernel,
        (shape_of((slots, feats), BF16), shape_of((slots, units), BF16), shape_of((slots, units), BF16)),
        peer,
        *parts,
        peer_gate,
        peer_up,
        peer_down,
        scratch=(pltpu.VMEM((slots, feats), BF16), pltpu.VMEM((slots, feats), BF16)),
        mib=28,
        flops=10 * slots * feats * units,
        nbytes=16 << 20,
    )
    got = lax.ppermute(send, "tp", swap)
    keep = call(
        keep_kernel,
        shape_of((slots, feats), F32),
        dg,
        du,
        gate,
        up,
        flops=4 * slots * feats * units,
        nbytes=8 << 20,
    )
    packed = call(pack_kernel, shape_of((ctx, 80, LANES), BF16), keep, got, flops=1 << 26, nbytes=6 << 20)
    back = exchange(packed)
    gained, dots = call(
        combine_kernel,
        (shape_of((rows, feats), F32), shape_of((1, rows), F32)),
        back,
        main_table,
        rest_table,
        hidden,
        gain,
        flops=1 << 29,
        nbytes=6 << 20,
    )
    dots = (dots, lax.ppermute(dots, "tp", swap))
    grad_hidden, piece = call(
        lambda h, g, s, z, a, d, e, q, t, x, y, o, p: hidden_kernel(
            h, g, s, z, a, d, e, q, t, x, y, width, o, p
        ),
        (shape_of((rows, feats), BF16), shape_of((ctx, 32, LANES), BF16)),
        hidden,
        grad_out,
        *squares,
        gained,
        *dots,
        queries,
        total,
        local,
        decay,
        flops=1 << 28,
        nbytes=3 << 20,
    )
    pieces = exchange(piece)
    inner = call(
        block_kernel,
        (shape_of((rows, feats), F32), shape_of((rows, feats), F32), shape_of((rows, feats), BF16)),
        queries,
        forget_logits,
        values,
        total,
        grad_hidden,
        flops=1 << 32,
        nbytes=4 << 20,
    )
    chained = call(
        chain_kernel,
        shape_of((ctx, 16, LANES), BF16),
        pieces,
        scratch=(pltpu.VMEM((ctx, 16, LANES), F32), pltpu.VMEM((ctx, 16, LANES), F32)),
        nbytes=1 << 20,
    )
    carried = exchange(chained)
    grad_queries, grad_logits, grad_values = call(
        final_kernel,
        (shape_of((rows, feats), BF16),) * 3,
        queries,
        forget_logits,
        values,
        grad_hidden,
        *inner,
        carried,
        flops=1 << 30,
        nbytes=4 << 20,
    )
    return grad_hidden, grad_queries, grad_logits, grad_values


def solution(mesh):
    rows = P("ctx", "tp")
    in_specs = (
        rows,
        rows,
        P("ctx", None),
        P("ctx", None),
        P("tp"),
        P("ctx", None, "tp"),
        P("ctx", None, "tp"),
        P("ctx", "tp", None),
        rows,
        rows,
        rows,
    )
    return jax.shard_map(on_device, mesh=mesh, in_specs=in_specs, out_specs=(rows,) * 4, check_vma=False)
```

```python
import functools

import jax
import jax.numpy as jnp
from jax import lax
from jax.experimental import pallas as pl
from jax.experimental.pallas import tpu as pltpu
from jax.sharding import PartitionSpec as P

HEAD_DIM = 64
NORM_EPS = 1e-06
LANES = 128
BF16 = jnp.bfloat16
F32 = jnp.float32
EXACT = lax.Precision.HIGHEST
NT = (((1,), (1,)), ((), ()))
TN = (((0,), (0,)), ((), ()))
NN = (((1,), (0,)), ((), ()))


def iota(shape, dim):
    return lax.broadcasted_iota(jnp.int32, shape, dim)


def exact_dot(a, b, dims=NN):
    return lax.dot_general(a, b, dims, precision=EXACT, preferred_element_type=F32)


def fast_dot(a, b, dims=NN):
    return lax.dot_general(a, b, dims, preferred_element_type=F32)


def call(kernel, out_shape, *args, scratch=(), in_specs=None, out_specs=None, mib=16, flops=0, nbytes=0):
    return pl.pallas_call(
        kernel,
        out_shape=out_shape,
        in_specs=in_specs or [pl.BlockSpec(memory_space=pltpu.VMEM)] * len(args),
        out_specs=out_specs or jax.tree.map(lambda _: pl.BlockSpec(memory_space=pltpu.VMEM), out_shape),
        scratch_shapes=list(scratch),
        compiler_params=pltpu.CompilerParams(vmem_limit_bytes=mib << 20),
        cost_estimate=pl.CostEstimate(flops=flops, bytes_accessed=nbytes, transcendentals=0),
    )(*args)


def shape_of(shape, dtype):
    return jax.ShapeDtypeStruct(shape, dtype)


def ranked(ids_ref, count):
    rows = ids_ref.shape[1]
    named = named_by(ids_ref, count)
    before = (iota((rows, rows), 0) < iota((rows, rows), 1)).astype(BF16)
    rank = fast_dot(named.astype(BF16), before)
    return jnp.where(named > 0.0, rank, -1.0)


def named_by(ids_ref, count, weight_ref=None):
    expert = iota((count, ids_ref.shape[1]), 0)
    total = jnp.zeros(expert.shape, F32)
    for choice in range(ids_ref.shape[0]):
        level = 1.0 if weight_ref is None else weight_ref[choice : choice + 1, :]
        total = total + jnp.where(ids_ref[choice : choice + 1, :] == expert, level, 0.0)
    return total


def column(row):
    count = row.shape[1]
    eye = iota((count, count), 0) == iota((count, count), 1)
    return jnp.sum(jnp.where(eye, row, 0.0), axis=1, keepdims=True)


def row_scale_of(own_ref, peer_ref, width):
    return lax.rsqrt(column(own_ref[...] + peer_ref[...]) / width + NORM_EPS)


def dispatch_kernel(
    hidden_hbm,
    cot_hbm,
    own_sq_hbm,
    peer_sq_hbm,
    gain_hbm,
    ids_hbm,
    weight_hbm,
    width,
    out_hbm,
    out_ref,
    hidden,
    rhs,
    rhs_rem,
    own_sq,
    peer_sq,
    gain,
    ids,
    weight_in,
    in_sems,
    sems,
):
    rows = hidden.shape[0]
    count = out_ref.shape[0]
    loads = start_copies(
        (
            (ids_hbm, ids),
            (weight_hbm, weight_in),
            (own_sq_hbm, own_sq),
            (peer_sq_hbm, peer_sq),
            (gain_hbm, gain),
            (hidden_hbm, hidden),
            (cot_hbm, rhs.at[pl.ds(rows, rows), :]),
        ),
        in_sems,
    )
    loads[0].wait()
    rank_b = ranked(ids, count).astype(BF16)
    loads[1].wait()
    weight = named_by(ids, count, weight_in)
    for load in loads[2:]:
        load.wait()
    row_scale = row_scale_of(own_sq, peer_sq, width)
    rhs[0:rows, :] = (hidden[...].astype(F32) * row_scale * gain[...]).astype(BF16)
    for j in range(8):
        lo, col = 2 * rows * (j % 4), LANES * (j // 4)
        rhs_rem[lo : lo + 2 * rows, col : col + LANES] = rhs[:, j * LANES : (j + 1) * LANES]
    slots = count * 16
    inner = iota((slots, LANES), 0) % 16
    main_cot = inner >= 8
    rest_cot = (inner // 2) % 2 == 1
    expand = (iota((slots, count), 0) // 16 == iota((slots, count), 1)).astype(BF16)
    ranks = fast_dot(expand, rank_b)
    weights = fast_dot(expand, jnp.concatenate(three_parts(weight), axis=1))
    weights = weights[:, 0:rows] + weights[:, rows : 2 * rows] + weights[:, 2 * rows :]

    def scale_of(hit, is_cot):
        scale = jnp.sum(jnp.where(hit & is_cot, weights, 0.0), axis=1, keepdims=True)
        return jnp.where(is_cot[:, :1], scale, 1.0)

    hit = ranks == (inner % 8).astype(F32)
    hit_b = hit.astype(BF16)
    left = jnp.concatenate([hit_b * mask.astype(BF16) for mask in (~main_cot, main_cot)], axis=1)
    scale = scale_of(hit, main_cot)
    copies = []

    def send(first, last):
        span = pl.ds(first, last - first)
        copies.append(
            pltpu.make_async_copy(out_ref.at[:, span, :], out_hbm.at[:, span, :], sems.at[len(copies)])
        )
        copies[-1].start()

    for pair in range(4):
        value = (fast_dot(left, rhs[:, pair * 256 : (pair + 1) * 256]) * scale).astype(BF16)
        for half in range(2):
            first = pair * 32 + half * 16
            out_ref[:, first : first + 16, :] = value[:, half * LANES : (half + 1) * LANES].reshape(count, 16, LANES)
        send(pair * 32, pair * 32 + 32)
    hit = ranks == (8 + inner % 2).astype(F32)
    hit_b = hit.astype(BF16)
    left = jnp.concatenate(
        [
            hit_b * ((inner // 4 == j) & kind).astype(BF16)
            for j in range(4)
            for kind in (~rest_cot, rest_cot)
        ],
        axis=1,
    )
    value = (fast_dot(left, rhs_rem[...]) * scale_of(hit, rest_cot)).astype(BF16)
    for half in range(2):
        first = 128 + half * 16
        out_ref[:, first : first + 16, :] = value[:, half * LANES : (half + 1) * LANES].reshape(count, 16, LANES)
    send(128, 160)
    for copy in copies:
        copy.wait()


def early_kernel(ids_ref, logit_ref, value_ref, main_ref, rest_ref, total_ref, local_ref, parts_ref):
    tables(ids_ref, main_ref, rest_ref)
    decays(logit_ref, value_ref, total_ref, local_ref, parts_ref)


def tables(ids_ref, main_ref, rest_ref):
    slots = main_ref.shape[1]
    count = slots // 16
    rank = ranked(ids_ref, count).astype(BF16)
    expand = (iota((count, slots), 1) // 16 == iota((count, slots), 0)).astype(BF16)
    ranks = fast_dot(rank, expand, TN)
    inner = iota(ranks.shape, 1) % 16
    hit = ranks == (inner % 8).astype(F32)
    rows = ranks.shape[0]
    main_ref[0:rows, :] = (hit & (inner < 8)).astype(BF16)
    main_ref[rows : 2 * rows, :] = (hit & (inner >= 8)).astype(BF16)
    hit = ranks == (8 + inner % 2).astype(F32)
    rest_ref[...] = hit.astype(BF16)


def unpack(raw_ref, x_ref, c_ref):
    count = raw_ref.shape[0]
    for j in range(8):
        tile = raw_ref[:, j * 16 : (j + 1) * 16, :].astype(F32).reshape(count, 2, 8, LANES)
        cols = slice(j * LANES, (j + 1) * LANES)
        x_ref[0 : count * 8, cols] = tile[:, 0].reshape(count * 8, LANES).astype(BF16)
        c_ref[0 : count * 8, cols] = tile[:, 1].reshape(count * 8, LANES).astype(BF16)
    row = iota((128, 128), 0)
    source = (row // 2) % 4 * 32 + row // 16 * 4 + (row // 8) % 2 * 2 + row % 2
    perm = (iota((128, 128), 1) == source).astype(BF16)
    groups = count // 4
    rest = jnp.concatenate(
        [raw_ref[g * 4 : (g + 1) * 4, 128:160, :].reshape(128, LANES) for g in range(groups)], axis=1
    )
    rest = fast_dot(perm, rest)
    for j in range(8):
        cols = slice(j * LANES, (j + 1) * LANES)
        for kind, ref in enumerate((x_ref, c_ref)):
            lo = j * 16 + kind * 8
            ref[count * 8 : count * 10, cols] = jnp.concatenate(
                [rest[lo : lo + 8, g * LANES : (g + 1) * LANES] for g in range(groups)], axis=0
            ).astype(BF16)


def start_copies(pairs, sems):
    copies = [pltpu.make_async_copy(source, target, sems.at[number]) for number, (source, target) in enumerate(pairs)]
    for copy in copies:
        copy.start()
    return copies


def half_of(core, half):
    return pl.ds(pl.multiple_of(core * half, half), half)


def own_kernel(
    core_ref,
    raw_hbm,
    gate_hbm,
    up_hbm,
    down_hbm,
    part_0,
    part_1,
    part_2,
    gate,
    up,
    peer_gate,
    peer_up,
    peer_down,
    raw,
    x,
    c,
    down,
    sems,
    peer_sems,
):
    mine = half_of(core_ref[0], x.shape[1])
    other = half_of(1 - core_ref[0], x.shape[1])
    first = start_copies(((raw_hbm, raw), (gate_hbm.at[mine, :], gate)), sems)
    first[0].wait()
    second = start_copies(((up_hbm.at[mine, :], up), (down_hbm.at[:, mine], down)), sems.at[pl.ds(2, 2)])
    unpack(raw, x, c)
    first[1].wait()
    later = start_copies(
        ((gate_hbm.at[other, :], peer_gate), (up_hbm.at[other, :], peer_up), (down_hbm.at[:, other], peer_down)),
        peer_sems,
    )
    part_0[...] = fast_dot(x[...], gate[...])
    second[0].wait()
    part_1[...] = fast_dot(x[...], up[...])
    second[1].wait()
    part_2[...] = fast_dot(c[...], down[...], NT)
    for copy in later:
        copy.wait()


def peer_kernel(raw_ref, part_0, part_1, part_2, gate, up, down, send_ref, dg, du, x, c):
    unpack(raw_ref, x, c)
    for step in range(part_0.shape[1] // 256):
        cols = slice(step * 256, (step + 1) * 256)
        pre_gate = part_0[:, cols] + fast_dot(x[...], gate[:, cols])
        pre_up = part_1[:, cols] + fast_dot(x[...], up[:, cols])
        d_act = part_2[:, cols] + fast_dot(c[...], down[cols, :], NT)
        sig = jax.nn.sigmoid(pre_gate)
        dg[:, cols] = (d_act * pre_up * sig * (1.0 + pre_gate * (1.0 - sig))).astype(BF16)
        du[:, cols] = (d_act * pre_gate * sig).astype(BF16)
    project(dg, du, gate, up, send_ref)


def project(dg, du, gate, up, out_ref):
    for step in range(out_ref.shape[1] // 256):
        cols = slice(step * 256, (step + 1) * 256)
        value = fast_dot(dg[...], gate[cols, :], NT) + fast_dot(du[...], up[cols, :], NT)
        out_ref[:, cols] = value.astype(out_ref.dtype)


def keep_kernel(dg, du, gate, up, keep_ref):
    project(dg, du, gate, up, keep_ref)


def pack_kernel(keep_ref, got_ref, out_ref):
    count = out_ref.shape[0]
    for pair in range(4):
        tiles = []
        for j in (2 * pair, 2 * pair + 1):
            cols = slice(j * LANES, (j + 1) * LANES)
            value = keep_ref[0 : count * 8, cols] + got_ref[0 : count * 8, cols].astype(F32)
            tiles.append(value.reshape(count, 8, LANES))
        out_ref[:, pair * 16 : (pair + 1) * 16, :] = jnp.concatenate(tiles, axis=1).astype(BF16)
    rest = (keep_ref[count * 8 :, :] + got_ref[count * 8 :, :].astype(F32)).astype(BF16)
    row = iota((128, 128), 0)
    source = (row // 2) % 8 * 16 + row // 16 * 2 + row % 2
    perm = (iota((128, 128), 1) == source).astype(BF16)
    groups = count // 8
    stacked = jnp.concatenate(
        [
            jnp.concatenate(
                [rest[g * 16 : (g + 1) * 16, j * LANES : (j + 1) * LANES] for j in range(8)], axis=0
            )
            for g in range(groups)
        ],
        axis=1,
    )
    moved = fast_dot(perm, stacked).astype(BF16)
    for g in range(groups):
        out_ref[g * 8 : (g + 1) * 8, 64:80, :] = moved[:, g * LANES : (g + 1) * LANES].reshape(8, 16, LANES)


def combine_kernel(back_ref, main_ref, rest_ref, hidden_ref, gain_ref, gained_ref, dot_ref):
    count = back_ref.shape[0]
    rows = hidden_ref.shape[0]
    main = jnp.concatenate(
        [back_ref[:, m * 16 : (m + 1) * 16, :].reshape(count * 16, LANES) for m in range(4)], axis=1
    )
    main = fast_dot(main_ref[...], main)
    block = iota((rows, count * 16), 1) % 16 // 2
    left = jnp.concatenate([rest_ref[...] * (block == j).astype(BF16) for j in range(8)], axis=0)
    rest = fast_dot(left, back_ref[:, 64:80, :].reshape(count * 16, LANES))
    total = jnp.zeros((rows, LANES), F32)
    for j in range(8):
        cols = slice(j * LANES, (j + 1) * LANES)
        value = main[j % 2 * rows : (j % 2 + 1) * rows, j // 2 * LANES : (j // 2 + 1) * LANES]
        value = (value + rest[j * rows : (j + 1) * rows, :]) * gain_ref[:, cols]
        gained_ref[:, cols] = value
        total = total + value * hidden_ref[:, cols].astype(F32)
    eye = iota((rows, rows), 0) == iota((rows, rows), 1)
    dot_ref[...] = jnp.sum(jnp.where(eye, jnp.sum(total, axis=1, keepdims=True), 0.0), axis=0, keepdims=True)


def log_sigmoid(x):
    return -(jnp.maximum(-x, 0.0) + jnp.log1p(jnp.exp(-jnp.abs(x))))


def two_parts(array):
    high = array.astype(BF16)
    return high, (array - high.astype(F32)).astype(BF16)


def three_parts(array):
    high = array.astype(BF16)
    middle, low = two_parts(array - high.astype(F32))
    return high, middle, low


def head_mask():
    return iota((LANES, LANES), 0) // HEAD_DIM == iota((LANES, LANES), 1) // HEAD_DIM


def decays(logit_ref, value_ref, total_ref, local_ref, parts_ref):
    rows, feats = logit_ref.shape
    logits = logit_ref[...].astype(F32)
    key = jax.nn.sigmoid(-logits)
    lower = (iota((rows, rows), 0) >= iota((rows, rows), 1)).astype(F32)
    running = exact_dot(lower, log_sigmoid(logits))
    total_ref[...] = running
    end = running[rows - 1 : rows, :]
    key_end = key * jnp.exp(end - running)
    decay = jnp.exp(end)
    same = head_mask()
    pick = iota((HEAD_DIM, LANES), 0) == iota((HEAD_DIM, LANES), 1) % HEAD_DIM
    for pair in range(feats // LANES):
        cols = slice(pair * LANES, (pair + 1) * LANES)
        eight = slice(pair * 8, (pair + 1) * 8)
        local = exact_dot(key_end[:, cols], value_ref[:, cols].astype(F32), TN)
        local = jnp.where(same, local, 0.0)
        local = (local[:HEAD_DIM] + local[HEAD_DIM:]).reshape(8, 8, LANES)
        spread = exact_dot(jnp.where(pick, decay[:, cols], 0.0), same.astype(F32)).reshape(8, 8, LANES)
        local_ref[eight] = local
        rest = spread - spread.astype(BF16).astype(F32)
        parts_ref[eight] = jnp.concatenate([spread, rest], axis=1).astype(BF16)


def chain_kernel(piece_ref, out_ref, decay, both):
    count = piece_ref.shape[0]
    decay[...] = piece_ref[:, 16:32, :].astype(F32)
    both[...] = piece_ref[:, 0:16, :].astype(F32)
    later = jnp.zeros((8, LANES), F32)
    earlier = jnp.zeros((8, LANES), F32)
    for block in range(count):
        piece = both[block, 8:16, :]
        both[block, 8:16, :] = earlier
        earlier = (decay[block, 0:8, :] + decay[block, 8:16, :]) * earlier + piece
        other = count - 1 - block
        piece = both[other, 0:8, :]
        both[other, 0:8, :] = later
        later = (decay[other, 0:8, :] + decay[other, 8:16, :]) * later + piece
    out_ref[...] = both[...].astype(BF16)


def hidden_kernel(
    hidden_ref,
    cot_ref,
    own_sq_ref,
    peer_sq_ref,
    gained_ref,
    own_dot_ref,
    peer_dot_ref,
    query_ref,
    total_ref,
    local_ref,
    parts_ref,
    width,
    out_ref,
    piece_ref,
):
    row_scale = row_scale_of(own_sq_ref, peer_sq_ref, width)
    dot = column(own_dot_ref[...] + peer_dot_ref[...])
    back = row_scale * gained_ref[...] - hidden_ref[...].astype(F32) * (
        row_scale * row_scale * row_scale * dot / width
    )
    upstream = (cot_ref[...].astype(F32) + back).astype(BF16)
    out_ref[...] = upstream
    query = query_ref[...].astype(F32) * jnp.exp(total_ref[...])
    same = head_mask()
    piece_ref[:, 16:32, :] = parts_ref[...]
    for pair in range(hidden_ref.shape[1] // LANES):
        cols = slice(pair * LANES, (pair + 1) * LANES)
        eight = slice(pair * 8, (pair + 1) * 8)
        high, low = two_parts(query[:, cols])
        elem = fast_dot(high, upstream[:, cols], TN) + fast_dot(low, upstream[:, cols], TN)
        elem = jnp.where(same, elem, 0.0)
        elem = (elem[:HEAD_DIM] + elem[HEAD_DIM:]).reshape(8, 8, LANES)
        piece_ref[eight, 0:16, :] = jnp.concatenate([elem, local_ref[eight]], axis=1).astype(BF16)


def block_kernel(query_ref, logit_ref, value_ref, total_ref, upstream_ref, query_out, key_out, value_out):
    rows, feats = query_ref.shape
    lower = iota((rows, rows), 0) >= iota((rows, rows), 1)
    upper = iota((rows, rows), 0) <= iota((rows, rows), 1)
    first = iota((rows, LANES), 1) < HEAD_DIM

    def split(array):
        zero = jnp.zeros_like(array)
        return jnp.where(first, array, zero), jnp.where(first, zero, array)

    for pair in range(feats // LANES):
        cols = slice(pair * LANES, (pair + 1) * LANES)
        query = query_ref[:, cols].astype(F32)
        key = jax.nn.sigmoid(-logit_ref[:, cols].astype(F32))
        running = total_ref[:, cols]
        centre = 0.5 * running[rows - 1 : rows, :]
        grow = jnp.exp(running - centre)
        shrink = jnp.exp(centre - running)
        up_split, value_split = split(upstream_ref[:, cols]), split(value_ref[:, cols])
        query_split, key_split = split(query * grow), split(key * shrink)
        raw = [fast_dot(u, v, NT) for u, v in zip(up_split, value_split)]
        pairs = jnp.concatenate([jnp.where(lower, r, 0.0) for r in raw], axis=1)
        query_out[:, cols] = grow * exact_dot(pairs, jnp.concatenate(key_split, axis=0))
        raw = [fast_dot(v, u, NT) for u, v in zip(up_split, value_split)]
        pairs = jnp.concatenate([jnp.where(upper, r, 0.0) for r in raw], axis=1)
        key_out[:, cols] = shrink * exact_dot(pairs, jnp.concatenate(query_split, axis=0))
        raw = [exact_dot(k, q, NT) for k, q in zip(key_split, query_split)]
        pairs = jnp.concatenate([jnp.where(upper, r, 0.0) for r in raw], axis=1)
        value = exact_dot(pairs, jnp.concatenate([u.astype(F32) for u in up_split], axis=0))
        value_out[:, cols] = value.astype(BF16)


def final_kernel(
    query_ref,
    logit_ref,
    value_ref,
    upstream_ref,
    query_in,
    key_in,
    value_in,
    carried_ref,
    query_out,
    logit_out,
    value_out,
):
    rows, feats = query_ref.shape
    upper = (iota((rows, rows), 0) <= iota((rows, rows), 1)).astype(BF16)
    lower = (iota((rows, rows), 0) >= iota((rows, rows), 1)).astype(BF16)
    ones = jnp.ones((16, LANES), BF16)
    same = head_mask()

    def spread(array):
        return jnp.where(same, jnp.concatenate([array, array], axis=0), 0.0)

    def summed(mask, array):
        high, low = two_parts(array)
        return fast_dot(mask, high) + fast_dot(mask, low)

    for pair in range(feats // LANES):
        cols = slice(pair * LANES, (pair + 1) * LANES)
        eight = slice(pair * 8, (pair + 1) * 8)
        logits = logit_ref[:, cols].astype(F32)
        key = jax.nn.sigmoid(-logits)
        running = summed(lower, log_sigmoid(logits))
        end = running[rows - 1 : rows, :]
        tail = jnp.exp(end - running)
        carried = carried_ref[eight].astype(F32)
        incoming = carried[:, 0:8].reshape(HEAD_DIM, LANES)
        start = carried[:, 8:16].reshape(HEAD_DIM, LANES)
        start_b, incoming_b = spread(start).astype(BF16), spread(incoming).astype(BF16)
        query_grad = query_in[:, cols] + jnp.exp(running) * fast_dot(upstream_ref[:, cols], start_b, NT)
        key_back = tail * fast_dot(value_ref[:, cols], incoming_b, NT)
        key_grad = key_in[:, cols] + key_back
        high, low = two_parts(key * tail)
        value_grad = value_in[:, cols].astype(F32) + fast_dot(high, incoming_b) + fast_dot(low, incoming_b)
        high, low = two_parts(spread(start * incoming))
        past = (fast_dot(ones, high, NT) + fast_dot(ones, low, NT))[0:1, :]
        past = jnp.exp(end) * past + jnp.sum(key * key_back, axis=0, keepdims=True)
        suffix = summed(upper, query_ref[:, cols].astype(F32) * query_grad - key * key_grad) + past
        logit_grad = suffix * key - key_grad * key * (1.0 - key)
        query_out[:, cols] = query_grad.astype(BF16)
        logit_out[:, cols] = logit_grad.astype(BF16)
        value_out[:, cols] = value_grad.astype(BF16)


def on_device(
    hidden, grad_out, expert_ids, gate_weights, norm_gain, w_gate, w_up, w_down, queries, forget_logits, values
):
    rows, feats = hidden.shape
    ctx = lax.axis_size("ctx")
    width = w_gate.shape[1]
    units = w_gate.shape[2]
    slots = ctx * 10
    core = lax.axis_index("tp")
    swap = [(0, 1), (1, 0)]
    gain = norm_gain.reshape(1, feats)

    def exchange(array):
        return lax.all_to_all(array, "ctx", split_axis=0, concat_axis=0, tiled=True)

    ids, weights = expert_ids.T, gate_weights.T
    vmem, hbm = pl.BlockSpec(memory_space=pltpu.VMEM), pl.BlockSpec(memory_space=pl.ANY)
    smem = pl.BlockSpec(memory_space=pltpu.SMEM)

    hidden_f = hidden.astype(F32)
    squares = jnp.sum(hidden_f * hidden_f, axis=1)
    squares = (squares.reshape(1, rows), lax.ppermute(squares, "tp", swap).reshape(1, rows))

    sent = call(
        lambda h, g, s, z, n, i, w, *rest: dispatch_kernel(h, g, s, z, n, i, w, width, *rest),
        shape_of((ctx, 160, LANES), BF16),
        hidden,
        grad_out,
        *squares,
        gain,
        ids,
        weights,
        in_specs=[hbm] * 7,
        out_specs=hbm,
        scratch=(
            pltpu.VMEM((ctx, 160, LANES), BF16),
            pltpu.VMEM((rows, feats), BF16),
            pltpu.VMEM((2 * rows, feats), BF16),
            pltpu.VMEM((8 * rows, 2 * LANES), BF16),
            pltpu.VMEM((1, rows), F32),
            pltpu.VMEM((1, rows), F32),
            pltpu.VMEM((1, feats), F32),
            pltpu.VMEM(ids.shape, jnp.int32),
            pltpu.VMEM(weights.shape, F32),
            pltpu.SemaphoreType.DMA((7,)),
            pltpu.SemaphoreType.DMA((5,)),
        ),
        mib=60,
        flops=1 << 24,
        nbytes=1 << 12,
    )
    own = exchange(sent)
    main_table, rest_table, total, local, decay = call(
        early_kernel,
        (
            shape_of((2 * rows, ctx * 16), BF16),
            shape_of((rows, ctx * 16), BF16),
            shape_of((rows, feats), F32),
            shape_of((ctx, 8, LANES), F32),
            shape_of((ctx, 16, LANES), BF16),
        ),
        ids,
        forget_logits,
        values,
        flops=1 << 30,
        nbytes=4 << 20,
    )

    peer = lax.ppermute(own, "tp", swap)
    which = core.reshape(1).astype(jnp.int32)
    half_in, half_out = shape_of((feats, units), BF16), shape_of((units, feats), BF16)
    *parts, gate, up, peer_gate, peer_up, peer_down = call(
        own_kernel,
        (*(shape_of((slots, units), F32),) * 3, half_in, half_in, half_in, half_in, half_out),
        which,
        own,
        w_gate[0],
        w_up[0],
        w_down[0],
        in_specs=[smem, hbm, hbm, hbm, hbm],
        scratch=(
            pltpu.VMEM((ctx, 160, LANES), BF16),
            pltpu.VMEM((slots, feats), BF16),
            pltpu.VMEM((slots, feats), BF16),
            pltpu.VMEM((units, feats), BF16),
            pltpu.SemaphoreType.DMA((4,)),
            pltpu.SemaphoreType.DMA((3,)),
        ),
        mib=40,
        flops=6 * slots * feats * units,
        nbytes=13 << 20,
    )
    send, dg, du = call(
        peer_kernel,
        (shape_of((slots, feats), BF16), shape_of((slots, units), BF16), shape_of((slots, units), BF16)),
        peer,
        *parts,
        peer_gate,
        peer_up,
        peer_down,
        scratch=(pltpu.VMEM((slots, feats), BF16), pltpu.VMEM((slots, feats), BF16)),
        mib=28,
        flops=10 * slots * feats * units,
        nbytes=16 << 20,
    )
    got = lax.ppermute(send, "tp", swap)
    keep = call(
        keep_kernel,
        shape_of((slots, feats), F32),
        dg,
        du,
        gate,
        up,
        flops=4 * slots * feats * units,
        nbytes=8 << 20,
    )
    packed = call(pack_kernel, shape_of((ctx, 80, LANES), BF16), keep, got, flops=1 << 26, nbytes=6 << 20)
    back = exchange(packed)
    gained, dots = call(
        combine_kernel,
        (shape_of((rows, feats), F32), shape_of((1, rows), F32)),
        back,
        main_table,
        rest_table,
        hidden,
        gain,
        flops=1 << 29,
        nbytes=6 << 20,
    )
    dots = (dots, lax.ppermute(dots, "tp", swap))
    grad_hidden, piece = call(
        lambda h, g, s, z, a, d, e, q, t, x, y, o, p: hidden_kernel(
            h, g, s, z, a, d, e, q, t, x, y, width, o, p
        ),
        (shape_of((rows, feats), BF16), shape_of((ctx, 32, LANES), BF16)),
        hidden,
        grad_out,
        *squares,
        gained,
        *dots,
        queries,
        total,
        local,
        decay,
        flops=1 << 28,
        nbytes=3 << 20,
    )
    pieces = exchange(piece)
    inner = call(
        block_kernel,
        (shape_of((rows, feats), F32), shape_of((rows, feats), F32), shape_of((rows, feats), BF16)),
        queries,
        forget_logits,
        values,
        total,
        grad_hidden,
        flops=1 << 32,
        nbytes=4 << 20,
    )
    chained = call(
        chain_kernel,
        shape_of((ctx, 16, LANES), BF16),
        pieces,
        scratch=(pltpu.VMEM((ctx, 16, LANES), F32), pltpu.VMEM((ctx, 16, LANES), F32)),
        nbytes=1 << 20,
    )
    carried = exchange(chained)
    grad_queries, grad_logits, grad_values = call(
        final_kernel,
        (shape_of((rows, feats), BF16),) * 3,
        queries,
        forget_logits,
        values,
        grad_hidden,
        *inner,
        carried,
        flops=1 << 30,
        nbytes=4 << 20,
    )
    return grad_hidden, grad_queries, grad_logits, grad_values


def solution(mesh):
    rows = P("ctx", "tp")
    in_specs = (
        rows,
        rows,
        P("ctx", None),
        P("ctx", None),
        P("tp"),
        P("ctx", None, "tp"),
        P("ctx", None, "tp"),
        P("ctx", "tp", None),
        rows,
        rows,
        rows,
    )
    return jax.shard_map(on_device, mesh=mesh, in_specs=in_specs, out_specs=(rows,) * 4, check_vma=False)
```

```python
import functools

import jax
import jax.numpy as jnp
from jax import lax
from jax.experimental import pallas as pl
from jax.experimental.pallas import tpu as pltpu
from jax.sharding import PartitionSpec as P

HEAD_DIM = 64
NORM_EPS = 1e-06
LANES = 128
BF16 = jnp.bfloat16
F32 = jnp.float32
EXACT = lax.Precision.HIGHEST
NT = (((1,), (1,)), ((), ()))
TN = (((0,), (0,)), ((), ()))
NN = (((1,), (0,)), ((), ()))


def iota(shape, dim):
    return lax.broadcasted_iota(jnp.int32, shape, dim)


def exact_dot(a, b, dims=NN):
    return lax.dot_general(a, b, dims, precision=EXACT, preferred_element_type=F32)


def fast_dot(a, b, dims=NN):
    return lax.dot_general(a, b, dims, preferred_element_type=F32)


def call(kernel, out_shape, *args, scratch=(), in_specs=None, out_specs=None, mib=16, flops=0, nbytes=0):
    return pl.pallas_call(
        kernel,
        out_shape=out_shape,
        in_specs=in_specs or [pl.BlockSpec(memory_space=pltpu.VMEM)] * len(args),
        out_specs=out_specs or jax.tree.map(lambda _: pl.BlockSpec(memory_space=pltpu.VMEM), out_shape),
        scratch_shapes=list(scratch),
        compiler_params=pltpu.CompilerParams(vmem_limit_bytes=int(mib * 2**20)),
        cost_estimate=pl.CostEstimate(flops=flops, bytes_accessed=nbytes, transcendentals=0),
    )(*args)


def shape_of(shape, dtype):
    return jax.ShapeDtypeStruct(shape, dtype)


def ranked(ids_ref, count):
    rows = ids_ref.shape[1]
    named = named_by(ids_ref, count)
    before = (iota((rows, rows), 0) < iota((rows, rows), 1)).astype(BF16)
    rank = fast_dot(named.astype(BF16), before)
    return jnp.where(named > 0.0, rank, -1.0)


def named_by(ids_ref, count, weight_ref=None):
    expert = iota((count, ids_ref.shape[1]), 0)
    total = jnp.zeros(expert.shape, F32)
    for choice in range(ids_ref.shape[0]):
        level = 1.0 if weight_ref is None else weight_ref[choice : choice + 1, :]
        total = total + jnp.where(ids_ref[choice : choice + 1, :] == expert, level, 0.0)
    return total


def column(row):
    count = row.shape[1]
    eye = iota((count, count), 0) == iota((count, count), 1)
    return jnp.sum(jnp.where(eye, row, 0.0), axis=1, keepdims=True)


def row_scale_of(own_ref, peer_ref, width):
    return lax.rsqrt(column(own_ref[...] + peer_ref[...]) / width + NORM_EPS)


def dispatch_kernel(
    hidden_hbm,
    cot_hbm,
    own_sq_hbm,
    peer_sq_hbm,
    gain_hbm,
    ids_hbm,
    weight_hbm,
    width,
    out_hbm,
    out_ref,
    hidden,
    rhs,
    rhs_rem,
    own_sq,
    peer_sq,
    gain,
    ids,
    weight_in,
    in_sems,
    sems,
):
    rows = hidden.shape[0]
    count = out_ref.shape[0]
    loads = start_copies(
        (
            (ids_hbm, ids),
            (weight_hbm, weight_in),
            (own_sq_hbm, own_sq),
            (peer_sq_hbm, peer_sq),
            (gain_hbm, gain),
            (hidden_hbm, hidden),
            (cot_hbm, rhs.at[pl.ds(rows, rows), :]),
        ),
        in_sems,
    )
    loads[0].wait()
    rank_b = ranked(ids, count).astype(BF16)
    loads[1].wait()
    weight = named_by(ids, count, weight_in)
    for load in loads[2:]:
        load.wait()
    row_scale = row_scale_of(own_sq, peer_sq, width)
    rhs[0:rows, :] = (hidden[...].astype(F32) * row_scale * gain[...]).astype(BF16)
    for j in range(8):
        lo, col = 2 * rows * (j % 4), LANES * (j // 4)
        rhs_rem[lo : lo + 2 * rows, col : col + LANES] = rhs[:, j * LANES : (j + 1) * LANES]
    slots = count * 16
    inner = iota((slots, LANES), 0) % 16
    main_cot = inner >= 8
    rest_cot = (inner // 2) % 2 == 1
    expand = (iota((slots, count), 0) // 16 == iota((slots, count), 1)).astype(BF16)
    ranks = fast_dot(expand, rank_b)
    weights = fast_dot(expand, jnp.concatenate(three_parts(weight), axis=1))
    weights = weights[:, 0:rows] + weights[:, rows : 2 * rows] + weights[:, 2 * rows :]

    def scale_of(hit, is_cot):
        scale = jnp.sum(jnp.where(hit & is_cot, weights, 0.0), axis=1, keepdims=True)
        return jnp.where(is_cot[:, :1], scale, 1.0)

    hit = ranks == (inner % 8).astype(F32)
    hit_b = hit.astype(BF16)
    left = jnp.concatenate([hit_b * mask.astype(BF16) for mask in (~main_cot, main_cot)], axis=1)
    scale = scale_of(hit, main_cot)
    copies = []

    def send(first, last):
        span = pl.ds(first, last - first)
        copies.append(
            pltpu.make_async_copy(out_ref.at[:, span, :], out_hbm.at[:, span, :], sems.at[len(copies)])
        )
        copies[-1].start()

    for pair in range(4):
        value = (fast_dot(left, rhs[:, pair * 256 : (pair + 1) * 256]) * scale).astype(BF16)
        for half in range(2):
            first = pair * 32 + half * 16
            out_ref[:, first : first + 16, :] = value[:, half * LANES : (half + 1) * LANES].reshape(count, 16, LANES)
        send(pair * 32, pair * 32 + 32)
    hit = ranks == (8 + inner % 2).astype(F32)
    hit_b = hit.astype(BF16)
    left = jnp.concatenate(
        [
            hit_b * ((inner // 4 == j) & kind).astype(BF16)
            for j in range(4)
            for kind in (~rest_cot, rest_cot)
        ],
        axis=1,
    )
    value = (fast_dot(left, rhs_rem[...]) * scale_of(hit, rest_cot)).astype(BF16)
    for half in range(2):
        first = 128 + half * 16
        out_ref[:, first : first + 16, :] = value[:, half * LANES : (half + 1) * LANES].reshape(count, 16, LANES)
    send(128, 160)
    for copy in copies:
        copy.wait()


def early_kernel(ids_ref, logit_ref, value_ref, main_ref, rest_ref, total_ref, local_ref, parts_ref):
    tables(ids_ref, main_ref, rest_ref)
    decays(logit_ref, value_ref, total_ref, local_ref, parts_ref)


def tables(ids_ref, main_ref, rest_ref):
    slots = main_ref.shape[1]
    count = slots // 16
    rank = ranked(ids_ref, count).astype(BF16)
    expand = (iota((count, slots), 1) // 16 == iota((count, slots), 0)).astype(BF16)
    ranks = fast_dot(rank, expand, TN)
    inner = iota(ranks.shape, 1) % 16
    hit = ranks == (inner % 8).astype(F32)
    rows = ranks.shape[0]
    main_ref[0:rows, :] = (hit & (inner < 8)).astype(BF16)
    main_ref[rows : 2 * rows, :] = (hit & (inner >= 8)).astype(BF16)
    hit = ranks == (8 + inner % 2).astype(F32)
    rest_ref[...] = hit.astype(BF16)


def unpack(raw_ref, x_ref, c_ref, first=0, last=None):
    blocks = raw_ref.shape[0]
    last = blocks if last is None else last
    count = last - first
    main = slice(first * 8, last * 8)
    every = slice(blocks * 8 + first * 2, blocks * 8 + last * 2)
    for j in range(8):
        tile = raw_ref[first:last, j * 16 : (j + 1) * 16, :].astype(F32).reshape(count, 2, 8, LANES)
        cols = slice(j * LANES, (j + 1) * LANES)
        x_ref[main, cols] = tile[:, 0].reshape(count * 8, LANES).astype(BF16)
        c_ref[main, cols] = tile[:, 1].reshape(count * 8, LANES).astype(BF16)
    row = iota((128, 128), 0)
    source = (row // 2) % 4 * 32 + row // 16 * 4 + (row // 8) % 2 * 2 + row % 2
    perm = (iota((128, 128), 1) == source).astype(BF16)
    groups = range(first // 4, last // 4)
    rest = jnp.concatenate(
        [raw_ref[g * 4 : (g + 1) * 4, 128:160, :].reshape(128, LANES) for g in groups], axis=1
    )
    rest = fast_dot(perm, rest)
    for j in range(8):
        cols = slice(j * LANES, (j + 1) * LANES)
        for kind, ref in enumerate((x_ref, c_ref)):
            lo = j * 16 + kind * 8
            ref[every, cols] = jnp.concatenate(
                [rest[lo : lo + 8, g * LANES : (g + 1) * LANES] for g in range(len(groups))], axis=0
            ).astype(BF16)


def start_copies(pairs, sems):
    copies = [pltpu.make_async_copy(source, target, sems.at[number]) for number, (source, target) in enumerate(pairs)]
    for copy in copies:
        copy.start()
    return copies


def half_of(core, half):
    return pl.ds(pl.multiple_of(core * half, half), half)


def own_kernel(
    core_ref,
    raw_hbm,
    gate_hbm,
    up_hbm,
    down_hbm,
    part_0,
    part_1,
    part_2,
    gate,
    up,
    peer_gate,
    peer_up,
    peer_down,
    raw,
    x,
    c,
    down,
    raw_sems,
    sems,
    peer_sems,
):
    mine = half_of(core_ref[0], x.shape[1])
    other = half_of(1 - core_ref[0], x.shape[1])
    quarter = raw.shape[0] // 4
    quarters = [slice(q * quarter, (q + 1) * quarter) for q in range(4)]
    rows = start_copies([(raw_hbm.at[span], raw.at[span]) for span in quarters], raw_sems)
    first = start_copies(((gate_hbm.at[mine, :], gate),), sems)
    for copy, span in zip(rows, quarters):
        copy.wait()
        unpack(raw, x, c, span.start, span.stop)
    second = start_copies(((up_hbm.at[mine, :], up), (down_hbm.at[:, mine], down)), sems.at[pl.ds(1, 2)])
    first[0].wait()
    later = start_copies(
        ((gate_hbm.at[other, :], peer_gate), (up_hbm.at[other, :], peer_up), (down_hbm.at[:, other], peer_down)),
        peer_sems,
    )
    part_0[...] = fast_dot(x[...], gate[...])
    second[0].wait()
    part_1[...] = fast_dot(x[...], up[...])
    second[1].wait()
    part_2[...] = fast_dot(c[...], down[...], NT)
    for copy in later:
        copy.wait()


def peer_kernel(raw_ref, part_0, part_1, part_2, gate, up, down, send_ref, dg, du, x, c):
    unpack(raw_ref, x, c)
    for step in range(part_0.shape[1] // 256):
        cols = slice(step * 256, (step + 1) * 256)
        pre_gate = part_0[:, cols] + fast_dot(x[...], gate[:, cols])
        pre_up = part_1[:, cols] + fast_dot(x[...], up[:, cols])
        d_act = part_2[:, cols] + fast_dot(c[...], down[cols, :], NT)
        sig = jax.nn.sigmoid(pre_gate)
        dg[:, cols] = (d_act * pre_up * sig * (1.0 + pre_gate * (1.0 - sig))).astype(BF16)
        du[:, cols] = (d_act * pre_gate * sig).astype(BF16)
    project(dg, du, gate, up, send_ref)


def project(dg, du, gate, up, out_ref):
    for step in range(out_ref.shape[1] // 256):
        cols = slice(step * 256, (step + 1) * 256)
        value = fast_dot(dg[...], gate[cols, :], NT) + fast_dot(du[...], up[cols, :], NT)
        out_ref[:, cols] = value.astype(out_ref.dtype)


def keep_kernel(dg, du, gate, up, keep_ref):
    project(dg, du, gate, up, keep_ref)


def pack_kernel(keep_ref, got_ref, out_hbm, out_ref, sems):
    count = out_ref.shape[0]
    rest = (keep_ref[count * 8 :, :] + got_ref[count * 8 :, :].astype(F32)).astype(BF16)
    row = iota((128, 128), 0)
    source = (row // 2) % 8 * 16 + row // 16 * 2 + row % 2
    perm = (iota((128, 128), 1) == source).astype(BF16)
    groups = count // 8
    stacked = jnp.concatenate(
        [
            jnp.concatenate(
                [rest[g * 16 : (g + 1) * 16, j * LANES : (j + 1) * LANES] for j in range(8)], axis=0
            )
            for g in range(groups)
        ],
        axis=1,
    )
    moved = fast_dot(perm, stacked).astype(BF16)
    for g in range(groups):
        out_ref[g * 8 : (g + 1) * 8, 64:80, :] = moved[:, g * LANES : (g + 1) * LANES].reshape(8, 16, LANES)
    copies = []

    def send(first, last):
        span = pl.ds(first, last - first)
        copies.append(
            pltpu.make_async_copy(out_ref.at[:, span, :], out_hbm.at[:, span, :], sems.at[len(copies)])
        )
        copies[-1].start()

    send(64, 80)
    for pair in range(4):
        tiles = []
        for j in (2 * pair, 2 * pair + 1):
            cols = slice(j * LANES, (j + 1) * LANES)
            value = keep_ref[0 : count * 8, cols] + got_ref[0 : count * 8, cols].astype(F32)
            tiles.append(value.reshape(count, 8, LANES))
        out_ref[:, pair * 16 : (pair + 1) * 16, :] = jnp.concatenate(tiles, axis=1).astype(BF16)
        send(pair * 16, pair * 16 + 16)
    for copy in copies:
        copy.wait()


def combine_kernel(back_ref, main_ref, rest_ref, hidden_ref, gain_ref, gained_ref, dot_ref):
    count = back_ref.shape[0]
    rows = hidden_ref.shape[0]
    main = jnp.concatenate(
        [back_ref[:, m * 16 : (m + 1) * 16, :].reshape(count * 16, LANES) for m in range(4)], axis=1
    )
    main = fast_dot(main_ref[...], main)
    block = iota((rows, count * 16), 1) % 16 // 2
    left = jnp.concatenate([rest_ref[...] * (block == j).astype(BF16) for j in range(8)], axis=0)
    rest = fast_dot(left, back_ref[:, 64:80, :].reshape(count * 16, LANES))
    total = jnp.zeros((rows, LANES), F32)
    for j in range(8):
        cols = slice(j * LANES, (j + 1) * LANES)
        value = main[j % 2 * rows : (j % 2 + 1) * rows, j // 2 * LANES : (j // 2 + 1) * LANES]
        value = (value + rest[j * rows : (j + 1) * rows, :]) * gain_ref[:, cols]
        gained_ref[:, cols] = value
        total = total + value * hidden_ref[:, cols].astype(F32)
    eye = iota((rows, rows), 0) == iota((rows, rows), 1)
    dot_ref[...] = jnp.sum(jnp.where(eye, jnp.sum(total, axis=1, keepdims=True), 0.0), axis=0, keepdims=True)


def log_sigmoid(x):
    return -(jnp.maximum(-x, 0.0) + jnp.log1p(jnp.exp(-jnp.abs(x))))


def two_parts(array):
    high = array.astype(BF16)
    return high, (array - high.astype(F32)).astype(BF16)


def three_parts(array):
    high = array.astype(BF16)
    middle, low = two_parts(array - high.astype(F32))
    return high, middle, low


def head_mask():
    return iota((LANES, LANES), 0) // HEAD_DIM == iota((LANES, LANES), 1) // HEAD_DIM


def decays(logit_ref, value_ref, total_ref, local_ref, parts_ref):
    rows, feats = logit_ref.shape
    logits = logit_ref[...].astype(F32)
    key = jax.nn.sigmoid(-logits)
    lower = (iota((rows, rows), 0) >= iota((rows, rows), 1)).astype(F32)
    running = exact_dot(lower, log_sigmoid(logits))
    total_ref[...] = running
    end = running[rows - 1 : rows, :]
    key_end = key * jnp.exp(end - running)
    decay = jnp.exp(end)
    same = head_mask()
    pick = iota((HEAD_DIM, LANES), 0) == iota((HEAD_DIM, LANES), 1) % HEAD_DIM
    for pair in range(feats // LANES):
        cols = slice(pair * LANES, (pair + 1) * LANES)
        eight = slice(pair * 8, (pair + 1) * 8)
        local = exact_dot(key_end[:, cols], value_ref[:, cols].astype(F32), TN)
        local = jnp.where(same, local, 0.0)
        local = (local[:HEAD_DIM] + local[HEAD_DIM:]).reshape(8, 8, LANES)
        spread = exact_dot(jnp.where(pick, decay[:, cols], 0.0), same.astype(F32)).reshape(8, 8, LANES)
        local_ref[eight] = local
        rest = spread - spread.astype(BF16).astype(F32)
        parts_ref[eight] = jnp.concatenate([spread, rest], axis=1).astype(BF16)


def chain_kernel(piece_ref, out_ref, decay, both):
    count = piece_ref.shape[0]
    decay[...] = piece_ref[:, 16:32, :].astype(F32)
    both[...] = piece_ref[:, 0:16, :].astype(F32)
    later = jnp.zeros((8, LANES), F32)
    earlier = jnp.zeros((8, LANES), F32)
    for block in range(count):
        piece = both[block, 8:16, :]
        both[block, 8:16, :] = earlier
        earlier = (decay[block, 0:8, :] + decay[block, 8:16, :]) * earlier + piece
        other = count - 1 - block
        piece = both[other, 0:8, :]
        both[other, 0:8, :] = later
        later = (decay[other, 0:8, :] + decay[other, 8:16, :]) * later + piece
    out_ref[...] = both[...].astype(BF16)


def hidden_kernel(
    hidden_ref,
    cot_ref,
    own_sq_ref,
    peer_sq_ref,
    gained_ref,
    own_dot_ref,
    peer_dot_ref,
    query_ref,
    total_ref,
    local_ref,
    parts_ref,
    width,
    out_ref,
    piece_ref,
):
    row_scale = row_scale_of(own_sq_ref, peer_sq_ref, width)
    dot = column(own_dot_ref[...] + peer_dot_ref[...])
    back = row_scale * gained_ref[...] - hidden_ref[...].astype(F32) * (
        row_scale * row_scale * row_scale * dot / width
    )
    upstream = (cot_ref[...].astype(F32) + back).astype(BF16)
    out_ref[...] = upstream
    query = query_ref[...].astype(F32) * jnp.exp(total_ref[...])
    same = head_mask()
    piece_ref[:, 16:32, :] = parts_ref[...]
    for pair in range(hidden_ref.shape[1] // LANES):
        cols = slice(pair * LANES, (pair + 1) * LANES)
        eight = slice(pair * 8, (pair + 1) * 8)
        high, low = two_parts(query[:, cols])
        elem = fast_dot(high, upstream[:, cols], TN) + fast_dot(low, upstream[:, cols], TN)
        elem = jnp.where(same, elem, 0.0)
        elem = (elem[:HEAD_DIM] + elem[HEAD_DIM:]).reshape(8, 8, LANES)
        piece_ref[eight, 0:16, :] = jnp.concatenate([elem, local_ref[eight]], axis=1).astype(BF16)


def block_kernel(query_ref, logit_ref, value_ref, total_ref, upstream_ref, query_out, key_out, value_out):
    rows, feats = query_ref.shape
    lower = iota((rows, rows), 0) >= iota((rows, rows), 1)
    upper = iota((rows, rows), 0) <= iota((rows, rows), 1)
    first = iota((rows, LANES), 1) < HEAD_DIM

    def split(array):
        zero = jnp.zeros_like(array)
        return jnp.where(first, array, zero), jnp.where(first, zero, array)

    for pair in range(feats // LANES):
        cols = slice(pair * LANES, (pair + 1) * LANES)
        query = query_ref[:, cols].astype(F32)
        key = jax.nn.sigmoid(-logit_ref[:, cols].astype(F32))
        running = total_ref[:, cols]
        centre = 0.5 * running[rows - 1 : rows, :]
        grow = jnp.exp(running - centre)
        shrink = jnp.exp(centre - running)
        up_split, value_split = split(upstream_ref[:, cols]), split(value_ref[:, cols])
        query_split, key_split = split(query * grow), split(key * shrink)
        raw = [fast_dot(u, v, NT) for u, v in zip(up_split, value_split)]
        pairs = jnp.concatenate([jnp.where(lower, r, 0.0) for r in raw], axis=1)
        query_out[:, cols] = grow * exact_dot(pairs, jnp.concatenate(key_split, axis=0))
        raw = [fast_dot(v, u, NT) for u, v in zip(up_split, value_split)]
        pairs = jnp.concatenate([jnp.where(upper, r, 0.0) for r in raw], axis=1)
        key_out[:, cols] = shrink * exact_dot(pairs, jnp.concatenate(query_split, axis=0))
        raw = [exact_dot(k, q, NT) for k, q in zip(key_split, query_split)]
        pairs = jnp.concatenate([jnp.where(upper, r, 0.0) for r in raw], axis=1)
        value = exact_dot(pairs, jnp.concatenate([u.astype(F32) for u in up_split], axis=0))
        value_out[:, cols] = value.astype(BF16)


def final_kernel(
    query_ref,
    logit_ref,
    value_ref,
    upstream_ref,
    query_in,
    key_in,
    value_in,
    carried_ref,
    query_out,
    logit_out,
    value_out,
):
    rows, feats = query_ref.shape
    upper = (iota((rows, rows), 0) <= iota((rows, rows), 1)).astype(BF16)
    lower = (iota((rows, rows), 0) >= iota((rows, rows), 1)).astype(BF16)
    ones = jnp.ones((16, LANES), BF16)
    same = head_mask()

    def spread(array):
        return jnp.where(same, jnp.concatenate([array, array], axis=0), 0.0)

    def summed(mask, array):
        high, low = two_parts(array)
        return fast_dot(mask, high) + fast_dot(mask, low)

    for pair in range(feats // LANES):
        cols = slice(pair * LANES, (pair + 1) * LANES)
        eight = slice(pair * 8, (pair + 1) * 8)
        logits = logit_ref[:, cols].astype(F32)
        key = jax.nn.sigmoid(-logits)
        running = summed(lower, log_sigmoid(logits))
        end = running[rows - 1 : rows, :]
        tail = jnp.exp(end - running)
        carried = carried_ref[eight].astype(F32)
        incoming = carried[:, 0:8].reshape(HEAD_DIM, LANES)
        start = carried[:, 8:16].reshape(HEAD_DIM, LANES)
        start_b, incoming_b = spread(start).astype(BF16), spread(incoming).astype(BF16)
        query_grad = query_in[:, cols] + jnp.exp(running) * fast_dot(upstream_ref[:, cols], start_b, NT)
        key_back = tail * fast_dot(value_ref[:, cols], incoming_b, NT)
        key_grad = key_in[:, cols] + key_back
        high, low = two_parts(key * tail)
        value_grad = value_in[:, cols].astype(F32) + fast_dot(high, incoming_b) + fast_dot(low, incoming_b)
        high, low = two_parts(spread(start * incoming))
        past = (fast_dot(ones, high, NT) + fast_dot(ones, low, NT))[0:1, :]
        past = jnp.exp(end) * past + jnp.sum(key * key_back, axis=0, keepdims=True)
        suffix = summed(upper, query_ref[:, cols].astype(F32) * query_grad - key * key_grad) + past
        logit_grad = suffix * key - key_grad * key * (1.0 - key)
        query_out[:, cols] = query_grad.astype(BF16)
        logit_out[:, cols] = logit_grad.astype(BF16)
        value_out[:, cols] = value_grad.astype(BF16)


def on_device(
    hidden, grad_out, expert_ids, gate_weights, norm_gain, w_gate, w_up, w_down, queries, forget_logits, values
):
    rows, feats = hidden.shape
    ctx = lax.axis_size("ctx")
    width = w_gate.shape[1]
    units = w_gate.shape[2]
    slots = ctx * 10
    core = lax.axis_index("tp")
    swap = [(0, 1), (1, 0)]
    gain = norm_gain.reshape(1, feats)

    def exchange(array):
        return lax.all_to_all(array, "ctx", split_axis=0, concat_axis=0, tiled=True)

    ids, weights = expert_ids.T, gate_weights.T
    vmem, hbm = pl.BlockSpec(memory_space=pltpu.VMEM), pl.BlockSpec(memory_space=pl.ANY)
    smem = pl.BlockSpec(memory_space=pltpu.SMEM)

    hidden_f = hidden.astype(F32)
    squares = jnp.sum(hidden_f * hidden_f, axis=1)
    squares = (squares.reshape(1, rows), lax.ppermute(squares, "tp", swap).reshape(1, rows))

    sent = call(
        lambda h, g, s, z, n, i, w, *rest: dispatch_kernel(h, g, s, z, n, i, w, width, *rest),
        shape_of((ctx, 160, LANES), BF16),
        hidden,
        grad_out,
        *squares,
        gain,
        ids,
        weights,
        in_specs=[hbm] * 7,
        out_specs=hbm,
        scratch=(
            pltpu.VMEM((ctx, 160, LANES), BF16),
            pltpu.VMEM((rows, feats), BF16),
            pltpu.VMEM((2 * rows, feats), BF16),
            pltpu.VMEM((8 * rows, 2 * LANES), BF16),
            pltpu.VMEM((1, rows), F32),
            pltpu.VMEM((1, rows), F32),
            pltpu.VMEM((1, feats), F32),
            pltpu.VMEM(ids.shape, jnp.int32),
            pltpu.VMEM(weights.shape, F32),
            pltpu.SemaphoreType.DMA((7,)),
            pltpu.SemaphoreType.DMA((5,)),
        ),
        mib=60,
        flops=1 << 24,
        nbytes=1 << 12,
    )
    own = exchange(sent)
    main_table, rest_table, total, local, decay = call(
        early_kernel,
        (
            shape_of((2 * rows, ctx * 16), BF16),
            shape_of((rows, ctx * 16), BF16),
            shape_of((rows, feats), F32),
            shape_of((ctx, 8, LANES), F32),
            shape_of((ctx, 16, LANES), BF16),
        ),
        ids,
        forget_logits,
        values,
        flops=1 << 30,
        nbytes=4 << 20,
    )

    peer = lax.ppermute(own, "tp", swap)
    which = core.reshape(1).astype(jnp.int32)
    half_in, half_out = shape_of((feats, units), BF16), shape_of((units, feats), BF16)
    *parts, gate, up, peer_gate, peer_up, peer_down = call(
        own_kernel,
        (*(shape_of((slots, units), F32),) * 3, half_in, half_in, half_in, half_in, half_out),
        which,
        own,
        w_gate[0],
        w_up[0],
        w_down[0],
        in_specs=[smem, hbm, hbm, hbm, hbm],
        scratch=(
            pltpu.VMEM((ctx, 160, LANES), BF16),
            pltpu.VMEM((slots, feats), BF16),
            pltpu.VMEM((slots, feats), BF16),
            pltpu.VMEM((units, feats), BF16),
            pltpu.SemaphoreType.DMA((4,)),
            pltpu.SemaphoreType.DMA((3,)),
            pltpu.SemaphoreType.DMA((3,)),
        ),
        mib=39.5,
        flops=6 * slots * feats * units,
        nbytes=13 << 20,
    )
    send, dg, du = call(
        peer_kernel,
        (shape_of((slots, feats), BF16), shape_of((slots, units), BF16), shape_of((slots, units), BF16)),
        peer,
        *parts,
        peer_gate,
        peer_up,
        peer_down,
        scratch=(pltpu.VMEM((slots, feats), BF16), pltpu.VMEM((slots, feats), BF16)),
        mib=28,
        flops=10 * slots * feats * units,
        nbytes=16 << 20,
    )
    got = lax.ppermute(send, "tp", swap)
    keep = call(
        keep_kernel,
        shape_of((slots, feats), F32),
        dg,
        du,
        gate,
        up,
        flops=4 * slots * feats * units,
        nbytes=8 << 20,
    )
    packed = call(
        pack_kernel,
        shape_of((ctx, 80, LANES), BF16),
        keep,
        got,
        out_specs=hbm,
        scratch=(pltpu.VMEM((ctx, 80, LANES), BF16), pltpu.SemaphoreType.DMA((5,))),
        flops=1 << 26,
        nbytes=6 << 20,
    )
    back = exchange(packed)
    gained, dots = call(
        combine_kernel,
        (shape_of((rows, feats), F32), shape_of((1, rows), F32)),
        back,
        main_table,
        rest_table,
        hidden,
        gain,
        flops=1 << 29,
        nbytes=6 << 20,
    )
    dots = (dots, lax.ppermute(dots, "tp", swap))
    grad_hidden, piece = call(
        lambda h, g, s, z, a, d, e, q, t, x, y, o, p: hidden_kernel(
            h, g, s, z, a, d, e, q, t, x, y, width, o, p
        ),
        (shape_of((rows, feats), BF16), shape_of((ctx, 32, LANES), BF16)),
        hidden,
        grad_out,
        *squares,
        gained,
        *dots,
        queries,
        total,
        local,
        decay,
        flops=1 << 28,
        nbytes=3 << 20,
    )
    pieces = exchange(piece)
    inner = call(
        block_kernel,
        (shape_of((rows, feats), F32), shape_of((rows, feats), F32), shape_of((rows, feats), BF16)),
        queries,
        forget_logits,
        values,
        total,
        grad_hidden,
        flops=1 << 32,
        nbytes=4 << 20,
    )
    chained = call(
        chain_kernel,
        shape_of((ctx, 16, LANES), BF16),
        pieces,
        scratch=(pltpu.VMEM((ctx, 16, LANES), F32), pltpu.VMEM((ctx, 16, LANES), F32)),
        nbytes=1 << 20,
    )
    carried = exchange(chained)
    grad_queries, grad_logits, grad_values = call(
        final_kernel,
        (shape_of((rows, feats), BF16),) * 3,
        queries,
        forget_logits,
        values,
        grad_hidden,
        *inner,
        carried,
        flops=1 << 30,
        nbytes=4 << 20,
    )
    return grad_hidden, grad_queries, grad_logits, grad_values


def solution(mesh):
    rows = P("ctx", "tp")
    in_specs = (
        rows,
        rows,
        P("ctx", None),
        P("ctx", None),
        P("tp"),
        P("ctx", None, "tp"),
        P("ctx", None, "tp"),
        P("ctx", "tp", None),
        rows,
        rows,
        rows,
    )
    return jax.shard_map(on_device, mesh=mesh, in_specs=in_specs, out_specs=(rows,) * 4, check_vma=False)
```

```python
import functools

import jax
import jax.numpy as jnp
from jax import lax
from jax.experimental import pallas as pl
from jax.experimental.pallas import tpu as pltpu
from jax.sharding import PartitionSpec as P

HEAD_DIM = 64
NORM_EPS = 1e-06
LANES = 128
BF16 = jnp.bfloat16
F32 = jnp.float32
EXACT = lax.Precision.HIGHEST
NT = (((1,), (1,)), ((), ()))
TN = (((0,), (0,)), ((), ()))
NN = (((1,), (0,)), ((), ()))


def iota(shape, dim):
    return lax.broadcasted_iota(jnp.int32, shape, dim)


def exact_dot(a, b, dims=NN):
    return lax.dot_general(a, b, dims, precision=EXACT, preferred_element_type=F32)


def fast_dot(a, b, dims=NN):
    return lax.dot_general(a, b, dims, preferred_element_type=F32)


def call(kernel, out_shape, *args, scratch=(), in_specs=None, out_specs=None, mib=16, flops=0, nbytes=0):
    return pl.pallas_call(
        kernel,
        out_shape=out_shape,
        in_specs=in_specs or [pl.BlockSpec(memory_space=pltpu.VMEM)] * len(args),
        out_specs=out_specs or jax.tree.map(lambda _: pl.BlockSpec(memory_space=pltpu.VMEM), out_shape),
        scratch_shapes=list(scratch),
        compiler_params=pltpu.CompilerParams(vmem_limit_bytes=int(mib * 2**20)),
        cost_estimate=pl.CostEstimate(flops=flops, bytes_accessed=nbytes, transcendentals=0),
    )(*args)


def shape_of(shape, dtype):
    return jax.ShapeDtypeStruct(shape, dtype)


def ranked(ids_ref, count):
    rows = ids_ref.shape[1]
    named = named_by(ids_ref, count)
    before = (iota((rows, rows), 0) < iota((rows, rows), 1)).astype(BF16)
    rank = fast_dot(named.astype(BF16), before)
    return jnp.where(named > 0.0, rank, -1.0)


def named_by(ids_ref, count, weight_ref=None):
    expert = iota((count, ids_ref.shape[1]), 0)
    total = jnp.zeros(expert.shape, F32)
    for choice in range(ids_ref.shape[0]):
        level = 1.0 if weight_ref is None else weight_ref[choice : choice + 1, :]
        total = total + jnp.where(ids_ref[choice : choice + 1, :] == expert, level, 0.0)
    return total


def column(row):
    count = row.shape[1]
    eye = iota((count, count), 0) == iota((count, count), 1)
    return jnp.sum(jnp.where(eye, row, 0.0), axis=1, keepdims=True)


def row_scale_of(own_ref, peer_ref, width):
    return lax.rsqrt(column(own_ref[...] + peer_ref[...]) / width + NORM_EPS)


def dispatch_kernel(
    hidden_hbm,
    cot_hbm,
    own_sq_hbm,
    peer_sq_hbm,
    gain_hbm,
    ids_hbm,
    weight_hbm,
    width,
    out_hbm,
    out_ref,
    hidden,
    rhs,
    rhs_rem,
    own_sq,
    peer_sq,
    gain,
    ids,
    weight_in,
    in_sems,
    sems,
):
    rows = hidden.shape[0]
    count = out_ref.shape[0]
    loads = start_copies(
        (
            (ids_hbm, ids),
            (weight_hbm, weight_in),
            (own_sq_hbm, own_sq),
            (peer_sq_hbm, peer_sq),
            (gain_hbm, gain),
            (hidden_hbm, hidden),
            (cot_hbm, rhs.at[pl.ds(rows, rows), :]),
        ),
        in_sems,
    )
    loads[0].wait()
    rank_b = ranked(ids, count).astype(BF16)
    loads[1].wait()
    weight = named_by(ids, count, weight_in)
    slots = count * 16
    inner = iota((slots, LANES), 0) % 16
    main_cot = inner >= 8
    rest_cot = (inner // 2) % 2 == 1
    expand = (iota((slots, count), 0) // 16 == iota((slots, count), 1)).astype(BF16)
    ranks = fast_dot(expand, rank_b)
    weights = fast_dot(expand, jnp.concatenate(three_parts(weight), axis=1))
    weights = weights[:, 0:rows] + weights[:, rows : 2 * rows] + weights[:, 2 * rows :]

    def scale_of(hit, is_cot):
        scale = jnp.sum(jnp.where(hit & is_cot, weights, 0.0), axis=1, keepdims=True)
        return jnp.where(is_cot[:, :1], scale, 1.0)

    hit = ranks == (inner % 8).astype(F32)
    hit_b = hit.astype(BF16)
    left = jnp.concatenate([hit_b * mask.astype(BF16) for mask in (~main_cot, main_cot)], axis=1)
    scale = scale_of(hit, main_cot)
    copies = []

    def send(first, last):
        span = pl.ds(first, last - first)
        copies.append(
            pltpu.make_async_copy(out_ref.at[:, span, :], out_hbm.at[:, span, :], sems.at[len(copies)])
        )
        copies[-1].start()

    for load in loads[2:]:
        load.wait()
    row_scale = row_scale_of(own_sq, peer_sq, width)
    rhs[0:rows, :] = (hidden[...].astype(F32) * row_scale * gain[...]).astype(BF16)
    for pair in range(4):
        value = (fast_dot(left, rhs[:, pair * 256 : (pair + 1) * 256]) * scale).astype(BF16)
        for half in range(2):
            first = pair * 32 + half * 16
            out_ref[:, first : first + 16, :] = value[:, half * LANES : (half + 1) * LANES].reshape(count, 16, LANES)
        send(pair * 32, pair * 32 + 32)
    for j in range(8):
        lo, col = 2 * rows * (j % 4), LANES * (j // 4)
        rhs_rem[lo : lo + 2 * rows, col : col + LANES] = rhs[:, j * LANES : (j + 1) * LANES]
    hit = ranks == (8 + inner % 2).astype(F32)
    hit_b = hit.astype(BF16)
    left = jnp.concatenate(
        [
            hit_b * ((inner // 4 == j) & kind).astype(BF16)
            for j in range(4)
            for kind in (~rest_cot, rest_cot)
        ],
        axis=1,
    )
    value = (fast_dot(left, rhs_rem[...]) * scale_of(hit, rest_cot)).astype(BF16)
    for half in range(2):
        first = 128 + half * 16
        out_ref[:, first : first + 16, :] = value[:, half * LANES : (half + 1) * LANES].reshape(count, 16, LANES)
    send(128, 160)
    for copy in copies:
        copy.wait()


def early_kernel(ids_ref, logit_ref, value_ref, main_ref, rest_ref, total_ref, local_ref, parts_ref):
    tables(ids_ref, main_ref, rest_ref)
    decays(logit_ref, value_ref, total_ref, local_ref, parts_ref)


def tables(ids_ref, main_ref, rest_ref):
    slots = main_ref.shape[1]
    count = slots // 16
    rank = ranked(ids_ref, count).astype(BF16)
    expand = (iota((count, slots), 1) // 16 == iota((count, slots), 0)).astype(BF16)
    ranks = fast_dot(rank, expand, TN)
    inner = iota(ranks.shape, 1) % 16
    hit = ranks == (inner % 8).astype(F32)
    rows = ranks.shape[0]
    main_ref[0:rows, :] = (hit & (inner < 8)).astype(BF16)
    main_ref[rows : 2 * rows, :] = (hit & (inner >= 8)).astype(BF16)
    hit = ranks == (8 + inner % 2).astype(F32)
    rest_ref[...] = hit.astype(BF16)


def unpack(raw_ref, x_ref, c_ref, first=0, last=None):
    blocks = raw_ref.shape[0]
    last = blocks if last is None else last
    count = last - first
    main = slice(first * 8, last * 8)
    every = slice(blocks * 8 + first * 2, blocks * 8 + last * 2)
    for j in range(8):
        tile = raw_ref[first:last, j * 16 : (j + 1) * 16, :].astype(F32).reshape(count, 2, 8, LANES)
        cols = slice(j * LANES, (j + 1) * LANES)
        x_ref[main, cols] = tile[:, 0].reshape(count * 8, LANES).astype(BF16)
        c_ref[main, cols] = tile[:, 1].reshape(count * 8, LANES).astype(BF16)
    row = iota((128, 128), 0)
    source = (row // 2) % 4 * 32 + row // 16 * 4 + (row // 8) % 2 * 2 + row % 2
    perm = (iota((128, 128), 1) == source).astype(BF16)
    groups = range(first // 4, last // 4)
    rest = jnp.concatenate(
        [raw_ref[g * 4 : (g + 1) * 4, 128:160, :].reshape(128, LANES) for g in groups], axis=1
    )
    rest = fast_dot(perm, rest)
    for j in range(8):
        cols = slice(j * LANES, (j + 1) * LANES)
        for kind, ref in enumerate((x_ref, c_ref)):
            lo = j * 16 + kind * 8
            ref[every, cols] = jnp.concatenate(
                [rest[lo : lo + 8, g * LANES : (g + 1) * LANES] for g in range(len(groups))], axis=0
            ).astype(BF16)


def start_copies(pairs, sems):
    copies = [pltpu.make_async_copy(source, target, sems.at[number]) for number, (source, target) in enumerate(pairs)]
    for copy in copies:
        copy.start()
    return copies


def half_of(core, half):
    return pl.ds(pl.multiple_of(core * half, half), half)


def own_kernel(
    core_ref,
    raw_hbm,
    gate_hbm,
    up_hbm,
    down_hbm,
    part_0,
    part_1,
    part_2,
    gate,
    up,
    peer_gate,
    peer_up,
    peer_down,
    raw,
    x,
    c,
    down,
    raw_sems,
    sems,
    peer_sems,
):
    mine = half_of(core_ref[0], x.shape[1])
    other = half_of(1 - core_ref[0], x.shape[1])
    quarter = raw.shape[0] // 4
    quarters = [slice(q * quarter, (q + 1) * quarter) for q in range(4)]
    rows = start_copies([(raw_hbm.at[span], raw.at[span]) for span in quarters], raw_sems)
    first = start_copies(((gate_hbm.at[mine, :], gate),), sems)
    for copy, span in zip(rows, quarters):
        copy.wait()
        unpack(raw, x, c, span.start, span.stop)
    second = start_copies(((up_hbm.at[mine, :], up), (down_hbm.at[:, mine], down)), sems.at[pl.ds(1, 2)])
    first[0].wait()
    later = start_copies(
        ((gate_hbm.at[other, :], peer_gate), (up_hbm.at[other, :], peer_up), (down_hbm.at[:, other], peer_down)),
        peer_sems,
    )
    part_0[...] = fast_dot(x[...], gate[...])
    second[0].wait()
    part_1[...] = fast_dot(x[...], up[...])
    second[1].wait()
    part_2[...] = fast_dot(c[...], down[...], NT)
    for copy in later:
        copy.wait()


def peer_kernel(raw_ref, part_0, part_1, part_2, gate, up, down, send_ref, dg, du, x, c):
    unpack(raw_ref, x, c)
    for step in range(part_0.shape[1] // 256):
        cols = slice(step * 256, (step + 1) * 256)
        pre_gate = part_0[:, cols] + fast_dot(x[...], gate[:, cols])
        pre_up = part_1[:, cols] + fast_dot(x[...], up[:, cols])
        d_act = part_2[:, cols] + fast_dot(c[...], down[cols, :], NT)
        sig = jax.nn.sigmoid(pre_gate)
        dg[:, cols] = (d_act * pre_up * sig * (1.0 + pre_gate * (1.0 - sig))).astype(BF16)
        du[:, cols] = (d_act * pre_gate * sig).astype(BF16)
    project(dg, du, gate, up, send_ref)


def project(dg, du, gate, up, out_ref):
    for step in range(out_ref.shape[1] // 256):
        cols = slice(step * 256, (step + 1) * 256)
        value = fast_dot(dg[...], gate[cols, :], NT) + fast_dot(du[...], up[cols, :], NT)
        out_ref[:, cols] = value.astype(out_ref.dtype)


def keep_kernel(dg, du, gate, up, keep_ref):
    project(dg, du, gate, up, keep_ref)


def pack_kernel(keep_ref, got_ref, out_hbm, out_ref, sems):
    count = out_ref.shape[0]
    rest = (keep_ref[count * 8 :, :] + got_ref[count * 8 :, :].astype(F32)).astype(BF16)
    row = iota((128, 128), 0)
    source = (row // 2) % 8 * 16 + row // 16 * 2 + row % 2
    perm = (iota((128, 128), 1) == source).astype(BF16)
    groups = count // 8
    stacked = jnp.concatenate(
        [
            jnp.concatenate(
                [rest[g * 16 : (g + 1) * 16, j * LANES : (j + 1) * LANES] for j in range(8)], axis=0
            )
            for g in range(groups)
        ],
        axis=1,
    )
    moved = fast_dot(perm, stacked).astype(BF16)
    for g in range(groups):
        out_ref[g * 8 : (g + 1) * 8, 64:80, :] = moved[:, g * LANES : (g + 1) * LANES].reshape(8, 16, LANES)
    copies = []

    def send(first, last):
        span = pl.ds(first, last - first)
        copies.append(
            pltpu.make_async_copy(out_ref.at[:, span, :], out_hbm.at[:, span, :], sems.at[len(copies)])
        )
        copies[-1].start()

    send(64, 80)
    for pair in range(4):
        tiles = []
        for j in (2 * pair, 2 * pair + 1):
            cols = slice(j * LANES, (j + 1) * LANES)
            value = keep_ref[0 : count * 8, cols] + got_ref[0 : count * 8, cols].astype(F32)
            tiles.append(value.reshape(count, 8, LANES))
        out_ref[:, pair * 16 : (pair + 1) * 16, :] = jnp.concatenate(tiles, axis=1).astype(BF16)
        send(pair * 16, pair * 16 + 16)
    for copy in copies:
        copy.wait()


def combine_kernel(back_ref, main_ref, rest_ref, hidden_ref, gain_ref, gained_ref, dot_ref):
    count = back_ref.shape[0]
    rows = hidden_ref.shape[0]
    main = jnp.concatenate(
        [back_ref[:, m * 16 : (m + 1) * 16, :].reshape(count * 16, LANES) for m in range(4)], axis=1
    )
    main = fast_dot(main_ref[...], main)
    block = iota((rows, count * 16), 1) % 16 // 2
    left = jnp.concatenate([rest_ref[...] * (block == j).astype(BF16) for j in range(8)], axis=0)
    rest = fast_dot(left, back_ref[:, 64:80, :].reshape(count * 16, LANES))
    total = jnp.zeros((rows, LANES), F32)
    for j in range(8):
        cols = slice(j * LANES, (j + 1) * LANES)
        value = main[j % 2 * rows : (j % 2 + 1) * rows, j // 2 * LANES : (j // 2 + 1) * LANES]
        value = (value + rest[j * rows : (j + 1) * rows, :]) * gain_ref[:, cols]
        gained_ref[:, cols] = value
        total = total + value * hidden_ref[:, cols].astype(F32)
    eye = iota((rows, rows), 0) == iota((rows, rows), 1)
    dot_ref[...] = jnp.sum(jnp.where(eye, jnp.sum(total, axis=1, keepdims=True), 0.0), axis=0, keepdims=True)


def log_sigmoid(x):
    return -(jnp.maximum(-x, 0.0) + jnp.log1p(jnp.exp(-jnp.abs(x))))


def two_parts(array):
    high = array.astype(BF16)
    return high, (array - high.astype(F32)).astype(BF16)


def three_parts(array):
    high = array.astype(BF16)
    middle, low = two_parts(array - high.astype(F32))
    return high, middle, low


def head_mask():
    return iota((LANES, LANES), 0) // HEAD_DIM == iota((LANES, LANES), 1) // HEAD_DIM


def decays(logit_ref, value_ref, total_ref, local_ref, parts_ref):
    rows, feats = logit_ref.shape
    logits = logit_ref[...].astype(F32)
    key = jax.nn.sigmoid(-logits)
    lower = (iota((rows, rows), 0) >= iota((rows, rows), 1)).astype(F32)
    running = exact_dot(lower, log_sigmoid(logits))
    total_ref[...] = running
    end = running[rows - 1 : rows, :]
    key_end = key * jnp.exp(end - running)
    decay = jnp.exp(end)
    same = head_mask()
    pick = iota((HEAD_DIM, LANES), 0) == iota((HEAD_DIM, LANES), 1) % HEAD_DIM
    for pair in range(feats // LANES):
        cols = slice(pair * LANES, (pair + 1) * LANES)
        eight = slice(pair * 8, (pair + 1) * 8)
        local = exact_dot(key_end[:, cols], value_ref[:, cols].astype(F32), TN)
        local = jnp.where(same, local, 0.0)
        local = (local[:HEAD_DIM] + local[HEAD_DIM:]).reshape(8, 8, LANES)
        spread = exact_dot(jnp.where(pick, decay[:, cols], 0.0), same.astype(F32)).reshape(8, 8, LANES)
        local_ref[eight] = local
        rest = spread - spread.astype(BF16).astype(F32)
        parts_ref[eight] = jnp.concatenate([spread, rest], axis=1).astype(BF16)


def chain_kernel(piece_ref, out_ref, decay, both):
    count = piece_ref.shape[0]
    decay[...] = piece_ref[:, 16:32, :].astype(F32)
    both[...] = piece_ref[:, 0:16, :].astype(F32)
    later = jnp.zeros((8, LANES), F32)
    earlier = jnp.zeros((8, LANES), F32)
    for block in range(count):
        piece = both[block, 8:16, :]
        both[block, 8:16, :] = earlier
        earlier = (decay[block, 0:8, :] + decay[block, 8:16, :]) * earlier + piece
        other = count - 1 - block
        piece = both[other, 0:8, :]
        both[other, 0:8, :] = later
        later = (decay[other, 0:8, :] + decay[other, 8:16, :]) * later + piece
    out_ref[...] = both[...].astype(BF16)


def hidden_kernel(
    hidden_ref,
    cot_ref,
    own_sq_ref,
    peer_sq_ref,
    gained_ref,
    own_dot_ref,
    peer_dot_ref,
    query_ref,
    total_ref,
    local_ref,
    parts_ref,
    width,
    out_ref,
    piece_ref,
):
    row_scale = row_scale_of(own_sq_ref, peer_sq_ref, width)
    dot = column(own_dot_ref[...] + peer_dot_ref[...])
    back = row_scale * gained_ref[...] - hidden_ref[...].astype(F32) * (
        row_scale * row_scale * row_scale * dot / width
    )
    upstream = (cot_ref[...].astype(F32) + back).astype(BF16)
    out_ref[...] = upstream
    query = query_ref[...].astype(F32) * jnp.exp(total_ref[...])
    same = head_mask()
    piece_ref[:, 16:32, :] = parts_ref[...]
    for pair in range(hidden_ref.shape[1] // LANES):
        cols = slice(pair * LANES, (pair + 1) * LANES)
        eight = slice(pair * 8, (pair + 1) * 8)
        high, low = two_parts(query[:, cols])
        elem = fast_dot(high, upstream[:, cols], TN) + fast_dot(low, upstream[:, cols], TN)
        elem = jnp.where(same, elem, 0.0)
        elem = (elem[:HEAD_DIM] + elem[HEAD_DIM:]).reshape(8, 8, LANES)
        piece_ref[eight, 0:16, :] = jnp.concatenate([elem, local_ref[eight]], axis=1).astype(BF16)


def block_kernel(query_ref, logit_ref, value_ref, total_ref, upstream_ref, query_out, key_out, value_out):
    rows, feats = query_ref.shape
    lower = iota((rows, rows), 0) >= iota((rows, rows), 1)
    upper = iota((rows, rows), 0) <= iota((rows, rows), 1)
    first = iota((rows, LANES), 1) < HEAD_DIM

    def split(array):
        zero = jnp.zeros_like(array)
        return jnp.where(first, array, zero), jnp.where(first, zero, array)

    for pair in range(feats // LANES):
        cols = slice(pair * LANES, (pair + 1) * LANES)
        query = query_ref[:, cols].astype(F32)
        key = jax.nn.sigmoid(-logit_ref[:, cols].astype(F32))
        running = total_ref[:, cols]
        centre = 0.5 * running[rows - 1 : rows, :]
        grow = jnp.exp(running - centre)
        shrink = jnp.exp(centre - running)
        up_split, value_split = split(upstream_ref[:, cols]), split(value_ref[:, cols])
        query_split, key_split = split(query * grow), split(key * shrink)
        raw = [fast_dot(u, v, NT) for u, v in zip(up_split, value_split)]
        pairs = jnp.concatenate([jnp.where(lower, r, 0.0) for r in raw], axis=1)
        query_out[:, cols] = grow * exact_dot(pairs, jnp.concatenate(key_split, axis=0))
        raw = [fast_dot(v, u, NT) for u, v in zip(up_split, value_split)]
        pairs = jnp.concatenate([jnp.where(upper, r, 0.0) for r in raw], axis=1)
        key_out[:, cols] = shrink * exact_dot(pairs, jnp.concatenate(query_split, axis=0))
        raw = [exact_dot(k, q, NT) for k, q in zip(key_split, query_split)]
        pairs = jnp.concatenate([jnp.where(upper, r, 0.0) for r in raw], axis=1)
        value = exact_dot(pairs, jnp.concatenate([u.astype(F32) for u in up_split], axis=0))
        value_out[:, cols] = value.astype(BF16)


def final_kernel(
    query_ref,
    logit_ref,
    value_ref,
    upstream_ref,
    query_in,
    key_in,
    value_in,
    carried_ref,
    query_out,
    logit_out,
    value_out,
):
    rows, feats = query_ref.shape
    upper = (iota((rows, rows), 0) <= iota((rows, rows), 1)).astype(BF16)
    lower = (iota((rows, rows), 0) >= iota((rows, rows), 1)).astype(BF16)
    ones = jnp.ones((16, LANES), BF16)
    same = head_mask()

    def spread(array):
        return jnp.where(same, jnp.concatenate([array, array], axis=0), 0.0)

    def summed(mask, array):
        high, low = two_parts(array)
        return fast_dot(mask, high) + fast_dot(mask, low)

    for pair in range(feats // LANES):
        cols = slice(pair * LANES, (pair + 1) * LANES)
        eight = slice(pair * 8, (pair + 1) * 8)
        logits = logit_ref[:, cols].astype(F32)
        key = jax.nn.sigmoid(-logits)
        running = summed(lower, log_sigmoid(logits))
        end = running[rows - 1 : rows, :]
        tail = jnp.exp(end - running)
        carried = carried_ref[eight].astype(F32)
        incoming = carried[:, 0:8].reshape(HEAD_DIM, LANES)
        start = carried[:, 8:16].reshape(HEAD_DIM, LANES)
        start_b, incoming_b = spread(start).astype(BF16), spread(incoming).astype(BF16)
        query_grad = query_in[:, cols] + jnp.exp(running) * fast_dot(upstream_ref[:, cols], start_b, NT)
        key_back = tail * fast_dot(value_ref[:, cols], incoming_b, NT)
        key_grad = key_in[:, cols] + key_back
        high, low = two_parts(key * tail)
        value_grad = value_in[:, cols].astype(F32) + fast_dot(high, incoming_b) + fast_dot(low, incoming_b)
        high, low = two_parts(spread(start * incoming))
        past = (fast_dot(ones, high, NT) + fast_dot(ones, low, NT))[0:1, :]
        past = jnp.exp(end) * past + jnp.sum(key * key_back, axis=0, keepdims=True)
        suffix = summed(upper, query_ref[:, cols].astype(F32) * query_grad - key * key_grad) + past
        logit_grad = suffix * key - key_grad * key * (1.0 - key)
        query_out[:, cols] = query_grad.astype(BF16)
        logit_out[:, cols] = logit_grad.astype(BF16)
        value_out[:, cols] = value_grad.astype(BF16)


def on_device(
    hidden, grad_out, expert_ids, gate_weights, norm_gain, w_gate, w_up, w_down, queries, forget_logits, values
):
    rows, feats = hidden.shape
    ctx = lax.axis_size("ctx")
    width = w_gate.shape[1]
    units = w_gate.shape[2]
    slots = ctx * 10
    core = lax.axis_index("tp")
    swap = [(0, 1), (1, 0)]
    gain = norm_gain.reshape(1, feats)

    def exchange(array):
        return lax.all_to_all(array, "ctx", split_axis=0, concat_axis=0, tiled=True)

    ids, weights = expert_ids.T, gate_weights.T
    vmem, hbm = pl.BlockSpec(memory_space=pltpu.VMEM), pl.BlockSpec(memory_space=pl.ANY)
    smem = pl.BlockSpec(memory_space=pltpu.SMEM)

    hidden_f = hidden.astype(F32)
    squares = jnp.sum(hidden_f * hidden_f, axis=1)
    squares = (squares.reshape(1, rows), lax.ppermute(squares, "tp", swap).reshape(1, rows))

    sent = call(
        lambda h, g, s, z, n, i, w, *rest: dispatch_kernel(h, g, s, z, n, i, w, width, *rest),
        shape_of((ctx, 160, LANES), BF16),
        hidden,
        grad_out,
        *squares,
        gain,
        ids,
        weights,
        in_specs=[hbm] * 7,
        out_specs=hbm,
        scratch=(
            pltpu.VMEM((ctx, 160, LANES), BF16),
            pltpu.VMEM((rows, feats), BF16),
            pltpu.VMEM((2 * rows, feats), BF16),
            pltpu.VMEM((8 * rows, 2 * LANES), BF16),
            pltpu.VMEM((1, rows), F32),
            pltpu.VMEM((1, rows), F32),
            pltpu.VMEM((1, feats), F32),
            pltpu.VMEM(ids.shape, jnp.int32),
            pltpu.VMEM(weights.shape, F32),
            pltpu.SemaphoreType.DMA((7,)),
            pltpu.SemaphoreType.DMA((5,)),
        ),
        mib=60,
        flops=1 << 24,
        nbytes=1 << 12,
    )
    own = exchange(sent)
    main_table, rest_table, total, local, decay = call(
        early_kernel,
        (
            shape_of((2 * rows, ctx * 16), BF16),
            shape_of((rows, ctx * 16), BF16),
            shape_of((rows, feats), F32),
            shape_of((ctx, 8, LANES), F32),
            shape_of((ctx, 16, LANES), BF16),
        ),
        ids,
        forget_logits,
        values,
        flops=1 << 30,
        nbytes=4 << 20,
    )

    peer = lax.ppermute(own, "tp", swap)
    which = core.reshape(1).astype(jnp.int32)
    half_in, half_out = shape_of((feats, units), BF16), shape_of((units, feats), BF16)
    *parts, gate, up, peer_gate, peer_up, peer_down = call(
        own_kernel,
        (*(shape_of((slots, units), F32),) * 3, half_in, half_in, half_in, half_in, half_out),
        which,
        own,
        w_gate[0],
        w_up[0],
        w_down[0],
        in_specs=[smem, hbm, hbm, hbm, hbm],
        scratch=(
            pltpu.VMEM((ctx, 160, LANES), BF16),
            pltpu.VMEM((slots, feats), BF16),
            pltpu.VMEM((slots, feats), BF16),
            pltpu.VMEM((units, feats), BF16),
            pltpu.SemaphoreType.DMA((4,)),
            pltpu.SemaphoreType.DMA((3,)),
            pltpu.SemaphoreType.DMA((3,)),
        ),
        mib=39.5,
        flops=6 * slots * feats * units,
        nbytes=13 << 20,
    )
    send, dg, du = call(
        peer_kernel,
        (shape_of((slots, feats), BF16), shape_of((slots, units), BF16), shape_of((slots, units), BF16)),
        peer,
        *parts,
        peer_gate,
        peer_up,
        peer_down,
        scratch=(pltpu.VMEM((slots, feats), BF16), pltpu.VMEM((slots, feats), BF16)),
        mib=28,
        flops=10 * slots * feats * units,
        nbytes=16 << 20,
    )
    got = lax.ppermute(send, "tp", swap)
    keep = call(
        keep_kernel,
        shape_of((slots, feats), F32),
        dg,
        du,
        gate,
        up,
        flops=4 * slots * feats * units,
        nbytes=8 << 20,
    )
    packed = call(
        pack_kernel,
        shape_of((ctx, 80, LANES), BF16),
        keep,
        got,
        out_specs=hbm,
        scratch=(pltpu.VMEM((ctx, 80, LANES), BF16), pltpu.SemaphoreType.DMA((5,))),
        flops=1 << 26,
        nbytes=6 << 20,
    )
    back = exchange(packed)
    gained, dots = call(
        combine_kernel,
        (shape_of((rows, feats), F32), shape_of((1, rows), F32)),
        back,
        main_table,
        rest_table,
        hidden,
        gain,
        flops=1 << 29,
        nbytes=6 << 20,
    )
    dots = (dots, lax.ppermute(dots, "tp", swap))
    grad_hidden, piece = call(
        lambda h, g, s, z, a, d, e, q, t, x, y, o, p: hidden_kernel(
            h, g, s, z, a, d, e, q, t, x, y, width, o, p
        ),
        (shape_of((rows, feats), BF16), shape_of((ctx, 32, LANES), BF16)),
        hidden,
        grad_out,
        *squares,
        gained,
        *dots,
        queries,
        total,
        local,
        decay,
        flops=1 << 28,
        nbytes=3 << 20,
    )
    pieces = exchange(piece)
    inner = call(
        block_kernel,
        (shape_of((rows, feats), F32), shape_of((rows, feats), F32), shape_of((rows, feats), BF16)),
        queries,
        forget_logits,
        values,
        total,
        grad_hidden,
        flops=1 << 32,
        nbytes=4 << 20,
    )
    chained = call(
        chain_kernel,
        shape_of((ctx, 16, LANES), BF16),
        pieces,
        scratch=(pltpu.VMEM((ctx, 16, LANES), F32), pltpu.VMEM((ctx, 16, LANES), F32)),
        nbytes=1 << 20,
    )
    carried = exchange(chained)
    grad_queries, grad_logits, grad_values = call(
        final_kernel,
        (shape_of((rows, feats), BF16),) * 3,
        queries,
        forget_logits,
        values,
        grad_hidden,
        *inner,
        carried,
        flops=1 << 30,
        nbytes=4 << 20,
    )
    return grad_hidden, grad_queries, grad_logits, grad_values


def solution(mesh):
    rows = P("ctx", "tp")
    in_specs = (
        rows,
        rows,
        P("ctx", None),
        P("ctx", None),
        P("tp"),
        P("ctx", None, "tp"),
        P("ctx", None, "tp"),
        P("ctx", "tp", None),
        rows,
        rows,
        rows,
    )
    return jax.shard_map(on_device, mesh=mesh, in_specs=in_specs, out_specs=(rows,) * 4, check_vma=False)
```
